32 devices in a mesh: parts: 2 (over y), wide: 4 (over z), narrow: 2 (over x), pair: 2 (over core).
Axes of the slice: x: 2, y: 2, z: 4, core: 2. Of those that a mesh axis runs over, the one named last changes fastest.
Arguments:
- low_sino: bfloat16 [8, 24, 32, 512], P(('parts', 'wide'), None, None, ('narrow', 'pair')), parts along dimension 0, may hold values from -6 to 6
- angle_weight: bfloat16 [4, 24, 24], replicated, may hold values from -1.25 to 1.25
- angle_bias: float32 [24], replicated, may hold values from -3 to 3
- column_weight: bfloat16 [4, 24, 24], replicated, may hold values from -0.875 to 0.875
- column_bias: float32 [24], replicated, may hold values from -3 to 3
- head_weight: float32 [24], replicated, may hold values from -1.25 to 1.25
- sparse_views: int32 [4, 16], P(('parts', 'narrow')), parts along dimension 0, may hold values from 0 to 7
- measured: float32 [32, 16, 512], P('parts', 'wide', ('narrow', 'pair')), parts along dimension 0, may hold values from -6 to 6
- row_weights: float32 [512, 512], P(('narrow', 'pair')), may hold values from -0.25 to 0.25
Outputs:
- predicted: float32 [16, 16, 512], P('parts', 'wide', ('narrow', 'pair')), parts along dimension 0
- adjoint: float32 [32, 16, 512], P('parts', 'wide', ('narrow', 'pair')), parts along dimension 0
The draws below stay inside these ranges and needn't reach their ends.
There are 2 independent parts, one for each index of `parts`. The reference program is written for one: setup_inputs(seed, part) draws one part's arguments, and reference() takes and returns one part's arrays. A program takes and returns all parts, laid end to end along the dimension named above; an argument that names none is the same for every part. Nothing has to cross between parts.
All inputs are finite; a program needn't handle non-finite values.
Results may differ from the reference program's by a relative error of at most 0.0034.
Values may be sent and summed in bfloat16 or wider, within the bound.
No kernel may reach another device: no remote copies, remote signals or barrier semaphores. Data moves between devices by JAX's collectives and lax.ppermute only.
A program may use at most 64 MiB of HBM per device.

```python
import jax
import jax.numpy as jnp
from jax import lax

C = 24
ROW_DEV = 128
K = 16
V_IN = 4
V_OUT = 8
W = 32
WOUT = 16
ROWS = 512
BANDS = 2


def touch_ends(result, key, least, top_value):
    extent = result.shape
    spot = [jax.random.randint(jax.random.fold_in(key, axis), (), 0, extent[axis]) for axis in range(len(extent))]
    result = result.at[tuple(spot)].set(least)
    longest = extent.index(max(extent))
    spot[longest] = (spot[longest] + 1) % extent[longest]
    return result.at[tuple(spot)].set(top_value)


def level_of(own_key, extent, cuts, low, largest):
    def one(position, shards_of):
        heights = jax.random.uniform(jax.random.fold_in(jax.random.fold_in(own_key, 6), position), (shards_of,), jnp.float32, low / len(cuts), largest / len(cuts))
        return jnp.repeat(jnp.exp(heights), extent[position] // shards_of).reshape((-1,) + (1,) * (len(extent) - position - 1))

    factor_of = one(*cuts[0])
    for cut in cuts[1:]:
        factor_of = factor_of * one(*cut)
    return factor_of


def noise(rng, dims, spread, reach, cuts=(), kind=jnp.bfloat16):
    result = spread * jax.random.normal(rng, dims, jnp.float32)
    if cuts:
        result = result * level_of(rng, dims, cuts, -0.22, 0.18)
    return jnp.clip(result, -reach, reach).astype(kind)


def setup_inputs(seed: int = 0, part: int = 0) -> dict:
    splits = jax.random.split(jax.random.key(seed), 10)
    part_keys = jax.random.split(jax.random.fold_in(splits[9], part), 10)
    low_sino = noise(part_keys[0], (V_IN, C, W, ROWS), 1.0, 6.0, ((0, 4), (3, 4)))
    angle_weight = noise(splits[1], (4, C, C), C ** -0.5, 1.25)
    angle_bias = noise(splits[2], (C,), 0.5, 3.0, (), jnp.float32)
    column_weight = noise(splits[3], (4, C, C), (2 * C) ** -0.5, 0.875)
    column_bias = noise(splits[4], (C,), 0.5, 3.0, (), jnp.float32)
    head_weight = noise(splits[5], (C,), C ** -0.5, 1.25, (), jnp.float32)
    sparse_views = touch_ends(jax.random.randint(part_keys[6], (BANDS, K), 0, V_OUT), jax.random.fold_in(part_keys[6], 1), 0, V_OUT - 1).astype(jnp.int32)
    measured = noise(part_keys[7], (K, WOUT, ROWS), 1.0, 6.0, ((1, 4), (2, 4)), jnp.float32)
    row_weights = noise(splits[8], (ROWS, ROWS), ROWS ** -0.5, 0.25, ((0, 4),), jnp.float32)
    return {"low_sino": low_sino, "angle_weight": angle_weight, "angle_bias": angle_bias, "column_weight": column_weight, "column_bias": column_bias, "head_weight": head_weight, "sparse_views": sparse_views, "measured": measured, "row_weights": row_weights}


def leaky_relu(values):
    return jnp.where(values > 0, values, 0.1 * values)


def channel_mix(inputs, weight):
    return jnp.einsum('vcwr,cd->vdwr', inputs.astype(jnp.float32), weight.astype(jnp.float32))


def upsample(current, weight, bias_values):
    previous = jnp.roll(current, 1, axis=0)
    even_views = channel_mix(current, weight[0]) + channel_mix(previous, weight[2])
    odd_views = channel_mix(current, weight[1]) + channel_mix(previous, weight[3])
    stacked = jnp.stack([even_views, odd_views], axis=1) + bias_values[None, None, :, None, None]
    return leaky_relu(stacked).reshape(2 * current.shape[0], current.shape[1], current.shape[2], current.shape[3]).astype(jnp.bfloat16)


def detector_layer(upsampled, weight, bias_values, head_weight):
    padded = jnp.pad(upsampled, ((0, 0), (0, 0), (1, 1), (0, 0)))
    col_count = upsampled.shape[2]
    summed = channel_mix(padded[:, :, 0:col_count:2], weight[0])
    for tap_index in range(1, 4):
        summed = summed + channel_mix(padded[:, :, tap_index:tap_index + col_count:2], weight[tap_index])
    hidden = leaky_relu(summed + bias_values[None, :, None, None])
    return jnp.sum(hidden * head_weight[None, :, None, None], axis=1)


def reference(low_sino, angle_weight, angle_bias, column_weight, column_bias, head_weight, sparse_views, measured, row_weights):
    def one_block(block_index):
        row_block = lax.dynamic_slice_in_dim(low_sino, block_index * ROW_DEV, ROW_DEV, 3)
        upsampled = upsample(row_block, angle_weight, angle_bias)
        return detector_layer(upsampled, column_weight, column_bias, head_weight)

    blocks = lax.map(one_block, jnp.arange(ROWS // ROW_DEV, dtype=jnp.int32))
    predicted = jnp.transpose(blocks, (1, 2, 0, 3)).reshape(V_OUT, WOUT, ROWS)
    banded = predicted.reshape(V_OUT, WOUT, BANDS, ROWS // BANDS)
    picked = jnp.stack([jnp.take(banded[:, :, band_index], sparse_views[band_index], axis=0) for band_index in range(BANDS)], axis=2)
    residual_slab = picked.reshape(K, WOUT, ROWS) - measured
    adjoint = jnp.einsum('kjr,zr->kjz', residual_slab, row_weights, precision=lax.Precision.HIGHEST)
    return (predicted, adjoint)
```

```python
import functools

import jax
import jax.numpy as jnp
from jax import lax
from jax.experimental import pallas as pl
from jax.experimental.pallas import tpu as pltpu
from jax.sharding import PartitionSpec as P

F32, BF16 = jnp.float32, jnp.bfloat16
VMEM = pl.BlockSpec(memory_space=pltpu.VMEM)
SMEM = pl.BlockSpec(memory_space=pltpu.SMEM)
TAPS = 4


def call(kernel, outs, in_specs, scratch=(), vmem=16, flops=10**6):
    nbytes = sum(o.size * o.dtype.itemsize for o in jax.tree.leaves(outs))
    return pl.pallas_call(
        kernel,
        out_shape=outs,
        in_specs=in_specs,
        out_specs=jax.tree.map(lambda _: VMEM, outs),
        scratch_shapes=list(scratch),
        compiler_params=pltpu.CompilerParams(vmem_limit_bytes=vmem << 20),
        cost_estimate=pl.CostEstimate(flops=flops, bytes_accessed=nbytes, transcendentals=0),
    )


def leaky_relu(values):
    return jnp.maximum(values, 0.1 * values)


def split(index, size):
    whole = ((index.astype(F32) + 0.5) * (1.0 / size)).astype(jnp.int32)
    return whole, index - whole * size


def iota(shape, axis):
    return lax.broadcasted_iota(jnp.int32, shape, axis)


def pack_kernel(wide, low_ref, *refs):
    windows, rows_ref = refs[:-1], refs[-1]
    _, channels, width, rows = low_ref.shape
    rows_ref[...] = low_ref[0].astype(F32).reshape(channels * width, rows)
    own = width // wide
    me = lax.axis_index("wide")
    for shift in range(wide):
        first = lax.rem(me + shift, wide) * own - 1
        columns = []
        for i in range(own + 2):
            column = jnp.clip(first + i, 0, width - 1)
            columns.append(rows_ref[pl.ds(column, channels, stride=width), :])
        windows[shift][...] = jnp.concatenate(columns, axis=0).astype(BF16)


def expand_kernel(wide, own_out, aw_ref, ab_ref, cw_ref, cb_ref, hw_ref, rw_ref, a1_ref, a2_ref, b1_ref, b2_ref, h_ref, hi_ref, lo_ref):
    channels = aw_ref.shape[1]
    span = 2 * own_out + 2
    size, outs = span * channels, own_out * channels
    rows, columns = split(iota((size, channels), 0), channels)
    pick = (columns == iota((size, channels), 1)).astype(F32)
    pick16 = pick.astype(BF16)
    out_channel, _ = split(iota((outs, channels), 0), own_out)
    pick_out = (out_channel == iota((outs, channels), 1)).astype(F32)
    pick_out16 = pick_out.astype(BF16)

    def spread(left, weight):
        half = lax.dot_general(left, weight, (((1,), (1,)), ((), ())), preferred_element_type=F32)
        return lax.dot_general(half.astype(BF16), pick16, (((1,), (1,)), ((), ())), preferred_element_type=F32)

    same = split(iota((size, size), 0), channels)[0] == split(iota((size, size), 1), channels)[0]
    for tap in range(4):
        full = jnp.where(same, spread(pick16, aw_ref[tap]), 0.0).astype(BF16)
        a1_ref[tap // 2, (tap % 2) * size : (tap % 2 + 1) * size, :] = full

    in_column = split(iota((outs, size), 1), channels)[0]
    out_column = split(iota((outs, size), 0), own_out)[1]
    me = lax.axis_index("wide")
    absolute = in_column + me * (2 * own_out) - 1
    inside = (absolute >= 0) & (absolute < 2 * own_out * wide)
    total = jnp.zeros((outs, size), F32)
    for tap in range(TAPS):
        here = (in_column == 2 * out_column + tap) & inside
        total = jnp.where(here, spread(pick_out16, cw_ref[tap]), total)
    a2_ref[...] = total.astype(BF16)

    def along(left, vector_ref, out_ref):
        out_ref[...] = jnp.broadcast_to(jnp.sum(left * vector_ref[...], axis=1, keepdims=True), out_ref.shape)

    along(pick, ab_ref, b1_ref)
    along(pick_out, cb_ref, b2_ref)
    along(pick_out, hw_ref, h_ref)

    turned = rw_ref[...].T
    high = turned.astype(BF16)
    hi_ref[...] = high
    lo_ref[...] = (turned - high.astype(F32)).astype(BF16)


def net_kernel(wide, own_out, *refs):
    views = refs[:wide]
    a1_ref, a2_ref, b1_ref, b2_ref, h_ref, sparse_ref, measured_ref, predicted_ref, residual_ref = refs[wide:]
    size, lanes = views[0].shape
    outs = a2_ref.shape[0]
    me = lax.axis_index("wide")
    group = 2 if wide % 2 == 0 else 1
    wider = lambda ref, times: jnp.concatenate([ref[...]] * times, axis=1)
    b1 = wider(b1_ref, group)
    b2, h = wider(b2_ref, 2 * group), wider(h_ref, 2 * group)
    fold = 8 // own_out
    for start in range(0, wide, group):
        current = jnp.concatenate([views[start + i][...] for i in range(group)], axis=1)
        previous = jnp.concatenate([views[(start + i + 1) % wide][...] for i in range(group)], axis=1)
        upsampled = []
        for e in range(2):
            rows = pl.ds(e * size, size)
            summed = jnp.dot(a1_ref[0, rows, :], current, preferred_element_type=F32)
            summed += jnp.dot(a1_ref[1, rows, :], previous, preferred_element_type=F32)
            upsampled.append(leaky_relu(summed + b1).astype(BF16))
        both = jnp.concatenate(upsampled, axis=1)
        hidden = leaky_relu(jnp.dot(a2_ref[...], both, preferred_element_type=F32) + b2) * h
        part = jnp.sum(hidden.reshape(outs // 8, 8, hidden.shape[1]), axis=0)
        value = part[:own_out]
        for i in range(1, fold):
            value += part[i * own_out : (i + 1) * own_out]
        for e in range(2):
            for i in range(group):
                view = lax.rem(me - (start + i) + wide, wide)
                at = (e * group + i) * lanes
                predicted_ref[2 * view + e] = value[:, at : at + lanes]
    for k in range(measured_ref.shape[0]):
        residual = predicted_ref[sparse_ref[0, k]] - measured_ref[k]
        residual_ref[k * own_out : (k + 1) * own_out, :] = residual


def adjoint_kernel(count, own_out, *refs):
    residuals = refs[:count]
    hi_ref, lo_ref, out_ref = refs[count:]
    lanes = residuals[0].shape[1]
    me = lax.axis_index(("narrow", "pair"))
    total = None
    for shift in range(count):
        block = lax.rem(me - shift + count, count)
        rows = pl.ds(pl.multiple_of(block * lanes, lanes), lanes)
        values = residuals[shift][...]
        high = values.astype(BF16)
        low = (values - high.astype(F32)).astype(BF16)
        term = jnp.dot(high, hi_ref[rows, :], preferred_element_type=F32)
        term += jnp.dot(low, hi_ref[rows, :], preferred_element_type=F32)
        term += jnp.dot(high, lo_ref[rows, :], preferred_element_type=F32)
        total = term if total is None else total + term
    for k in range(out_ref.shape[0]):
        out_ref[k] = total[k * own_out : (k + 1) * own_out]


def send(block, axis, distance):
    count = lax.axis_size(axis)
    return lax.ppermute(block, axis, [(i, (i + distance) % count) for i in range(count)])


def local(
    low_sino,
    angle_weight,
    angle_bias,
    column_weight,
    column_bias,
    head_weight,
    sparse_views,
    measured,
    row_weights,
):
    wide = lax.axis_size("wide")
    group = ("narrow", "pair")
    count = lax.axis_size(group)
    _, channels, width, lanes = low_sino.shape
    own_out = width // wide // 2
    span = 2 * own_out + 2
    size, outs = span * channels, own_out * channels
    shape = jax.ShapeDtypeStruct
    big = 16 if width <= 64 else 48

    windows = call(
        functools.partial(pack_kernel, wide),
        [shape((size, lanes), BF16)] * wide,
        [VMEM],
        [pltpu.VMEM((channels * width, lanes), F32)],
        vmem=big,
    )(low_sino)
    views = [windows[0]] + [send(windows[s], "wide", s) for s in range(1, wide)]

    rows = row_weights.shape[1]
    a1, a2, b1, b2, head, high, low = call(
        functools.partial(expand_kernel, wide, own_out),
        [
            shape((2, 2 * size, size), BF16),
            shape((outs, size), BF16),
            shape((size, lanes), F32),
            shape((outs, lanes), F32),
            shape((outs, lanes), F32),
            shape((rows, lanes), BF16),
            shape((rows, lanes), BF16),
        ],
        [VMEM] * 6,
        vmem=big,
    )(angle_weight, angle_bias[None], column_weight, column_bias[None], head_weight[None], row_weights)

    sparse_count = measured.shape[0]
    predicted, residual = call(
        functools.partial(net_kernel, wide, own_out),
        [shape((2 * wide, own_out, lanes), F32), shape((sparse_count * own_out, lanes), F32)],
        [VMEM] * (wide + 5) + [SMEM, VMEM],
        vmem=big,
    )(*views, a1, a2, b1, b2, head, sparse_views, measured)

    blocks = [residual] + [send(residual, group, s) for s in range(1, count)]
    adjoint = call(
        functools.partial(adjoint_kernel, count, own_out),
        shape((sparse_count, own_out, lanes), F32),
        [VMEM] * (count + 2),
        vmem=big,
    )(*blocks, high, low)
    return (predicted, adjoint)


def solution(mesh):
    in_specs = (
        P(("parts", "wide"), None, None, ("narrow", "pair")),
        P(),
        P(),
        P(),
        P(),
        P(),
        P(("parts", "narrow"), None),
        P("parts", "wide", ("narrow", "pair")),
        P(("narrow", "pair"), None),
    )
    out_specs = (P("parts", "wide", ("narrow", "pair")), P("parts", "wide", ("narrow", "pair")))
    return jax.shard_map(local, mesh=mesh, in_specs=in_specs, out_specs=out_specs, check_vma=False)
```

```python
import functools

import jax
import jax.numpy as jnp
from jax import lax
from jax.experimental import pallas as pl
from jax.experimental.pallas import tpu as pltpu
from jax.sharding import PartitionSpec as P

F32, BF16 = jnp.float32, jnp.bfloat16
VMEM = pl.BlockSpec(memory_space=pltpu.VMEM)
SMEM = pl.BlockSpec(memory_space=pltpu.SMEM)
TAPS = 4


def call(kernel, outs, in_specs, scratch=(), vmem=16, flops=10**6):
    nbytes = sum(o.size * o.dtype.itemsize for o in jax.tree.leaves(outs))
    return pl.pallas_call(
        kernel,
        out_shape=outs,
        in_specs=in_specs,
        out_specs=jax.tree.map(lambda _: VMEM, outs),
        scratch_shapes=list(scratch),
        compiler_params=pltpu.CompilerParams(vmem_limit_bytes=vmem << 20),
        cost_estimate=pl.CostEstimate(flops=flops, bytes_accessed=nbytes, transcendentals=0),
    )


def leaky_relu(values):
    return jnp.maximum(values, 0.1 * values)


def split(index, size):
    whole = ((index.astype(F32) + 0.5) * (1.0 / size)).astype(jnp.int32)
    return whole, index - whole * size


def iota(shape, axis):
    return lax.broadcasted_iota(jnp.int32, shape, axis)


def pack_kernel(wide, low_ref, *refs):
    windows, rows_ref = refs[:-1], refs[-1]
    _, channels, width, rows = low_ref.shape
    rows_ref[...] = low_ref[0].astype(F32).reshape(channels * width, rows)
    own = width // wide
    me = lax.axis_index("wide")
    for shift in range(wide):
        first = lax.rem(me + shift, wide) * own - 1
        columns = []
        for i in range(own + 2):
            column = jnp.clip(first + i, 0, width - 1)
            columns.append(rows_ref[pl.ds(column, channels, stride=width), :])
        windows[shift][...] = jnp.concatenate(columns, axis=0).astype(BF16)


def prepare_kernel(
    wide, own_out, aw_ref, ab_ref, cw_ref, cb_ref, hw_ref, rw_ref, sparse_ref, measured_ref, *refs
):
    waiting, refs = refs[: wide - 1], refs[wide - 1 :]
    onward, refs = refs[: wide - 1], refs[wide - 1 :]
    a1_ref, a2_ref, b1_ref, b2_ref, h_ref, hi_ref, lo_ref, select_ref, target_ref = refs
    for source, copy in zip(waiting, onward):
        copy[...] = source[...]
    channels = aw_ref.shape[1]
    span = 2 * own_out + 2
    size, outs = span * channels, own_out * channels
    rows, columns = split(iota((size, channels), 0), channels)
    pick = (columns == iota((size, channels), 1)).astype(F32)
    pick16 = pick.astype(BF16)
    out_channel, _ = split(iota((outs, channels), 0), own_out)
    pick_out = (out_channel == iota((outs, channels), 1)).astype(F32)
    pick_out16 = pick_out.astype(BF16)

    def spread(left, weight):
        half = lax.dot_general(left, weight, (((1,), (1,)), ((), ())), preferred_element_type=F32)
        return lax.dot_general(half.astype(BF16), pick16, (((1,), (1,)), ((), ())), preferred_element_type=F32)

    same = split(iota((size, size), 0), channels)[0] == split(iota((size, size), 1), channels)[0]
    for tap in range(4):
        full = jnp.where(same, spread(pick16, aw_ref[tap]), 0.0).astype(BF16)
        a1_ref[tap // 2, (tap % 2) * size : (tap % 2 + 1) * size, :] = full

    in_column = split(iota((outs, size), 1), channels)[0]
    out_column = split(iota((outs, size), 0), own_out)[1]
    me = lax.axis_index("wide")
    absolute = in_column + me * (2 * own_out) - 1
    inside = (absolute >= 0) & (absolute < 2 * own_out * wide)
    total = jnp.zeros((outs, size), F32)
    for tap in range(TAPS):
        here = (in_column == 2 * out_column + tap) & inside
        total = jnp.where(here, spread(pick_out16, cw_ref[tap]), total)
    a2_ref[...] = total.astype(BF16)

    def along(left, vector_ref, out_ref):
        out_ref[...] = jnp.broadcast_to(jnp.sum(left * vector_ref[...], axis=1, keepdims=True), out_ref.shape)

    along(pick, ab_ref, b1_ref)
    along(pick_out, cb_ref, b2_ref)
    along(pick_out, hw_ref, h_ref)

    turned = rw_ref[...].T
    high = turned.astype(BF16)
    hi_ref[...] = high
    lo_ref[...] = (turned - high.astype(F32)).astype(BF16)

    for k in range(measured_ref.shape[0]):
        rows = slice(k * own_out, (k + 1) * own_out)
        select_ref[rows, :] = jnp.full((own_out, select_ref.shape[1]), sparse_ref[0, k], jnp.int32)
        target_ref[rows, :] = measured_ref[k]


def net_kernel(wide, own_out, *refs):
    near, wrapped, refs = refs[:wide], refs[wide : 2 * wide - 1], refs[2 * wide - 1 :]
    a1_ref, a2_ref, b1_ref, b2_ref, h_ref, select_ref, target_ref, predicted_ref, residual_ref = refs
    size, lanes = near[0].shape
    outs = a2_ref.shape[0]
    me = lax.axis_index("wide")
    views = [near[0][...]]
    for shift in range(1, wide):
        views.append(jnp.where(me >= shift, near[shift][...], wrapped[shift - 1][...]))
    group = 2 if wide % 2 == 0 else 1
    wider = lambda ref, times: jnp.concatenate([ref[...]] * times, axis=1)
    b1 = wider(b1_ref, group)
    b2, h = wider(b2_ref, 2 * group), wider(h_ref, 2 * group)
    select = select_ref[...]
    picked = jnp.zeros(select.shape, F32)
    for start in range(0, wide, group):
        current = jnp.concatenate([views[start + i] for i in range(group)], axis=1)
        previous = jnp.concatenate([views[(start + i + 1) % wide] for i in range(group)], axis=1)
        upsampled = []
        for e in range(2):
            rows = pl.ds(e * size, size)
            summed = jnp.dot(a1_ref[0, rows, :], current, preferred_element_type=F32)
            summed += jnp.dot(a1_ref[1, rows, :], previous, preferred_element_type=F32)
            upsampled.append(leaky_relu(summed + b1).astype(BF16))
        both = jnp.concatenate(upsampled, axis=1)
        hidden = leaky_relu(jnp.dot(a2_ref[...], both, preferred_element_type=F32) + b2) * h
        value = jnp.sum(hidden.reshape(outs // 8, 8, hidden.shape[1]), axis=0)
        apart = own_out
        while apart < 8:
            value += pltpu.roll(value, apart, 0)
            apart *= 2
        for e in range(2):
            for i in range(group):
                view = 2 * lax.rem(me - (start + i) + wide, wide) + e
                at = (e * group + i) * lanes
                tile = value[:, at : at + lanes]
                predicted_ref[view] = tile[:own_out]
                repeated = jnp.concatenate([tile] * (select.shape[0] // 8), axis=0)
                picked = jnp.where(select == view, repeated, picked)
    residual_ref[...] = (picked - target_ref[...]).astype(BF16)


def adjoint_kernel(count, own_out, *refs):
    residuals = refs[:count]
    hi_ref, lo_ref, predicted_ref, out_ref, copied_ref = refs[count:]
    copied_ref[...] = predicted_ref[...]
    lanes = residuals[0].shape[1]
    me = lax.axis_index(("narrow", "pair"))
    total = None
    for shift in range(count):
        block = lax.rem(me - shift + count, count)
        rows = pl.ds(pl.multiple_of(block * lanes, lanes), lanes)
        values = residuals[shift][...]
        term = jnp.dot(values, hi_ref[rows, :], preferred_element_type=F32)
        term += jnp.dot(values, lo_ref[rows, :], preferred_element_type=F32)
        total = term if total is None else total + term
    for k in range(out_ref.shape[0]):
        out_ref[k] = total[k * own_out : (k + 1) * own_out]


def send(block, axis, distance):
    count = lax.axis_size(axis)
    return lax.ppermute(block, axis, [(i, (i + distance) % count) for i in range(count)])


def send_onward(block, axis, distance):
    count = lax.axis_size(axis)
    return lax.ppermute(block, axis, [(i, i + distance) for i in range(count) if 0 <= i + distance < count])


def local(
    low_sino,
    angle_weight,
    angle_bias,
    column_weight,
    column_bias,
    head_weight,
    sparse_views,
    measured,
    row_weights,
):
    wide = lax.axis_size("wide")
    group = ("narrow", "pair")
    count = lax.axis_size(group)
    _, channels, width, lanes = low_sino.shape
    own_out = width // wide // 2
    span = 2 * own_out + 2
    size, outs = span * channels, own_out * channels
    sparse_count = measured.shape[0]
    shape = jax.ShapeDtypeStruct
    big = 16 if width <= 64 else 48
    window = shape((size, lanes), BF16)

    windows = call(
        functools.partial(pack_kernel, wide),
        [window] * wide,
        [VMEM],
        [pltpu.VMEM((channels * width, lanes), F32)],
        vmem=big,
    )(low_sino)
    wrapped = [send_onward(windows[s], "wide", s - wide) for s in range(1, wide)]

    rows = row_weights.shape[1]
    flat = (sparse_count * own_out, lanes)
    prepared = call(
        functools.partial(prepare_kernel, wide, own_out),
        [window] * (wide - 1)
        + [
            shape((2, 2 * size, size), BF16),
            shape((outs, size), BF16),
            shape((size, lanes), F32),
            shape((outs, lanes), F32),
            shape((outs, lanes), F32),
            shape((rows, lanes), BF16),
            shape((rows, lanes), BF16),
            shape(flat, jnp.int32),
            shape(flat, F32),
        ],
        [VMEM] * 6 + [SMEM] + [VMEM] * wide,
        vmem=big,
    )(
        angle_weight,
        angle_bias[None],
        column_weight,
        column_bias[None],
        head_weight[None],
        row_weights,
        sparse_views,
        measured,
        *windows[1:],
    )
    onward, (a1, a2, b1, b2, head, high, low, select, target) = prepared[: wide - 1], prepared[wide - 1 :]
    near = [windows[0]] + [send_onward(onward[s - 1], "wide", s) for s in range(1, wide)]

    predicted, residual = call(
        functools.partial(net_kernel, wide, own_out),
        [shape((2 * wide, own_out, lanes), F32), shape(flat, BF16)],
        [VMEM] * (2 * wide + 6),
        vmem=big,
    )(*near, *wrapped, a1, a2, b1, b2, head, select, target)

    blocks = [residual] + [send(residual, group, s) for s in range(1, count)]
    adjoint, predicted = call(
        functools.partial(adjoint_kernel, count, own_out),
        [shape((sparse_count, own_out, lanes), F32), shape(predicted.shape, F32)],
        [VMEM] * (count + 3),
        vmem=big,
    )(*blocks, high, low, predicted)
    return (predicted, adjoint)


def solution(mesh):
    in_specs = (
        P(("parts", "wide"), None, None, ("narrow", "pair")),
        P(),
        P(),
        P(),
        P(),
        P(),
        P(("parts", "narrow"), None),
        P("parts", "wide", ("narrow", "pair")),
        P(("narrow", "pair"), None),
    )
    out_specs = (P("parts", "wide", ("narrow", "pair")), P("parts", "wide", ("narrow", "pair")))
    return jax.shard_map(local, mesh=mesh, in_specs=in_specs, out_specs=out_specs, check_vma=False)
```

```python
import functools

import jax
import jax.numpy as jnp
from jax import lax
from jax.experimental import pallas as pl
from jax.experimental.pallas import tpu as pltpu
from jax.sharding import PartitionSpec as P

F32, BF16 = jnp.float32, jnp.bfloat16
VMEM = pl.BlockSpec(memory_space=pltpu.VMEM)
TAPS = 4


def call(kernel, outs, in_specs, scratch=(), vmem=16, flops=10**6):
    nbytes = sum(o.size * o.dtype.itemsize for o in jax.tree.leaves(outs))
    return pl.pallas_call(
        kernel,
        out_shape=outs,
        in_specs=in_specs,
        out_specs=jax.tree.map(lambda _: VMEM, outs),
        scratch_shapes=list(scratch),
        compiler_params=pltpu.CompilerParams(vmem_limit_bytes=vmem << 20),
        cost_estimate=pl.CostEstimate(flops=flops, bytes_accessed=nbytes, transcendentals=0),
    )


def leaky_relu(values):
    return jnp.maximum(values, 0.1 * values)


def split(index, size):
    whole = ((index.astype(F32) + 0.5) * (1.0 / size)).astype(jnp.int32)
    return whole, index - whole * size


def iota(shape, axis):
    return lax.broadcasted_iota(jnp.int32, shape, axis)


def pack_kernel(wide, low_ref, *refs):
    windows, rows_ref = refs[:-1], refs[-1]
    _, channels, width, rows = low_ref.shape
    rows_ref[...] = low_ref[0].astype(F32).reshape(channels * width, rows)
    own = width // wide
    me = lax.axis_index("wide")
    for shift in range(wide):
        first = lax.rem(me + shift, wide) * own - 1
        columns = []
        for i in range(own + 2):
            column = jnp.clip(first + i, 0, width - 1)
            columns.append(rows_ref[pl.ds(column, channels, stride=width), :])
        windows[shift][...] = jnp.concatenate(columns, axis=0).astype(BF16)


def prepare_kernel(
    wide,
    own_out,
    aw_ref,
    ab_ref,
    cw_ref,
    cb_ref,
    hw_ref,
    rw_ref,
    measured_ref,
    sparse_ref,
    a1_ref,
    a2_ref,
    b1_ref,
    b2_ref,
    h_ref,
    hi_ref,
    lo_ref,
    select_ref,
    target_ref,
):
    channels = aw_ref.shape[1]
    span = 2 * own_out + 2
    size, outs = span * channels, own_out * channels
    rows, columns = split(iota((size, channels), 0), channels)
    pick = (columns == iota((size, channels), 1)).astype(F32)
    pick16 = pick.astype(BF16)
    out_channel, _ = split(iota((outs, channels), 0), own_out)
    pick_out = (out_channel == iota((outs, channels), 1)).astype(F32)
    pick_out16 = pick_out.astype(BF16)

    def spread(left, weight):
        half = lax.dot_general(left, weight, (((1,), (1,)), ((), ())), preferred_element_type=F32)
        return lax.dot_general(half.astype(BF16), pick16, (((1,), (1,)), ((), ())), preferred_element_type=F32)

    same = split(iota((size, size), 0), channels)[0] == split(iota((size, size), 1), channels)[0]
    for tap in range(4):
        full = jnp.where(same, spread(pick16, aw_ref[tap]), 0.0).astype(BF16)
        a1_ref[tap // 2, (tap % 2) * size : (tap % 2 + 1) * size, :] = full

    in_column = split(iota((outs, size), 1), channels)[0]
    out_column = split(iota((outs, size), 0), own_out)[1]
    me = lax.axis_index("wide")
    absolute = in_column + me * (2 * own_out) - 1
    inside = (absolute >= 0) & (absolute < 2 * own_out * wide)
    total = jnp.zeros((outs, size), F32)
    for tap in range(TAPS):
        here = (in_column == 2 * out_column + tap) & inside
        total = jnp.where(here, spread(pick_out16, cw_ref[tap]), total)
    a2_ref[...] = total.astype(BF16)

    def along(left, vector_ref, out_ref):
        out_ref[...] = jnp.broadcast_to(jnp.sum(left * vector_ref[...].astype(F32), axis=1, keepdims=True), out_ref.shape)

    along(pick, ab_ref, b1_ref)
    along(pick_out, cb_ref, b2_ref)
    along(pick_out, hw_ref, h_ref)

    turned = rw_ref[...].T
    high = turned.astype(BF16)
    hi_ref[...] = high
    lo_ref[...] = (turned - high.astype(F32)).astype(BF16)

    sparse_count = measured_ref.shape[0]
    wanted = (select_ref.shape[0], sparse_count)
    pick_view = (split(iota(wanted, 0), own_out)[0] == iota(wanted, 1)).astype(F32)
    along(pick_view, sparse_ref, select_ref)
    for k in range(sparse_count):
        target_ref[k * own_out : (k + 1) * own_out, :] = measured_ref[k]


def net_kernel(wide, own_out, *refs):
    views, refs = [ref[...] for ref in refs[:wide]], refs[wide:]
    a1_ref, a2_ref, b1_ref, b2_ref, h_ref, select_ref, target_ref, predicted_ref, residual_ref = refs
    size, lanes = views[0].shape
    outs = a2_ref.shape[0]
    me = lax.axis_index("wide")
    group = 2 if wide % 2 == 0 else 1
    wider = lambda ref, times: jnp.concatenate([ref[...]] * times, axis=1)
    b1 = wider(b1_ref, group)
    b2, h = wider(b2_ref, 2 * group), wider(h_ref, 2 * group)
    select = select_ref[...]
    picked = jnp.zeros(select.shape, F32)
    for start in range(0, wide, group):
        current = jnp.concatenate([views[start + i] for i in range(group)], axis=1)
        previous = jnp.concatenate([views[(start + i + 1) % wide] for i in range(group)], axis=1)
        upsampled = []
        for e in range(2):
            rows = pl.ds(e * size, size)
            summed = jnp.dot(a1_ref[0, rows, :], current, preferred_element_type=F32)
            summed += jnp.dot(a1_ref[1, rows, :], previous, preferred_element_type=F32)
            upsampled.append(leaky_relu(summed + b1).astype(BF16))
        both = jnp.concatenate(upsampled, axis=1)
        hidden = leaky_relu(jnp.dot(a2_ref[...], both, preferred_element_type=F32) + b2) * h
        value = jnp.sum(hidden.reshape(outs // 8, 8, hidden.shape[1]), axis=0)
        apart = own_out
        while apart < 8:
            value += pltpu.roll(value, apart, 0)
            apart *= 2
        for e in range(2):
            for i in range(group):
                view = 2 * lax.rem(me - (start + i) + wide, wide) + e
                at = (e * group + i) * lanes
                tile = value[:, at : at + lanes]
                predicted_ref[view] = tile[:own_out]
                repeated = jnp.concatenate([tile] * (select.shape[0] // 8), axis=0)
                picked = jnp.where(select == view.astype(F32), repeated, picked)
    residual_ref[...] = (picked - target_ref[...]).astype(BF16)


def adjoint_kernel(shifts, own_out, *refs):
    residuals, refs = refs[: len(shifts)], refs[len(shifts) :]
    hi_ref, lo_ref, predicted_ref, out_ref, copied_ref = refs
    copied_ref[...] = predicted_ref[...]
    lanes = residuals[0].shape[1]
    total = None
    for residual_ref, (narrow_shift, pair_shift) in zip(residuals, shifts):
        narrow, pair = came_from("narrow", narrow_shift), came_from("pair", pair_shift)
        block = narrow * lax.axis_size("pair") + pair
        rows = pl.ds(pl.multiple_of(block * lanes, lanes), lanes)
        values = residual_ref[...]
        term = jnp.dot(values, hi_ref[rows, :], preferred_element_type=F32)
        term += jnp.dot(values, lo_ref[rows, :], preferred_element_type=F32)
        total = term if total is None else total + term
    for k in range(out_ref.shape[0]):
        out_ref[k] = total[k * own_out : (k + 1) * own_out]


def came_from(axis, distance):
    count = lax.axis_size(axis)
    return lax.rem(lax.axis_index(axis) - distance + count, count)


def send(block, axis, distance):
    count = lax.axis_size(axis)
    return lax.ppermute(block, axis, [(i, (i + distance) % count) for i in range(count)])


def local(
    low_sino,
    angle_weight,
    angle_bias,
    column_weight,
    column_bias,
    head_weight,
    sparse_views,
    measured,
    row_weights,
):
    wide, narrow, pair = (lax.axis_size(axis) for axis in ("wide", "narrow", "pair"))
    _, channels, width, lanes = low_sino.shape
    own_out = width // wide // 2
    span = 2 * own_out + 2
    size, outs = span * channels, own_out * channels
    sparse_count = measured.shape[0]
    rows = row_weights.shape[1]
    flat = (sparse_count * own_out, lanes)
    shape = jax.ShapeDtypeStruct
    big = 16 if width <= 64 else 48

    small = (
        angle_weight,
        angle_bias[None],
        column_weight,
        column_bias[None],
        head_weight[None],
        row_weights,
        measured,
        sparse_views,
    )
    windows = call(
        functools.partial(pack_kernel, wide),
        [shape((size, lanes), BF16)] * wide,
        [VMEM],
        [pltpu.VMEM((channels * width, lanes), F32)],
        vmem=big,
    )(low_sino)
    views = [windows[0]] + [send(windows[s], "wide", s) for s in range(1, wide)]

    a1, a2, b1, b2, head, high, low, select, target = call(
        functools.partial(prepare_kernel, wide, own_out),
        [
            shape((2, 2 * size, size), BF16),
            shape((outs, size), BF16),
            shape((size, lanes), F32),
            shape((outs, lanes), F32),
            shape((outs, lanes), F32),
            shape((rows, lanes), BF16),
            shape((rows, lanes), BF16),
            shape(flat, F32),
            shape(flat, F32),
        ],
        [VMEM] * 8,
        vmem=big,
    )(*small)

    predicted, residual = call(
        functools.partial(net_kernel, wide, own_out),
        [shape((2 * wide, own_out, lanes), F32), shape(flat, BF16)],
        [VMEM] * (wide + 7),
        vmem=big,
    )(*views, a1, a2, b1, b2, head, select, target)

    shifts = [(0, 0)] + [(s, 0) for s in range(1, narrow)] + [(0, t) for t in range(1, pair)]
    blocks = [residual] + [send(residual, "narrow", s) for s in range(1, narrow)]
    blocks += [send(residual, "pair", t) for t in range(1, pair)]
    for s in range(1, narrow):
        for t in range(1, pair):
            shifts.append((s, t))
            blocks.append(send(blocks[s], "pair", t))
    adjoint, predicted = call(
        functools.partial(adjoint_kernel, shifts, own_out),
        [shape((sparse_count, own_out, lanes), F32), shape(predicted.shape, F32)],
        [VMEM] * (len(blocks) + 3),
        vmem=big,
    )(*blocks, high, low, predicted)
    return (predicted, adjoint)


def solution(mesh):
    in_specs = (
        P(("parts", "wide"), None, None, ("narrow", "pair")),
        P(),
        P(),
        P(),
        P(),
        P(),
        P(("parts", "narrow"), None),
        P("parts", "wide", ("narrow", "pair")),
        P(("narrow", "pair"), None),
    )
    out_specs = (P("parts", "wide", ("narrow", "pair")), P("parts", "wide", ("narrow", "pair")))
    return jax.shard_map(local, mesh=mesh, in_specs=in_specs, out_specs=out_specs, check_vma=False)
```

```python
import functools

import jax
import jax.numpy as jnp
from jax import lax
from jax.experimental import pallas as pl
from jax.experimental.pallas import tpu as pltpu
from jax.sharding import PartitionSpec as P

F32, BF16 = jnp.float32, jnp.bfloat16
VMEM = pl.BlockSpec(memory_space=pltpu.VMEM)
TAPS = 4


def call(kernel, outs, in_specs, scratch=(), vmem=16, flops=10**6):
    nbytes = sum(o.size * o.dtype.itemsize for o in jax.tree.leaves(outs))
    return pl.pallas_call(
        kernel,
        out_shape=outs,
        in_specs=in_specs,
        out_specs=jax.tree.map(lambda _: VMEM, outs),
        scratch_shapes=list(scratch),
        compiler_params=pltpu.CompilerParams(vmem_limit_bytes=vmem << 20),
        cost_estimate=pl.CostEstimate(flops=flops, bytes_accessed=nbytes, transcendentals=0),
    )


def leaky_relu(values):
    return jnp.maximum(values, 0.1 * values)


def split(index, size):
    whole = ((index.astype(F32) + 0.5) * (1.0 / size)).astype(jnp.int32)
    return whole, index - whole * size


def iota(shape, axis):
    return lax.broadcasted_iota(jnp.int32, shape, axis)


def pack_kernel(wide, low_ref, *refs):
    windows, rows_ref = refs[:-1], refs[-1]
    _, channels, width, rows = low_ref.shape
    rows_ref[...] = low_ref[0].astype(F32).reshape(channels * width, rows)
    own = width // wide
    me = lax.axis_index("wide")
    for shift in range(wide):
        first = lax.rem(me + shift, wide) * own - 1
        columns = []
        for i in range(own + 2):
            column = jnp.clip(first + i, 0, width - 1)
            columns.append(rows_ref[pl.ds(column, channels, stride=width), :])
        windows[shift][...] = jnp.concatenate(columns, axis=0).astype(BF16)


def prepare_kernel(
    wide,
    own_out,
    aw_ref,
    ab_ref,
    cw_ref,
    cb_ref,
    hw_ref,
    rw_ref,
    measured_ref,
    sparse_ref,
    a1_ref,
    a2_ref,
    b1_ref,
    b2_ref,
    h_ref,
    hi_ref,
    lo_ref,
    select_ref,
    target_ref,
):
    channels = aw_ref.shape[1]
    span = 2 * own_out + 2
    size, outs = span * channels, own_out * channels
    rows, columns = split(iota((size, channels), 0), channels)
    pick = (columns == iota((size, channels), 1)).astype(F32)
    pick16 = pick.astype(BF16)
    out_channel, _ = split(iota((outs, channels), 0), own_out)
    pick_out = (out_channel == iota((outs, channels), 1)).astype(F32)
    pick_out16 = pick_out.astype(BF16)

    def spread(left, weight):
        half = lax.dot_general(left, weight, (((1,), (1,)), ((), ())), preferred_element_type=F32)
        return lax.dot_general(half.astype(BF16), pick16, (((1,), (1,)), ((), ())), preferred_element_type=F32)

    same = split(iota((size, size), 0), channels)[0] == split(iota((size, size), 1), channels)[0]
    for tap in range(4):
        full = jnp.where(same, spread(pick16, aw_ref[tap]), 0.0).astype(BF16)
        a1_ref[tap // 2, (tap % 2) * size : (tap % 2 + 1) * size, :] = full

    in_column = split(iota((outs, size), 1), channels)[0]
    out_column = split(iota((outs, size), 0), own_out)[1]
    me = lax.axis_index("wide")
    absolute = in_column + me * (2 * own_out) - 1
    inside = (absolute >= 0) & (absolute < 2 * own_out * wide)
    total = jnp.zeros((outs, size), F32)
    for tap in range(TAPS):
        here = (in_column == 2 * out_column + tap) & inside
        total = jnp.where(here, spread(pick_out16, cw_ref[tap]), total)
    a2_ref[...] = total.astype(BF16)

    def along(left, vector_ref, out_ref):
        out_ref[...] = jnp.broadcast_to(jnp.sum(left * vector_ref[...].astype(F32), axis=1, keepdims=True), out_ref.shape)

    along(pick, ab_ref, b1_ref)
    along(pick_out, cb_ref, b2_ref)
    along(pick_out, hw_ref, h_ref)

    turned = rw_ref[...].T
    high = turned.astype(BF16)
    hi_ref[...] = high
    lo_ref[...] = (turned - high.astype(F32)).astype(BF16)

    sparse_count = measured_ref.shape[0]
    wanted = (select_ref.shape[0], sparse_count)
    pick_view = (split(iota(wanted, 0), own_out)[0] == iota(wanted, 1)).astype(F32)
    along(pick_view, sparse_ref, select_ref)
    for k in range(sparse_count):
        target_ref[k * own_out : (k + 1) * own_out, :] = measured_ref[k]


def net_kernel(wide, own_out, *refs):
    views, refs = [ref[...] for ref in refs[:wide]], refs[wide:]
    a1_ref, a2_ref, b1_ref, b2_ref, h_ref, select_ref, target_ref, predicted_ref, residual_ref = refs
    size, lanes = views[0].shape
    outs = a2_ref.shape[0]
    me = lax.axis_index("wide")
    group = 2 if wide % 2 == 0 else 1
    wider = lambda ref, times: jnp.concatenate([ref[...]] * times, axis=1)
    b1 = wider(b1_ref, group)
    b2, h = wider(b2_ref, 2 * group), wider(h_ref, 2 * group)
    select = select_ref[...]
    picked = jnp.zeros(select.shape, F32)
    for start in range(0, wide, group):
        current = jnp.concatenate([views[start + i] for i in range(group)], axis=1)
        previous = jnp.concatenate([views[(start + i + 1) % wide] for i in range(group)], axis=1)
        upsampled = []
        for e in range(2):
            rows = pl.ds(e * size, size)
            summed = jnp.dot(a1_ref[0, rows, :], current, preferred_element_type=F32)
            summed += jnp.dot(a1_ref[1, rows, :], previous, preferred_element_type=F32)
            upsampled.append(leaky_relu(summed + b1).astype(BF16))
        both = jnp.concatenate(upsampled, axis=1)
        hidden = leaky_relu(jnp.dot(a2_ref[...], both, preferred_element_type=F32) + b2) * h
        value = jnp.sum(hidden.reshape(outs // 8, 8, hidden.shape[1]), axis=0)
        apart = own_out
        while apart < 8:
            value += pltpu.roll(value, apart, 0)
            apart *= 2
        for e in range(2):
            for i in range(group):
                view = 2 * lax.rem(me - (start + i) + wide, wide) + e
                at = (e * group + i) * lanes
                tile = value[:, at : at + lanes]
                predicted_ref[view] = tile[:own_out]
                repeated = jnp.concatenate([tile] * (select.shape[0] // 8), axis=0)
                picked = jnp.where(select == view.astype(F32), repeated, picked)
    residual_ref[...] = (picked - target_ref[...]).astype(BF16)


def adjoint_kernel(own_out, residual_ref, hi_ref, lo_ref, predicted_ref, out_ref, copied_ref):
    copied_ref[...] = predicted_ref[...]
    count, size, lanes = residual_ref.shape
    total = jnp.zeros((size, lanes), F32)
    for block in range(count):
        rows = slice(block * lanes, (block + 1) * lanes)
        total += jnp.dot(residual_ref[block], hi_ref[rows, :], preferred_element_type=F32)
        total += jnp.dot(residual_ref[block], lo_ref[rows, :], preferred_element_type=F32)
    for k in range(out_ref.shape[0]):
        out_ref[k] = total[k * own_out : (k + 1) * own_out]


def send(block, axis, distance):
    count = lax.axis_size(axis)
    return lax.ppermute(block, axis, [(i, (i + distance) % count) for i in range(count)])


def local(
    low_sino,
    angle_weight,
    angle_bias,
    column_weight,
    column_bias,
    head_weight,
    sparse_views,
    measured,
    row_weights,
):
    wide = lax.axis_size("wide")
    _, channels, width, lanes = low_sino.shape
    own_out = width // wide // 2
    span = 2 * own_out + 2
    size, outs = span * channels, own_out * channels
    sparse_count = measured.shape[0]
    rows = row_weights.shape[1]
    flat = (sparse_count * own_out, lanes)
    shape = jax.ShapeDtypeStruct
    big = 16 if width <= 64 else 48

    small = (
        angle_weight,
        angle_bias[None],
        column_weight,
        column_bias[None],
        head_weight[None],
        row_weights,
        measured,
        sparse_views,
    )
    windows = call(
        functools.partial(pack_kernel, wide),
        [shape((size, lanes), BF16)] * wide,
        [VMEM],
        [pltpu.VMEM((channels * width, lanes), F32)],
        vmem=big,
    )(low_sino)
    views = [windows[0]] + [send(windows[s], "wide", s) for s in range(1, wide)]

    a1, a2, b1, b2, head, high, low, select, target = call(
        functools.partial(prepare_kernel, wide, own_out),
        [
            shape((2, 2 * size, size), BF16),
            shape((outs, size), BF16),
            shape((size, lanes), F32),
            shape((outs, lanes), F32),
            shape((outs, lanes), F32),
            shape((rows, lanes), BF16),
            shape((rows, lanes), BF16),
            shape(flat, F32),
            shape(flat, F32),
        ],
        [VMEM] * 8,
        vmem=big,
    )(*small)

    predicted, residual = call(
        functools.partial(net_kernel, wide, own_out),
        [shape((2 * wide, own_out, lanes), F32), shape(flat, BF16)],
        [VMEM] * (wide + 7),
        vmem=big,
    )(*views, a1, a2, b1, b2, head, select, target)

    gathered = lax.all_gather(residual, ("narrow", "pair"), axis=0)
    adjoint, predicted = call(
        functools.partial(adjoint_kernel, own_out),
        [shape((sparse_count, own_out, lanes), F32), shape(predicted.shape, F32)],
        [VMEM] * 4,
        vmem=big,
    )(gathered, high, low, predicted)
    return (predicted, adjoint)


def solution(mesh):
    in_specs = (
        P(("parts", "wide"), None, None, ("narrow", "pair")),
        P(),
        P(),
        P(),
        P(),
        P(),
        P(("parts", "narrow"), None),
        P("parts", "wide", ("narrow", "pair")),
        P(("narrow", "pair"), None),
    )
    out_specs = (P("parts", "wide", ("narrow", "pair")), P("parts", "wide", ("narrow", "pair")))
    return jax.shard_map(local, mesh=mesh, in_specs=in_specs, out_specs=out_specs, check_vma=False)
```

```python
import functools

import jax
import jax.numpy as jnp
from jax import lax
from jax.experimental import pallas as pl
from jax.experimental.pallas import tpu as pltpu
from jax.sharding import PartitionSpec as P

F32, BF16 = jnp.float32, jnp.bfloat16
VMEM = pl.BlockSpec(memory_space=pltpu.VMEM)
TAPS = 4


def call(kernel, outs, in_specs, scratch=(), vmem=16, flops=10**6):
    nbytes = sum(o.size * o.dtype.itemsize for o in jax.tree.leaves(outs))
    return pl.pallas_call(
        kernel,
        out_shape=outs,
        in_specs=in_specs,
        out_specs=jax.tree.map(lambda _: VMEM, outs),
        scratch_shapes=list(scratch),
        compiler_params=pltpu.CompilerParams(vmem_limit_bytes=vmem << 20),
        cost_estimate=pl.CostEstimate(flops=flops, bytes_accessed=nbytes, transcendentals=0),
    )


def leaky_relu(values):
    return jnp.maximum(values, 0.1 * values)


def split(index, size):
    whole = ((index.astype(F32) + 0.5) * (1.0 / size)).astype(jnp.int32)
    return whole, index - whole * size


def iota(shape, axis):
    return lax.broadcasted_iota(jnp.int32, shape, axis)


def pack_kernel(wide, low_ref, *refs):
    windows, rows_ref = refs[:-1], refs[-1]
    _, channels, width, rows = low_ref.shape
    rows_ref[...] = low_ref[0].astype(F32).reshape(channels * width, rows)
    own = width // wide
    me = lax.axis_index("wide")
    for shift in range(wide):
        first = lax.rem(me + shift, wide) * own - 1
        columns = []
        for i in range(own + 2):
            column = jnp.clip(first + i, 0, width - 1)
            columns.append(rows_ref[pl.ds(column, channels, stride=width), :])
        windows[shift][...] = jnp.concatenate(columns, axis=0).astype(BF16)


def prepare_kernel(
    wide,
    own_out,
    aw_ref,
    ab_ref,
    cw_ref,
    cb_ref,
    hw_ref,
    rw_ref,
    measured_ref,
    sparse_ref,
    a1_ref,
    a2_ref,
    b1_ref,
    b2_ref,
    h_ref,
    turned_ref,
    select_ref,
    target_ref,
):
    channels = aw_ref.shape[1]
    span = 2 * own_out + 2
    size, outs = span * channels, own_out * channels
    rows, columns = split(iota((size, channels), 0), channels)
    pick = (columns == iota((size, channels), 1)).astype(F32)
    pick16 = pick.astype(BF16)
    out_channel, _ = split(iota((outs, channels), 0), own_out)
    pick_out = (out_channel == iota((outs, channels), 1)).astype(F32)
    pick_out16 = pick_out.astype(BF16)

    def spread(left, weight):
        half = lax.dot_general(left, weight, (((1,), (1,)), ((), ())), preferred_element_type=F32)
        return lax.dot_general(half.astype(BF16), pick16, (((1,), (1,)), ((), ())), preferred_element_type=F32)

    same = split(iota((size, size), 0), channels)[0] == split(iota((size, size), 1), channels)[0]
    for tap in range(4):
        full = jnp.where(same, spread(pick16, aw_ref[tap]), 0.0).astype(BF16)
        a1_ref[tap // 2, (tap % 2) * size : (tap % 2 + 1) * size, :] = full

    in_column = split(iota((outs, size), 1), channels)[0]
    out_column = split(iota((outs, size), 0), own_out)[1]
    me = lax.axis_index("wide")
    absolute = in_column + me * (2 * own_out) - 1
    inside = (absolute >= 0) & (absolute < 2 * own_out * wide)
    total = jnp.zeros((outs, size), F32)
    for tap in range(TAPS):
        here = (in_column == 2 * out_column + tap) & inside
        total = jnp.where(here, spread(pick_out16, cw_ref[tap]), total)
    a2_ref[...] = total.astype(BF16)

    def along(left, vector_ref, out_ref):
        out_ref[...] = jnp.broadcast_to(jnp.sum(left * vector_ref[...].astype(F32), axis=1, keepdims=True), out_ref.shape)

    along(pick, ab_ref, b1_ref)
    along(pick_out, cb_ref, b2_ref)
    along(pick_out, hw_ref, h_ref)

    turned = rw_ref[...].T
    high = turned.astype(BF16)
    turned_ref[:, : high.shape[1]] = high
    turned_ref[:, high.shape[1] :] = (turned - high.astype(F32)).astype(BF16)

    sparse_count = measured_ref.shape[0]
    wanted = (select_ref.shape[0], sparse_count)
    pick_view = (split(iota(wanted, 0), own_out)[0] == iota(wanted, 1)).astype(F32)
    along(pick_view, sparse_ref, select_ref)
    for k in range(sparse_count):
        target_ref[k * own_out : (k + 1) * own_out, :] = measured_ref[k]


def net_kernel(wide, own_out, *refs):
    views, refs = [ref[...] for ref in refs[:wide]], refs[wide:]
    a1_ref, a2_ref, b1_ref, b2_ref, h_ref, select_ref, target_ref, predicted_ref, residual_ref = refs
    size, lanes = views[0].shape
    outs = a2_ref.shape[0]
    me = lax.axis_index("wide")
    group = 2 if wide % 2 == 0 else 1
    wider = lambda ref, times: jnp.concatenate([ref[...]] * times, axis=1)
    b1 = wider(b1_ref, group)
    b2, h = wider(b2_ref, 2 * group), wider(h_ref, 2 * group)
    select = select_ref[...]
    picked = jnp.zeros(select.shape, F32)
    for start in range(0, wide, group):
        current = jnp.concatenate([views[start + i] for i in range(group)], axis=1)
        previous = jnp.concatenate([views[(start + i + 1) % wide] for i in range(group)], axis=1)
        upsampled = []
        for e in range(2):
            rows = pl.ds(e * size, size)
            summed = jnp.dot(a1_ref[0, rows, :], current, preferred_element_type=F32)
            summed += jnp.dot(a1_ref[1, rows, :], previous, preferred_element_type=F32)
            upsampled.append(leaky_relu(summed + b1).astype(BF16))
        both = jnp.concatenate(upsampled, axis=1)
        hidden = leaky_relu(jnp.dot(a2_ref[...], both, preferred_element_type=F32) + b2) * h
        value = jnp.sum(hidden.reshape(outs // 8, 8, hidden.shape[1]), axis=0)
        apart = own_out
        while apart < 8:
            value += pltpu.roll(value, apart, 0)
            apart *= 2
        for e in range(2):
            for i in range(group):
                view = 2 * lax.rem(me - (start + i) + wide, wide) + e
                at = (e * group + i) * lanes
                tile = value[:, at : at + lanes]
                predicted_ref[view] = tile[:own_out]
                repeated = jnp.concatenate([tile] * (select.shape[0] // 8), axis=0)
                picked = jnp.where(select == view.astype(F32), repeated, picked)
    residual_ref[...] = (picked - target_ref[...]).astype(BF16)


def adjoint_kernel(shifts, own_out, *refs):
    residuals, refs = refs[: len(shifts)], refs[len(shifts) :]
    turned_ref, predicted_ref, out_ref, copied_ref = refs
    copied_ref[...] = predicted_ref[...]
    lanes = residuals[0].shape[1]
    weights = []
    for narrow_shift, pair_shift in shifts:
        narrow, pair = came_from("narrow", narrow_shift), came_from("pair", pair_shift)
        block = narrow * lax.axis_size("pair") + pair
        weights.append(turned_ref[pl.ds(pl.multiple_of(block * lanes, lanes), lanes), :])
    values = jnp.concatenate([ref[...] for ref in residuals], axis=1)
    both = jnp.dot(values, jnp.concatenate(weights, axis=0), preferred_element_type=F32)
    total = both[:, :lanes] + both[:, lanes:]
    for k in range(out_ref.shape[0]):
        out_ref[k] = total[k * own_out : (k + 1) * own_out]


def came_from(axis, distance):
    count = lax.axis_size(axis)
    return lax.rem(lax.axis_index(axis) - distance + count, count)


def send(block, axis, distance):
    count = lax.axis_size(axis)
    return lax.ppermute(block, axis, [(i, (i + distance) % count) for i in range(count)])


def send_both(block, narrow_distance, pair_distance):
    narrow, pair = lax.axis_size("narrow"), lax.axis_size("pair")
    route = []
    for i in range(narrow):
        for j in range(pair):
            target = (i + narrow_distance) % narrow * pair + (j + pair_distance) % pair
            route.append((i * pair + j, target))
    return lax.ppermute(block, ("narrow", "pair"), route)


def local(
    low_sino,
    angle_weight,
    angle_bias,
    column_weight,
    column_bias,
    head_weight,
    sparse_views,
    measured,
    row_weights,
):
    wide, narrow, pair = (lax.axis_size(axis) for axis in ("wide", "narrow", "pair"))
    _, channels, width, lanes = low_sino.shape
    own_out = width // wide // 2
    span = 2 * own_out + 2
    size, outs = span * channels, own_out * channels
    sparse_count = measured.shape[0]
    rows = row_weights.shape[1]
    flat = (sparse_count * own_out, lanes)
    shape = jax.ShapeDtypeStruct
    big = 16 if width <= 64 else 48

    small = (
        angle_weight,
        angle_bias[None],
        column_weight,
        column_bias[None],
        head_weight[None],
        row_weights,
        measured,
        sparse_views,
    )
    windows = call(
        functools.partial(pack_kernel, wide),
        [shape((size, lanes), BF16)] * wide,
        [VMEM],
        [pltpu.VMEM((channels * width, lanes), F32)],
        vmem=big,
    )(low_sino)
    views = [windows[0]] + [send(windows[s], "wide", s) for s in range(1, wide)]

    a1, a2, b1, b2, head, turned, select, target = call(
        functools.partial(prepare_kernel, wide, own_out),
        [
            shape((2, 2 * size, size), BF16),
            shape((outs, size), BF16),
            shape((size, lanes), F32),
            shape((outs, lanes), F32),
            shape((outs, lanes), F32),
            shape((rows, 2 * lanes), BF16),
            shape(flat, F32),
            shape(flat, F32),
        ],
        [VMEM] * 8,
        vmem=big,
    )(*small)

    predicted, residual = call(
        functools.partial(net_kernel, wide, own_out),
        [shape((2 * wide, own_out, lanes), F32), shape(flat, BF16)],
        [VMEM] * (wide + 7),
        vmem=big,
    )(*views, a1, a2, b1, b2, head, select, target)

    shifts = [(s, t) for s in range(1, narrow) for t in range(1, pair)]
    shifts += [(s, 0) for s in range(1, narrow)] + [(0, t) for t in range(1, pair)]
    blocks = [residual] + [send_both(residual, s, t) for s, t in shifts]
    shifts.insert(0, (0, 0))
    adjoint, predicted = call(
        functools.partial(adjoint_kernel, shifts, own_out),
        [shape((sparse_count, own_out, lanes), F32), shape(predicted.shape, F32)],
        [VMEM] * (len(blocks) + 2),
        vmem=big,
    )(*blocks, turned, predicted)
    return (predicted, adjoint)


def solution(mesh):
    in_specs = (
        P(("parts", "wide"), None, None, ("narrow", "pair")),
        P(),
        P(),
        P(),
        P(),
        P(),
        P(("parts", "narrow"), None),
        P("parts", "wide", ("narrow", "pair")),
        P(("narrow", "pair"), None),
    )
    out_specs = (P("parts", "wide", ("narrow", "pair")), P("parts", "wide", ("narrow", "pair")))
    return jax.shard_map(local, mesh=mesh, in_specs=in_specs, out_specs=out_specs, check_vma=False)
```

```python
import functools

import jax
import jax.numpy as jnp
from jax import lax
from jax.experimental import pallas as pl
from jax.experimental.pallas import tpu as pltpu
from jax.sharding import PartitionSpec as P

F32, BF16 = jnp.float32, jnp.bfloat16
VMEM = pl.BlockSpec(memory_space=pltpu.VMEM)
TAPS = 4


def call(kernel, outs, in_specs, scratch=(), vmem=16, flops=10**6):
    nbytes = sum(o.size * o.dtype.itemsize for o in jax.tree.leaves(outs))
    return pl.pallas_call(
        kernel,
        out_shape=outs,
        in_specs=in_specs,
        out_specs=jax.tree.map(lambda _: VMEM, outs),
        scratch_shapes=list(scratch),
        compiler_params=pltpu.CompilerParams(vmem_limit_bytes=int(vmem * 2**20)),
        cost_estimate=pl.CostEstimate(flops=flops, bytes_accessed=nbytes, transcendentals=0),
    )


def leaky_relu(values):
    return jnp.maximum(values, 0.1 * values)


def split(index, size):
    whole = ((index.astype(F32) + 0.5) * (1.0 / size)).astype(jnp.int32)
    return whole, index - whole * size


def iota(shape, axis):
    return lax.broadcasted_iota(jnp.int32, shape, axis)


def pack_kernel(wide, low_ref, *refs):
    windows, (block_ref, rows_ref, sems) = refs[:wide], refs[wide:]
    _, channels, width, rows = low_ref.shape
    parts = sems.shape[0]
    each = channels // parts
    pieces = []
    for i in range(parts):
        piece = pl.ds(i * each, each)
        pieces.append(pltpu.make_async_copy(low_ref.at[0, piece], block_ref.at[piece], sems.at[i]))
        pieces[-1].start()
    for i in range(parts):
        pieces[i].wait()
        values = block_ref[i * each : (i + 1) * each].astype(F32).reshape(each * width, rows)
        rows_ref[i * each * width : (i + 1) * each * width, :] = values
    own = width // wide
    me = lax.axis_index("wide")
    for shift in range(wide):
        first = lax.rem(me + shift, wide) * own - 1
        columns = []
        for i in range(own + 2):
            column = jnp.clip(first + i, 0, width - 1)
            columns.append(rows_ref[pl.ds(column, channels, stride=width), :])
        windows[shift][...] = jnp.concatenate(columns, axis=0).astype(BF16)


def prepare_kernel(
    wide,
    own_out,
    aw_ref,
    ab_ref,
    cw_ref,
    cb_ref,
    hw_ref,
    rw_ref,
    measured_ref,
    sparse_ref,
    a1_ref,
    a2_ref,
    b1_ref,
    b2_ref,
    h_ref,
    turned_ref,
    select_ref,
    target_ref,
):
    channels = aw_ref.shape[1]
    span = 2 * own_out + 2
    size, outs = span * channels, own_out * channels
    rows, columns = split(iota((size, channels), 0), channels)
    pick = (columns == iota((size, channels), 1)).astype(F32)
    pick16 = pick.astype(BF16)
    out_channel, _ = split(iota((outs, channels), 0), own_out)
    pick_out = (out_channel == iota((outs, channels), 1)).astype(F32)
    pick_out16 = pick_out.astype(BF16)

    def spread(left, weight):
        half = lax.dot_general(left, weight, (((1,), (1,)), ((), ())), preferred_element_type=F32)
        return lax.dot_general(half.astype(BF16), pick16, (((1,), (1,)), ((), ())), preferred_element_type=F32)

    same = split(iota((size, size), 0), channels)[0] == split(iota((size, size), 1), channels)[0]
    for tap in range(4):
        full = jnp.where(same, spread(pick16, aw_ref[tap]), 0.0).astype(BF16)
        a1_ref[tap // 2, (tap % 2) * size : (tap % 2 + 1) * size, :] = full

    in_column = split(iota((outs, size), 1), channels)[0]
    out_column = split(iota((outs, size), 0), own_out)[1]
    me = lax.axis_index("wide")
    absolute = in_column + me * (2 * own_out) - 1
    inside = (absolute >= 0) & (absolute < 2 * own_out * wide)
    total = jnp.zeros((outs, size), F32)
    for tap in range(TAPS):
        here = (in_column == 2 * out_column + tap) & inside
        total = jnp.where(here, spread(pick_out16, cw_ref[tap]), total)
    a2_ref[...] = total.astype(BF16)

    def along(left, vector_ref, out_ref):
        out_ref[...] = jnp.broadcast_to(jnp.sum(left * vector_ref[...].astype(F32), axis=1, keepdims=True), out_ref.shape)

    along(pick, ab_ref, b1_ref)
    along(pick_out, cb_ref, b2_ref)
    along(pick_out, hw_ref, h_ref)

    turned = rw_ref[...].T
    high = turned.astype(BF16)
    turned_ref[:, : high.shape[1]] = high
    turned_ref[:, high.shape[1] :] = (turned - high.astype(F32)).astype(BF16)

    sparse_count = measured_ref.shape[0]
    wanted = (select_ref.shape[0], sparse_count)
    pick_view = (split(iota(wanted, 0), own_out)[0] == iota(wanted, 1)).astype(F32)
    along(pick_view, sparse_ref, select_ref)
    for k in range(sparse_count):
        target_ref[k * own_out : (k + 1) * own_out, :] = measured_ref[k]


def net_kernel(wide, own_out, *refs):
    views, refs = [ref[...] for ref in refs[:wide]], refs[wide:]
    a1_ref, a2_ref, b1_ref, b2_ref, h_ref, select_ref, target_ref, predicted_ref, residual_ref = refs
    size, lanes = views[0].shape
    outs = a2_ref.shape[0]
    me = lax.axis_index("wide")
    group = 2 if wide % 2 == 0 else 1
    wider = lambda ref, times: jnp.concatenate([ref[...]] * times, axis=1)
    b1 = wider(b1_ref, group)
    b2, h = wider(b2_ref, 2 * group), wider(h_ref, 2 * group)
    select = select_ref[...]
    picked = jnp.zeros(select.shape, F32)
    for start in range(0, wide, group):
        current = jnp.concatenate([views[start + i] for i in range(group)], axis=1)
        previous = jnp.concatenate([views[(start + i + 1) % wide] for i in range(group)], axis=1)
        upsampled = []
        for e in range(2):
            rows = pl.ds(e * size, size)
            summed = jnp.dot(a1_ref[0, rows, :], current, preferred_element_type=F32)
            summed += jnp.dot(a1_ref[1, rows, :], previous, preferred_element_type=F32)
            upsampled.append(leaky_relu(summed + b1).astype(BF16))
        both = jnp.concatenate(upsampled, axis=1)
        hidden = leaky_relu(jnp.dot(a2_ref[...], both, preferred_element_type=F32) + b2) * h
        value = jnp.sum(hidden.reshape(outs // 8, 8, hidden.shape[1]), axis=0)
        apart = own_out
        while apart < 8:
            value += pltpu.roll(value, apart, 0)
            apart *= 2
        for e in range(2):
            for i in range(group):
                view = 2 * lax.rem(me - (start + i) + wide, wide) + e
                at = (e * group + i) * lanes
                tile = value[:, at : at + lanes]
                predicted_ref[view] = tile[:own_out]
                repeated = jnp.concatenate([tile] * (select.shape[0] // 8), axis=0)
                picked = jnp.where(select == view.astype(F32), repeated, picked)
    residual_ref[...] = (picked - target_ref[...]).astype(BF16)


def adjoint_kernel(shifts, own_out, *refs):
    residuals, refs = refs[: len(shifts)], refs[len(shifts) :]
    turned_ref, predicted_ref, out_ref, copied_ref = refs
    copied_ref[...] = predicted_ref[...]
    lanes = residuals[0].shape[1]
    weights = []
    for narrow_shift, pair_shift in shifts:
        narrow, pair = came_from("narrow", narrow_shift), came_from("pair", pair_shift)
        block = narrow * lax.axis_size("pair") + pair
        weights.append(turned_ref[pl.ds(pl.multiple_of(block * lanes, lanes), lanes), :])
    values = jnp.concatenate([ref[...] for ref in residuals], axis=1)
    both = jnp.dot(values, jnp.concatenate(weights, axis=0), preferred_element_type=F32)
    total = both[:, :lanes] + both[:, lanes:]
    for k in range(out_ref.shape[0]):
        out_ref[k] = total[k * own_out : (k + 1) * own_out]


def came_from(axis, distance):
    count = lax.axis_size(axis)
    return lax.rem(lax.axis_index(axis) - distance + count, count)


def send(block, axis, distance):
    count = lax.axis_size(axis)
    return lax.ppermute(block, axis, [(i, (i + distance) % count) for i in range(count)])


def send_both(block, narrow_distance, pair_distance):
    narrow, pair = lax.axis_size("narrow"), lax.axis_size("pair")
    route = []
    for i in range(narrow):
        for j in range(pair):
            target = (i + narrow_distance) % narrow * pair + (j + pair_distance) % pair
            route.append((i * pair + j, target))
    return lax.ppermute(block, ("narrow", "pair"), route)


def local(
    low_sino,
    angle_weight,
    angle_bias,
    column_weight,
    column_bias,
    head_weight,
    sparse_views,
    measured,
    row_weights,
):
    wide, narrow, pair = (lax.axis_size(axis) for axis in ("wide", "narrow", "pair"))
    _, channels, width, lanes = low_sino.shape
    own_out = width // wide // 2
    span = 2 * own_out + 2
    size, outs = span * channels, own_out * channels
    sparse_count = measured.shape[0]
    rows = row_weights.shape[1]
    flat = (sparse_count * own_out, lanes)
    shape = jax.ShapeDtypeStruct
    big = 16 if width <= 64 else 48

    small = (
        angle_weight,
        angle_bias[None],
        column_weight,
        column_bias[None],
        head_weight[None],
        row_weights,
        measured,
        sparse_views,
    )
    windows = call(
        functools.partial(pack_kernel, wide),
        [shape((size, lanes), BF16)] * wide,
        [pl.BlockSpec(memory_space=pltpu.HBM)],
        [
            pltpu.VMEM((channels, width, lanes), BF16),
            pltpu.VMEM((channels * width, lanes), F32),
            pltpu.SemaphoreType.DMA((4,)),
        ],
        vmem=53.6 if width <= 64 else 48,
    )(low_sino)
    views = [windows[0]] + [send(windows[s], "wide", s) for s in range(1, wide)]

    a1, a2, b1, b2, head, turned, select, target = call(
        functools.partial(prepare_kernel, wide, own_out),
        [
            shape((2, 2 * size, size), BF16),
            shape((outs, size), BF16),
            shape((size, lanes), F32),
            shape((outs, lanes), F32),
            shape((outs, lanes), F32),
            shape((rows, 2 * lanes), BF16),
            shape(flat, F32),
            shape(flat, F32),
        ],
        [VMEM] * 8,
        vmem=big,
    )(*small)

    predicted, residual = call(
        functools.partial(net_kernel, wide, own_out),
        [shape((2 * wide, own_out, lanes), F32), shape(flat, BF16)],
        [VMEM] * (wide + 7),
        vmem=big,
    )(*views, a1, a2, b1, b2, head, select, target)

    shifts = [(0, t) for t in range(1, pair)] + [(s, 0) for s in range(1, narrow)]
    shifts += [(s, t) for s in range(1, narrow) for t in range(1, pair)]
    blocks = [residual] + [send_both(residual, s, t) for s, t in shifts]
    shifts.insert(0, (0, 0))
    adjoint, predicted = call(
        functools.partial(adjoint_kernel, shifts, own_out),
        [shape((sparse_count, own_out, lanes), F32), shape(predicted.shape, F32)],
        [VMEM] * (len(blocks) + 2),
        vmem=big,
    )(*blocks, turned, predicted)
    return (predicted, adjoint)


def solution(mesh):
    in_specs = (
        P(("parts", "wide"), None, None, ("narrow", "pair")),
        P(),
        P(),
        P(),
        P(),
        P(),
        P(("parts", "narrow"), None),
        P("parts", "wide", ("narrow", "pair")),
        P(("narrow", "pair"), None),
    )
    out_specs = (P("parts", "wide", ("narrow", "pair")), P("parts", "wide", ("narrow", "pair")))
    return jax.shard_map(local, mesh=mesh, in_specs=in_specs, out_specs=out_specs, check_vma=False)
```

```python
import functools

import jax
import jax.numpy as jnp
from jax import lax
from jax.experimental import pallas as pl
from jax.experimental.pallas import tpu as pltpu
from jax.sharding import PartitionSpec as P

F32, BF16 = jnp.float32, jnp.bfloat16
VMEM = pl.BlockSpec(memory_space=pltpu.VMEM)
TAPS = 4


def call(kernel, outs, in_specs, scratch=(), vmem=16, flops=10**6):
    nbytes = sum(o.size * o.dtype.itemsize for o in jax.tree.leaves(outs))
    return pl.pallas_call(
        kernel,
        out_shape=outs,
        in_specs=in_specs,
        out_specs=jax.tree.map(lambda _: VMEM, outs),
        scratch_shapes=list(scratch),
        compiler_params=pltpu.CompilerParams(vmem_limit_bytes=int(vmem * 2**20)),
        cost_estimate=pl.CostEstimate(flops=flops, bytes_accessed=nbytes, transcendentals=0),
    )


def leaky_relu(values):
    return jnp.maximum(values, 0.1 * values)


def split(index, size):
    whole = ((index.astype(F32) + 0.5) * (1.0 / size)).astype(jnp.int32)
    return whole, index - whole * size


def iota(shape, axis):
    return lax.broadcasted_iota(jnp.int32, shape, axis)


def rounds(count):
    if count == 4:
        return [(2, 3, 1, 0), (3, 2, 0, 1), (1, 0, 3, 2)]
    return [tuple((i + shift) % count for i in range(count)) for shift in range(1, count)]


def entry(table, index):
    value = jnp.int32(table[0])
    for i in range(1, len(table)):
        value = jnp.where(index == i, jnp.int32(table[i]), value)
    return value


def column_groups(channels, span):
    most = max(1, 256 // (2 * channels) // 2 * 2)
    return [(first, min(most, span - first)) for first in range(0, span, most)]


def pack_kernel(routes, low_ref, *refs):
    windows, (block_ref, rows_ref, sems) = refs[: len(routes) + 1], refs[len(routes) + 1 :]
    _, channels, width, rows = low_ref.shape
    parts = sems.shape[0]
    each = channels // parts
    pieces = []
    for i in range(parts):
        piece = pl.ds(i * each, each)
        pieces.append(pltpu.make_async_copy(low_ref.at[0, piece], block_ref.at[piece], sems.at[i]))
        pieces[-1].start()
    edge = jnp.zeros((8, rows), F32)
    rows_ref[0:8, :] = edge
    rows_ref[8 + channels * width : 16 + channels * width, :] = edge
    for i in range(parts):
        pieces[i].wait()
        values = block_ref[i * each : (i + 1) * each].astype(F32).reshape(each * width, rows)
        rows_ref[8 + i * each * width : 8 + (i + 1) * each * width, :] = values
    own = width // (len(routes) + 1)
    me = lax.axis_index("wide")
    for window, target in zip(windows, [me] + [entry(route, me) for route in routes]):
        first = target * own + 7
        columns = [rows_ref[pl.ds(first + i, channels, stride=width), :] for i in range(own + 2)]
        window[...] = jnp.concatenate(columns, axis=0).astype(BF16)


def prepare_kernel(
    wide,
    own_out,
    groups,
    aw_ref,
    ab_ref,
    cw_ref,
    cb_ref,
    hw_ref,
    rw_ref,
    measured_ref,
    sparse_ref,
    *refs,
):
    firsts, (a2_ref, b1_ref, b2_ref, h_ref, turned_ref, select_ref, target_ref) = refs[:-7], refs[-7:]
    channels = aw_ref.shape[1]
    span = 2 * own_out + 2
    size, outs = span * channels, own_out * channels
    rows, columns = split(iota((size, channels), 0), channels)
    pick = (columns == iota((size, channels), 1)).astype(F32)
    pick16 = pick.astype(BF16)
    out_channel, _ = split(iota((outs, channels), 0), own_out)
    pick_out = (out_channel == iota((outs, channels), 1)).astype(F32)
    pick_out16 = pick_out.astype(BF16)

    def spread(left, weight, right):
        half = lax.dot_general(left, weight, (((1,), (1,)), ((), ())), preferred_element_type=F32)
        return lax.dot_general(half.astype(BF16), right, (((1,), (1,)), ((), ())), preferred_element_type=F32)

    for first_ref in firsts:
        many = first_ref.shape[0] // 2
        taken = many // channels
        which, channel = split(iota((2 * many, channels), 0), channels)
        is_channel = channel == iota((2 * many, channels), 1)
        sides = [is_channel & (which >= side * taken) & (which < (side + 1) * taken) for side in range(2)]
        sides = [side.astype(F32).astype(BF16) for side in sides]
        row_column = split(iota((many, 2 * many), 0), channels)[0]
        column_column = split(iota((many, 2 * many), 1), channels)[0]
        same = (row_column == column_column) | (row_column + taken == column_column)
        for e in range(2):
            full = spread(pick16[:many], aw_ref[e], sides[0]) + spread(pick16[:many], aw_ref[e + 2], sides[1])
            first_ref[e * many : (e + 1) * many, :] = jnp.where(same, full, 0.0).astype(BF16)

    in_column = split(iota((outs, size), 1), channels)[0]
    out_column = split(iota((outs, size), 0), own_out)[1]
    me = lax.axis_index("wide")
    absolute = in_column + me * (2 * own_out) - 1
    inside = (absolute >= 0) & (absolute < 2 * own_out * wide)
    total = jnp.zeros((outs, size), F32)
    for tap in range(TAPS):
        here = (in_column == 2 * out_column + tap) & inside
        total = jnp.where(here, spread(pick_out16, cw_ref[tap], pick16), total)
    a2_ref[...] = total.astype(BF16)

    def along(left, vector_ref, out_ref):
        summed = jnp.sum(left * vector_ref[...].astype(F32), axis=1, keepdims=True)
        out_ref[...] = jnp.broadcast_to(summed, out_ref.shape)

    along(pick, ab_ref, b1_ref)
    along(pick_out, cb_ref, b2_ref)
    along(pick_out, hw_ref, h_ref)

    turned = rw_ref[...].T
    high = turned.astype(BF16)
    turned_ref[:, : high.shape[1]] = high
    turned_ref[:, high.shape[1] :] = (turned - high.astype(F32)).astype(BF16)

    sparse_count = measured_ref.shape[0]
    wanted = (select_ref.shape[0], sparse_count)
    pick_view = (split(iota(wanted, 0), own_out)[0] == iota(wanted, 1)).astype(F32)
    along(pick_view, sparse_ref, select_ref)
    for k in range(sparse_count):
        target_ref[k * own_out : (k + 1) * own_out, :] = measured_ref[k]


def net_kernel(routes, own_out, groups, *refs):
    wide = len(routes) + 1
    windows, firsts, refs = refs[:wide], refs[wide : wide + len(groups)], refs[wide + len(groups) :]
    a2_ref, b1_ref, b2_ref, h_ref, select_ref, target_ref, predicted_ref, residual_ref, views_ref = refs
    size, lanes = windows[0].shape
    outs = a2_ref.shape[0]
    channels = outs // own_out
    me = lax.axis_index("wide")
    sources = [me] + [entry(tuple(route.index(i) for i in range(wide)), me) for route in routes]
    for window, source in zip(windows, sources):
        views_ref[:, pl.ds(pl.multiple_of((source + 1) * lanes, lanes), lanes)] = window[...]
    views_ref[:, :lanes] = views_ref[:, wide * lanes :]

    many = 2 if wide % 2 == 0 else 1
    wider = lambda ref, times: jnp.concatenate([ref[...]] * times, axis=1)
    b1 = wider(b1_ref, many)
    b2, h = wider(b2_ref, 2 * many), wider(h_ref, 2 * many)
    select = select_ref[...]
    picked = jnp.zeros(select.shape, F32)
    for view in range(0, wide, many):
        previous = slice(view * lanes, (view + many) * lanes)
        current = slice((view + 1) * lanes, (view + 1 + many) * lanes)
        pieces = ([], [])
        for (first, taken), first_ref in zip(groups, firsts):
            rows = slice(first * channels, (first + taken) * channels)
            half = taken * channels
            stacked = jnp.concatenate([views_ref[rows, current], views_ref[rows, previous]], axis=0)
            summed = jnp.dot(first_ref[...], stacked, preferred_element_type=F32)
            for e in range(2):
                pieces[e].append(leaky_relu(summed[e * half : (e + 1) * half] + b1[rows]).astype(BF16))
        both = jnp.concatenate([jnp.concatenate(piece, axis=0) for piece in pieces], axis=1)
        hidden = leaky_relu(jnp.dot(a2_ref[...], both, preferred_element_type=F32) + b2) * h
        value = jnp.sum(hidden.reshape(outs // 8, 8, hidden.shape[1]), axis=0)
        apart = own_out
        while apart < 8:
            value += pltpu.roll(value, apart, 0)
            apart *= 2
        for e in range(2):
            for i in range(many):
                out_view = 2 * (view + i) + e
                at = (e * many + i) * lanes
                tile = value[:, at : at + lanes]
                predicted_ref[out_view] = tile[:own_out]
                repeated = jnp.concatenate([tile] * (select.shape[0] // 8), axis=0)
                picked = jnp.where(select == out_view, repeated, picked)
    residual_ref[...] = (picked - target_ref[...]).astype(BF16)


def adjoint_kernel(shifts, own_out, *refs):
    residuals, refs = refs[: len(shifts)], refs[len(shifts) :]
    turned_ref, predicted_ref, out_ref, copied_ref = refs
    copied_ref[...] = predicted_ref[...]
    lanes = residuals[0].shape[1]
    weights = []
    for narrow_shift, pair_shift in shifts:
        narrow, pair = came_from("narrow", narrow_shift), came_from("pair", pair_shift)
        block = narrow * lax.axis_size("pair") + pair
        weights.append(turned_ref[pl.ds(pl.multiple_of(block * lanes, lanes), lanes), :])
    values = jnp.concatenate([ref[...] for ref in residuals], axis=1)
    both = jnp.dot(values, jnp.concatenate(weights, axis=0), preferred_element_type=F32)
    total = both[:, :lanes] + both[:, lanes:]
    for k in range(out_ref.shape[0]):
        out_ref[k] = total[k * own_out : (k + 1) * own_out]


def came_from(axis, distance):
    count = lax.axis_size(axis)
    return lax.rem(lax.axis_index(axis) - distance + count, count)


def send_both(block, narrow_distance, pair_distance):
    narrow, pair = lax.axis_size("narrow"), lax.axis_size("pair")
    route = []
    for i in range(narrow):
        for j in range(pair):
            target = (i + narrow_distance) % narrow * pair + (j + pair_distance) % pair
            route.append((i * pair + j, target))
    return lax.ppermute(block, ("narrow", "pair"), route)


def local(
    low_sino,
    angle_weight,
    angle_bias,
    column_weight,
    column_bias,
    head_weight,
    sparse_views,
    measured,
    row_weights,
):
    wide, narrow, pair = (lax.axis_size(axis) for axis in ("wide", "narrow", "pair"))
    _, channels, width, lanes = low_sino.shape
    own_out = width // wide // 2
    span = 2 * own_out + 2
    size, outs = span * channels, own_out * channels
    sparse_count = measured.shape[0]
    rows = row_weights.shape[1]
    flat = (sparse_count * own_out, lanes)
    shape = jax.ShapeDtypeStruct
    big = 16 if width <= 64 else 48

    small = (
        angle_weight,
        angle_bias[None],
        column_weight,
        column_bias[None],
        head_weight[None],
        row_weights,
        measured,
        sparse_views,
    )
    routes = rounds(wide)
    groups = column_groups(channels, span)
    windows = call(
        functools.partial(pack_kernel, routes),
        [shape((size, lanes), BF16)] * wide,
        [pl.BlockSpec(memory_space=pltpu.HBM)],
        [
            pltpu.VMEM((channels, width, lanes), BF16),
            pltpu.VMEM((16 + channels * width, lanes), F32),
            pltpu.SemaphoreType.DMA((4,)),
        ],
        vmem=53.6 if width <= 64 else 48,
    )(low_sino)
    windows = [windows[0]] + [
        lax.ppermute(window, "wide", list(enumerate(route))) for window, route in zip(windows[1:], routes)
    ]

    widths = sorted({taken for _, taken in groups})
    *firsts, a2, b1, b2, head, turned, select, target = call(
        functools.partial(prepare_kernel, wide, own_out, groups),
        [shape((2 * taken * channels, 2 * taken * channels), BF16) for taken in widths]
        + [
            shape((outs, size), BF16),
            shape((size, lanes), F32),
            shape((outs, lanes), F32),
            shape((outs, lanes), F32),
            shape((rows, 2 * lanes), BF16),
            shape(flat, F32),
            shape(flat, F32),
        ],
        [VMEM] * 8,
        vmem=big,
    )(*small)
    firsts = [firsts[widths.index(taken)] for _, taken in groups]

    predicted, residual = call(
        functools.partial(net_kernel, routes, own_out, groups),
        [shape((2 * wide, own_out, lanes), F32), shape(flat, BF16)],
        [VMEM] * (wide + len(groups) + 6),
        [pltpu.VMEM((size, (wide + 1) * lanes), BF16)],
        vmem=big,
    )(*windows, *firsts, a2, b1, b2, head, select, target)

    shifts = [(0, t) for t in range(1, pair)] + [(s, 0) for s in range(1, narrow)]
    shifts += [(s, t) for s in range(1, narrow) for t in range(1, pair)]
    blocks = [residual] + [send_both(residual, s, t) for s, t in shifts]
    shifts.insert(0, (0, 0))
    adjoint, predicted = call(
        functools.partial(adjoint_kernel, shifts, own_out),
        [shape((sparse_count, own_out, lanes), F32), shape(predicted.shape, F32)],
        [VMEM] * (len(blocks) + 2),
        vmem=big,
    )(*blocks, turned, predicted)
    return (predicted, adjoint)


def solution(mesh):
    in_specs = (
        P(("parts", "wide"), None, None, ("narrow", "pair")),
        P(),
        P(),
        P(),
        P(),
        P(),
        P(("parts", "narrow"), None),
        P("parts", "wide", ("narrow", "pair")),
        P(("narrow", "pair"), None),
    )
    out_specs = (P("parts", "wide", ("narrow", "pair")), P("parts", "wide", ("narrow", "pair")))
    return jax.shard_map(local, mesh=mesh, in_specs=in_specs, out_specs=out_specs, check_vma=False)
```

```python
import functools

import jax
import jax.numpy as jnp
from jax import lax
from jax.experimental import pallas as pl
from jax.experimental.pallas import tpu as pltpu
from jax.sharding import PartitionSpec as P

F32, BF16 = jnp.float32, jnp.bfloat16
VMEM = pl.BlockSpec(memory_space=pltpu.VMEM)
TAPS = 4


def call(kernel, outs, in_specs, scratch=(), vmem=16, flops=10**6):
    nbytes = sum(o.size * o.dtype.itemsize for o in jax.tree.leaves(outs))
    return pl.pallas_call(
        kernel,
        out_shape=outs,
        in_specs=in_specs,
        out_specs=jax.tree.map(lambda _: VMEM, outs),
        scratch_shapes=list(scratch),
        compiler_params=pltpu.CompilerParams(vmem_limit_bytes=int(vmem * 2**20)),
        cost_estimate=pl.CostEstimate(flops=flops, bytes_accessed=nbytes, transcendentals=0),
    )


def leaky_relu(values):
    return jnp.maximum(values, 0.1 * values)


def split(index, size):
    whole = ((index.astype(F32) + 0.5) * (1.0 / size)).astype(jnp.int32)
    return whole, index - whole * size


def iota(shape, axis):
    return lax.broadcasted_iota(jnp.int32, shape, axis)


def rounds(count):
    return [tuple((i + shift) % count for i in range(count)) for shift in range(1, count)]


def entry(table, index):
    value = jnp.int32(table[0])
    for i in range(1, len(table)):
        value = jnp.where(index == i, jnp.int32(table[i]), value)
    return value


def column_groups(channels, span):
    most = max(1, 256 // (2 * channels) // 2 * 2)
    return [(first, min(most, span - first)) for first in range(0, span, most)]


def pack_kernel(routes, low_ref, *refs):
    windows, (block_ref, rows_ref, sems) = refs[: len(routes) + 1], refs[len(routes) + 1 :]
    _, channels, width, rows = low_ref.shape
    parts = sems.shape[0]
    each = channels // parts
    pieces = []
    for i in range(parts):
        piece = pl.ds(i * each, each)
        pieces.append(pltpu.make_async_copy(low_ref.at[0, piece], block_ref.at[piece], sems.at[i]))
        pieces[-1].start()
    edge = jnp.zeros((8, rows), F32)
    rows_ref[0:8, :] = edge
    rows_ref[8 + channels * width : 16 + channels * width, :] = edge
    for i in range(parts):
        pieces[i].wait()
        values = block_ref[i * each : (i + 1) * each].astype(F32).reshape(each * width, rows)
        rows_ref[8 + i * each * width : 8 + (i + 1) * each * width, :] = values
    own = width // (len(routes) + 1)
    me = lax.axis_index("wide")
    for window, target in zip(windows, [me] + [entry(route, me) for route in routes]):
        first = target * own + 7
        columns = [rows_ref[pl.ds(first + i, channels, stride=width), :] for i in range(own + 2)]
        window[...] = jnp.concatenate(columns, axis=0).astype(BF16)


def prepare_kernel(
    wide,
    own_out,
    groups,
    aw_ref,
    ab_ref,
    cw_ref,
    cb_ref,
    hw_ref,
    rw_ref,
    measured_ref,
    sparse_ref,
    *refs,
):
    firsts, (a2_ref, b1_ref, b2_ref, h_ref, turned_ref, select_ref, target_ref) = refs[:-7], refs[-7:]
    channels = aw_ref.shape[1]
    span = 2 * own_out + 2
    size, outs = span * channels, own_out * channels
    rows, columns = split(iota((size, channels), 0), channels)
    pick = (columns == iota((size, channels), 1)).astype(F32)
    pick16 = pick.astype(BF16)
    out_channel, _ = split(iota((outs, channels), 0), own_out)
    pick_out = (out_channel == iota((outs, channels), 1)).astype(F32)
    pick_out16 = pick_out.astype(BF16)

    def spread(left, weight, right):
        half = lax.dot_general(left, weight, (((1,), (1,)), ((), ())), preferred_element_type=F32)
        return lax.dot_general(half.astype(BF16), right, (((1,), (1,)), ((), ())), preferred_element_type=F32)

    for first_ref in firsts:
        many = first_ref.shape[0] // 2
        taken = many // channels
        which, channel = split(iota((2 * many, channels), 0), channels)
        is_channel = channel == iota((2 * many, channels), 1)
        sides = [is_channel & (which >= side * taken) & (which < (side + 1) * taken) for side in range(2)]
        sides = [side.astype(F32).astype(BF16) for side in sides]
        row_column = split(iota((many, 2 * many), 0), channels)[0]
        column_column = split(iota((many, 2 * many), 1), channels)[0]
        same = (row_column == column_column) | (row_column + taken == column_column)
        for e in range(2):
            full = spread(pick16[:many], aw_ref[e], sides[0]) + spread(pick16[:many], aw_ref[e + 2], sides[1])
            first_ref[e * many : (e + 1) * many, :] = jnp.where(same, full, 0.0).astype(BF16)

    in_column = split(iota((outs, size), 1), channels)[0]
    out_column = split(iota((outs, size), 0), own_out)[1]
    me = lax.axis_index("wide")
    absolute = in_column + me * (2 * own_out) - 1
    inside = (absolute >= 0) & (absolute < 2 * own_out * wide)
    total = jnp.zeros((outs, size), F32)
    for tap in range(TAPS):
        here = (in_column == 2 * out_column + tap) & inside
        total = jnp.where(here, spread(pick_out16, cw_ref[tap], pick16), total)
    a2_ref[...] = total.astype(BF16)

    def along(left, vector_ref, out_ref):
        summed = jnp.sum(left * vector_ref[...].astype(F32), axis=1, keepdims=True)
        out_ref[...] = jnp.broadcast_to(summed, out_ref.shape)

    along(pick, ab_ref, b1_ref)
    along(pick_out, cb_ref, b2_ref)
    along(pick_out, hw_ref, h_ref)

    turned = rw_ref[...].T
    high = turned.astype(BF16)
    turned_ref[:, : high.shape[1]] = high
    turned_ref[:, high.shape[1] :] = (turned - high.astype(F32)).astype(BF16)

    sparse_count = measured_ref.shape[0]
    wanted = (select_ref.shape[0], sparse_count)
    pick_view = (split(iota(wanted, 0), own_out)[0] == iota(wanted, 1)).astype(F32)
    along(pick_view, sparse_ref, select_ref)
    for k in range(sparse_count):
        target_ref[k * own_out : (k + 1) * own_out, :] = measured_ref[k]


def net_kernel(routes, own_out, groups, *refs):
    wide = len(routes) + 1
    windows, firsts, refs = refs[:wide], refs[wide : wide + len(groups)], refs[wide + len(groups) :]
    a2_ref, b1_ref, b2_ref, h_ref, select_ref, target_ref, predicted_ref, residual_ref, views_ref = refs
    size, lanes = windows[0].shape
    outs = a2_ref.shape[0]
    channels = outs // own_out
    me = lax.axis_index("wide")
    sources = [me] + [entry(tuple(route.index(i) for i in range(wide)), me) for route in routes]
    for window, source in zip(windows, sources):
        views_ref[:, pl.ds(pl.multiple_of((source + 1) * lanes, lanes), lanes)] = window[...]
    views_ref[:, :lanes] = views_ref[:, wide * lanes :]

    many = 2 if wide % 2 == 0 else 1
    wider = lambda ref, times: jnp.concatenate([ref[...]] * times, axis=1)
    b1 = wider(b1_ref, many)
    b2, h = wider(b2_ref, 2 * many), wider(h_ref, 2 * many)
    select = select_ref[...]
    picked = jnp.zeros(select.shape, F32)
    for view in range(0, wide, many):
        previous = slice(view * lanes, (view + many) * lanes)
        current = slice((view + 1) * lanes, (view + 1 + many) * lanes)
        pieces = ([], [])
        for (first, taken), first_ref in zip(groups, firsts):
            rows = slice(first * channels, (first + taken) * channels)
            half = taken * channels
            stacked = jnp.concatenate([views_ref[rows, current], views_ref[rows, previous]], axis=0)
            summed = jnp.dot(first_ref[...], stacked, preferred_element_type=F32)
            for e in range(2):
                pieces[e].append(leaky_relu(summed[e * half : (e + 1) * half] + b1[rows]).astype(BF16))
        both = jnp.concatenate([jnp.concatenate(piece, axis=0) for piece in pieces], axis=1)
        hidden = leaky_relu(jnp.dot(a2_ref[...], both, preferred_element_type=F32) + b2) * h
        value = jnp.sum(hidden.reshape(outs // 8, 8, hidden.shape[1]), axis=0)
        apart = own_out
        while apart < 8:
            value += pltpu.roll(value, apart, 0)
            apart *= 2
        for e in range(2):
            for i in range(many):
                out_view = 2 * (view + i) + e
                at = (e * many + i) * lanes
                tile = value[:, at : at + lanes]
                predicted_ref[out_view] = tile[:own_out]
                repeated = jnp.concatenate([tile] * (select.shape[0] // 8), axis=0)
                picked = jnp.where(select == out_view, repeated, picked)
    residual_ref[...] = (picked - target_ref[...]).astype(BF16)


def adjoint_sum(residuals, shifts, turned_ref):
    lanes = residuals[0].shape[1]
    weights = []
    for narrow_shift, pair_shift in shifts:
        narrow, pair = came_from("narrow", narrow_shift), came_from("pair", pair_shift)
        block = narrow * lax.axis_size("pair") + pair
        weights.append(turned_ref[pl.ds(pl.multiple_of(block * lanes, lanes), lanes), :])
    values = jnp.concatenate([ref[...] for ref in residuals], axis=1)
    both = jnp.dot(values, jnp.concatenate(weights, axis=0), preferred_element_type=F32)
    return both[:, :lanes] + both[:, lanes:]


def near_kernel(shifts, *refs):
    residuals, (turned_ref, predicted_ref, partial_ref, copied_ref) = refs[: len(shifts)], refs[len(shifts) :]
    copied_ref[...] = predicted_ref[...]
    partial_ref[...] = adjoint_sum(residuals, shifts, turned_ref)


def far_kernel(shifts, own_out, *refs):
    residuals, (turned_ref, partial_ref, out_ref) = refs[: len(shifts)], refs[len(shifts) :]
    total = partial_ref[...] + adjoint_sum(residuals, shifts, turned_ref)
    for k in range(out_ref.shape[0]):
        out_ref[k] = total[k * own_out : (k + 1) * own_out]


def came_from(axis, distance):
    count = lax.axis_size(axis)
    return lax.rem(lax.axis_index(axis) - distance + count, count)


def send_both(block, narrow_distance, pair_distance):
    narrow, pair = lax.axis_size("narrow"), lax.axis_size("pair")
    route = []
    for i in range(narrow):
        for j in range(pair):
            target = (i + narrow_distance) % narrow * pair + (j + pair_distance) % pair
            route.append((i * pair + j, target))
    return lax.ppermute(block, ("narrow", "pair"), route)


def local(
    low_sino,
    angle_weight,
    angle_bias,
    column_weight,
    column_bias,
    head_weight,
    sparse_views,
    measured,
    row_weights,
):
    wide, narrow, pair = (lax.axis_size(axis) for axis in ("wide", "narrow", "pair"))
    _, channels, width, lanes = low_sino.shape
    own_out = width // wide // 2
    span = 2 * own_out + 2
    size, outs = span * channels, own_out * channels
    sparse_count = measured.shape[0]
    rows = row_weights.shape[1]
    flat = (sparse_count * own_out, lanes)
    shape = jax.ShapeDtypeStruct
    big = 16 if width <= 64 else 48

    small = (
        angle_weight,
        angle_bias[None],
        column_weight,
        column_bias[None],
        head_weight[None],
        row_weights,
        measured,
        sparse_views,
    )
    routes = rounds(wide)
    groups = column_groups(channels, span)
    windows = call(
        functools.partial(pack_kernel, routes),
        [shape((size, lanes), BF16)] * wide,
        [pl.BlockSpec(memory_space=pltpu.HBM)],
        [
            pltpu.VMEM((channels, width, lanes), BF16),
            pltpu.VMEM((16 + channels * width, lanes), F32),
            pltpu.SemaphoreType.DMA((4,)),
        ],
        vmem=53.6 if width <= 64 else 48,
    )(low_sino)
    windows = [windows[0]] + [
        lax.ppermute(window, "wide", list(enumerate(route))) for window, route in zip(windows[1:], routes)
    ]

    widths = sorted({taken for _, taken in groups})
    *firsts, a2, b1, b2, head, turned, select, target = call(
        functools.partial(prepare_kernel, wide, own_out, groups),
        [shape((2 * taken * channels, 2 * taken * channels), BF16) for taken in widths]
        + [
            shape((outs, size), BF16),
            shape((size, lanes), F32),
            shape((outs, lanes), F32),
            shape((outs, lanes), F32),
            shape((rows, 2 * lanes), BF16),
            shape(flat, F32),
            shape(flat, F32),
        ],
        [VMEM] * 8,
        vmem=big,
    )(*small)
    firsts = [firsts[widths.index(taken)] for _, taken in groups]

    predicted, residual = call(
        functools.partial(net_kernel, routes, own_out, groups),
        [shape((2 * wide, own_out, lanes), F32), shape(flat, BF16)],
        [VMEM] * (wide + len(groups) + 6),
        [pltpu.VMEM((size, (wide + 1) * lanes), BF16)],
        vmem=big,
    )(*windows, *firsts, a2, b1, b2, head, select, target)

    near_shifts = [(s, t) for s in range(1, narrow) for t in range(1, pair)]
    far_shifts = [(0, t) for t in range(1, pair)] + [(s, 0) for s in range(1, narrow)]
    near = [residual] + [send_both(residual, s, t) for s, t in near_shifts]
    far = [send_both(residual, s, t) for s, t in far_shifts]
    partial, predicted = call(
        functools.partial(near_kernel, [(0, 0)] + near_shifts),
        [shape(flat, F32), shape(predicted.shape, F32)],
        [VMEM] * (len(near) + 2),
        vmem=big,
    )(*near, turned, predicted)
    adjoint = call(
        functools.partial(far_kernel, far_shifts, own_out),
        shape((sparse_count, own_out, lanes), F32),
        [VMEM] * (len(far) + 2),
        vmem=big,
    )(*far, turned, partial)
    return (predicted, adjoint)


def solution(mesh):
    in_specs = (
        P(("parts", "wide"), None, None, ("narrow", "pair")),
        P(),
        P(),
        P(),
        P(),
        P(),
        P(("parts", "narrow"), None),
        P("parts", "wide", ("narrow", "pair")),
        P(("narrow", "pair"), None),
    )
    out_specs = (P("parts", "wide", ("narrow", "pair")), P("parts", "wide", ("narrow", "pair")))
    return jax.shard_map(local, mesh=mesh, in_specs=in_specs, out_specs=out_specs, check_vma=False)
```

```python
import functools

import jax
import jax.numpy as jnp
from jax import lax
from jax.experimental import pallas as pl
from jax.experimental.pallas import tpu as pltpu
from jax.sharding import PartitionSpec as P

F32, BF16 = jnp.float32, jnp.bfloat16
VMEM = pl.BlockSpec(memory_space=pltpu.VMEM)
TAPS = 4


def call(kernel, outs, in_specs, scratch=(), vmem=16, flops=10**6):
    nbytes = sum(o.size * o.dtype.itemsize for o in jax.tree.leaves(outs))
    return pl.pallas_call(
        kernel,
        out_shape=outs,
        in_specs=in_specs,
        out_specs=jax.tree.map(lambda _: VMEM, outs),
        scratch_shapes=list(scratch),
        compiler_params=pltpu.CompilerParams(vmem_limit_bytes=int(vmem * 2**20)),
        cost_estimate=pl.CostEstimate(flops=flops, bytes_accessed=nbytes, transcendentals=0),
    )


def leaky_relu(values):
    return jnp.maximum(values, 0.1 * values)


def split(index, size):
    whole = ((index.astype(F32) + 0.5) * (1.0 / size)).astype(jnp.int32)
    return whole, index - whole * size


def iota(shape, axis):
    return lax.broadcasted_iota(jnp.int32, shape, axis)


def rounds(count, cores):
    if count == 4:
        schedules = [
            [(1, 3, 0, 2), (3, 2, 1, 0), (2, 0, 3, 1)],
            [(2, 3, 1, 0), (3, 2, 0, 1), (1, 0, 3, 2)],
        ]
    else:
        schedules = [[tuple((i + shift) % count for i in range(count)) for shift in range(1, count)]]
    return [
        tuple(schedules[core % len(schedules)][r][i] for i in range(count) for core in range(cores))
        for r in range(count - 1)
    ]


def sources(route, cores):
    back = [0] * len(route)
    for place, target in enumerate(route):
        back[target * cores + place % cores] = place // cores
    return tuple(back)


def entry(table, axes):
    index = lax.axis_index(axes)
    value = jnp.int32(table[0])
    for i in range(1, len(table)):
        value = jnp.where(index == i, jnp.int32(table[i]), value)
    return value


def column_groups(channels, span):
    most = max(1, 256 // (2 * channels) // 2 * 2)
    return [(first, min(most, span - first)) for first in range(0, span, most)]


def pack_kernel(routes, low_ref, *refs):
    windows, (block_ref, rows_ref, sems) = refs[: len(routes) + 1], refs[len(routes) + 1 :]
    _, channels, width, rows = low_ref.shape
    parts = sems.shape[0]
    each = channels // parts
    pieces = []
    for i in range(parts):
        piece = pl.ds(i * each, each)
        pieces.append(pltpu.make_async_copy(low_ref.at[0, piece], block_ref.at[piece], sems.at[i]))
        pieces[-1].start()
    edge = jnp.zeros((8, rows), F32)
    rows_ref[0:8, :] = edge
    rows_ref[8 + channels * width : 16 + channels * width, :] = edge
    for i in range(parts):
        pieces[i].wait()
        values = block_ref[i * each : (i + 1) * each].astype(F32).reshape(each * width, rows)
        rows_ref[8 + i * each * width : 8 + (i + 1) * each * width, :] = values
    own = width // (len(routes) + 1)
    me = lax.axis_index("wide")
    for window, target in zip(windows, [me] + [entry(route, ("wide", "pair")) for route in routes]):
        first = target * own + 7
        columns = [rows_ref[pl.ds(first + i, channels, stride=width), :] for i in range(own + 2)]
        window[...] = jnp.concatenate(columns, axis=0).astype(BF16)


def prepare_kernel(
    wide,
    own_out,
    groups,
    aw_ref,
    ab_ref,
    cw_ref,
    cb_ref,
    hw_ref,
    rw_ref,
    measured_ref,
    sparse_ref,
    *refs,
):
    firsts, (a2_ref, b1_ref, b2_ref, h_ref, turned_ref, select_ref, target_ref) = refs[:-7], refs[-7:]
    channels = aw_ref.shape[1]
    span = 2 * own_out + 2
    size, outs = span * channels, own_out * channels
    rows, columns = split(iota((size, channels), 0), channels)
    pick = (columns == iota((size, channels), 1)).astype(F32)
    pick16 = pick.astype(BF16)
    out_channel, _ = split(iota((outs, channels), 0), own_out)
    pick_out = (out_channel == iota((outs, channels), 1)).astype(F32)
    pick_out16 = pick_out.astype(BF16)

    def spread(left, weight, right):
        half = lax.dot_general(left, weight, (((1,), (1,)), ((), ())), preferred_element_type=F32)
        return lax.dot_general(half.astype(BF16), right, (((1,), (1,)), ((), ())), preferred_element_type=F32)

    for first_ref in firsts:
        many = first_ref.shape[0] // 2
        taken = many // channels
        which, channel = split(iota((2 * many, channels), 0), channels)
        is_channel = channel == iota((2 * many, channels), 1)
        sides = [is_channel & (which >= side * taken) & (which < (side + 1) * taken) for side in range(2)]
        sides = [side.astype(F32).astype(BF16) for side in sides]
        row_column = split(iota((many, 2 * many), 0), channels)[0]
        column_column = split(iota((many, 2 * many), 1), channels)[0]
        same = (row_column == column_column) | (row_column + taken == column_column)
        for e in range(2):
            full = spread(pick16[:many], aw_ref[e], sides[0]) + spread(pick16[:many], aw_ref[e + 2], sides[1])
            first_ref[e * many : (e + 1) * many, :] = jnp.where(same, full, 0.0).astype(BF16)

    in_column = split(iota((outs, size), 1), channels)[0]
    out_column = split(iota((outs, size), 0), own_out)[1]
    me = lax.axis_index("wide")
    absolute = in_column + me * (2 * own_out) - 1
    inside = (absolute >= 0) & (absolute < 2 * own_out * wide)
    total = jnp.zeros((outs, size), F32)
    for tap in range(TAPS):
        here = (in_column == 2 * out_column + tap) & inside
        total = jnp.where(here, spread(pick_out16, cw_ref[tap], pick16), total)
    a2_ref[...] = total.astype(BF16)

    def along(left, vector_ref, out_ref):
        summed = jnp.sum(left * vector_ref[...].astype(F32), axis=1, keepdims=True)
        out_ref[...] = jnp.broadcast_to(summed, out_ref.shape)

    along(pick, ab_ref, b1_ref)
    along(pick_out, cb_ref, b2_ref)
    along(pick_out, hw_ref, h_ref)

    turned = rw_ref[...].T
    high = turned.astype(BF16)
    turned_ref[:, : high.shape[1]] = high
    turned_ref[:, high.shape[1] :] = (turned - high.astype(F32)).astype(BF16)

    sparse_count = measured_ref.shape[0]
    wanted = (select_ref.shape[0], sparse_count)
    pick_view = (split(iota(wanted, 0), own_out)[0] == iota(wanted, 1)).astype(F32)
    along(pick_view, sparse_ref, select_ref)
    for k in range(sparse_count):
        target_ref[k * own_out : (k + 1) * own_out, :] = measured_ref[k]


def net_kernel(routes, own_out, groups, *refs):
    wide = len(routes) + 1
    windows, firsts, refs = refs[:wide], refs[wide : wide + len(groups)], refs[wide + len(groups) :]
    a2_ref, b1_ref, b2_ref, h_ref, select_ref, target_ref, predicted_ref, residual_ref, views_ref = refs
    size, lanes = windows[0].shape
    outs = a2_ref.shape[0]
    channels = outs // own_out
    me = lax.axis_index("wide")
    cores = lax.axis_size("pair")
    origins = [me] + [entry(sources(route, cores), ("wide", "pair")) for route in routes]
    for window, source in zip(windows, origins):
        views_ref[:, pl.ds(pl.multiple_of((source + 1) * lanes, lanes), lanes)] = window[...]
    views_ref[:, :lanes] = views_ref[:, wide * lanes :]

    many = 2 if wide % 2 == 0 else 1
    wider = lambda ref, times: jnp.concatenate([ref[...]] * times, axis=1)
    b1 = wider(b1_ref, many)
    b2, h = wider(b2_ref, 2 * many), wider(h_ref, 2 * many)
    select = select_ref[...]
    picked = jnp.zeros(select.shape, F32)
    for view in range(0, wide, many):
        previous = slice(view * lanes, (view + many) * lanes)
        current = slice((view + 1) * lanes, (view + 1 + many) * lanes)
        pieces = ([], [])
        for (first, taken), first_ref in zip(groups, firsts):
            rows = slice(first * channels, (first + taken) * channels)
            half = taken * channels
            stacked = jnp.concatenate([views_ref[rows, current], views_ref[rows, previous]], axis=0)
            summed = jnp.dot(first_ref[...], stacked, preferred_element_type=F32)
            for e in range(2):
                pieces[e].append(leaky_relu(summed[e * half : (e + 1) * half] + b1[rows]).astype(BF16))
        both = jnp.concatenate([jnp.concatenate(piece, axis=0) for piece in pieces], axis=1)
        hidden = leaky_relu(jnp.dot(a2_ref[...], both, preferred_element_type=F32) + b2) * h
        value = jnp.sum(hidden.reshape(outs // 8, 8, hidden.shape[1]), axis=0)
        apart = own_out
        while apart < 8:
            value += pltpu.roll(value, apart, 0)
            apart *= 2
        for e in range(2):
            for i in range(many):
                out_view = 2 * (view + i) + e
                at = (e * many + i) * lanes
                tile = value[:, at : at + lanes]
                predicted_ref[out_view] = tile[:own_out]
                repeated = jnp.concatenate([tile] * (select.shape[0] // 8), axis=0)
                picked = jnp.where(select == out_view, repeated, picked)
    residual_ref[...] = (picked - target_ref[...]).astype(BF16)


def adjoint_kernel(shifts, own_out, *refs):
    residuals, refs = refs[: len(shifts)], refs[len(shifts) :]
    turned_ref, predicted_ref, out_ref, copied_ref = refs
    copied_ref[...] = predicted_ref[...]
    lanes = residuals[0].shape[1]
    weights = []
    for narrow_shift, pair_shift in shifts:
        narrow, pair = came_from("narrow", narrow_shift), came_from("pair", pair_shift)
        block = narrow * lax.axis_size("pair") + pair
        weights.append(turned_ref[pl.ds(pl.multiple_of(block * lanes, lanes), lanes), :])
    values = jnp.concatenate([ref[...] for ref in residuals], axis=1)
    both = jnp.dot(values, jnp.concatenate(weights, axis=0), preferred_element_type=F32)
    total = both[:, :lanes] + both[:, lanes:]
    for k in range(out_ref.shape[0]):
        out_ref[k] = total[k * own_out : (k + 1) * own_out]


def came_from(axis, distance):
    count = lax.axis_size(axis)
    return lax.rem(lax.axis_index(axis) - distance + count, count)


def send_both(block, narrow_distance, pair_distance):
    narrow, pair = lax.axis_size("narrow"), lax.axis_size("pair")
    route = []
    for i in range(narrow):
        for j in range(pair):
            target = (i + narrow_distance) % narrow * pair + (j + pair_distance) % pair
            route.append((i * pair + j, target))
    return lax.ppermute(block, ("narrow", "pair"), route)


def local(
    low_sino,
    angle_weight,
    angle_bias,
    column_weight,
    column_bias,
    head_weight,
    sparse_views,
    measured,
    row_weights,
):
    wide, narrow, pair = (lax.axis_size(axis) for axis in ("wide", "narrow", "pair"))
    _, channels, width, lanes = low_sino.shape
    own_out = width // wide // 2
    span = 2 * own_out + 2
    size, outs = span * channels, own_out * channels
    sparse_count = measured.shape[0]
    rows = row_weights.shape[1]
    flat = (sparse_count * own_out, lanes)
    shape = jax.ShapeDtypeStruct
    big = 16 if width <= 64 else 48

    small = (
        angle_weight,
        angle_bias[None],
        column_weight,
        column_bias[None],
        head_weight[None],
        row_weights,
        measured,
        sparse_views,
    )
    routes = rounds(wide, pair)
    groups = column_groups(channels, span)
    windows = call(
        functools.partial(pack_kernel, routes),
        [shape((size, lanes), BF16)] * wide,
        [pl.BlockSpec(memory_space=pltpu.HBM)],
        [
            pltpu.VMEM((channels, width, lanes), BF16),
            pltpu.VMEM((16 + channels * width, lanes), F32),
            pltpu.SemaphoreType.DMA((4,)),
        ],
        vmem=53.6 if width <= 64 else 48,
    )(low_sino)
    windows = [windows[0]] + [
        lax.ppermute(window, ("wide", "pair"), [(p, t * pair + p % pair) for p, t in enumerate(route)])
        for window, route in zip(windows[1:], routes)
    ]

    widths = sorted({taken for _, taken in groups})
    *firsts, a2, b1, b2, head, turned, select, target = call(
        functools.partial(prepare_kernel, wide, own_out, groups),
        [shape((2 * taken * channels, 2 * taken * channels), BF16) for taken in widths]
        + [
            shape((outs, size), BF16),
            shape((size, lanes), F32),
            shape((outs, lanes), F32),
            shape((outs, lanes), F32),
            shape((rows, 2 * lanes), BF16),
            shape(flat, F32),
            shape(flat, F32),
        ],
        [VMEM] * 8,
        vmem=big,
    )(*small)
    firsts = [firsts[widths.index(taken)] for _, taken in groups]

    predicted, residual = call(
        functools.partial(net_kernel, routes, own_out, groups),
        [shape((2 * wide, own_out, lanes), F32), shape(flat, BF16)],
        [VMEM] * (wide + len(groups) + 6),
        [pltpu.VMEM((size, (wide + 1) * lanes), BF16)],
        vmem=big,
    )(*windows, *firsts, a2, b1, b2, head, select, target)

    shifts = [(0, t) for t in range(1, pair)] + [(s, 0) for s in range(1, narrow)]
    shifts += [(s, t) for s in range(1, narrow) for t in range(1, pair)]
    blocks = [residual] + [send_both(residual, s, t) for s, t in shifts]
    shifts.insert(0, (0, 0))
    adjoint, predicted = call(
        functools.partial(adjoint_kernel, shifts, own_out),
        [shape((sparse_count, own_out, lanes), F32), shape(predicted.shape, F32)],
        [VMEM] * (len(blocks) + 2),
        vmem=big,
    )(*blocks, turned, predicted)
    return (predicted, adjoint)


def solution(mesh):
    in_specs = (
        P(("parts", "wide"), None, None, ("narrow", "pair")),
        P(),
        P(),
        P(),
        P(),
        P(),
        P(("parts", "narrow"), None),
        P("parts", "wide", ("narrow", "pair")),
        P(("narrow", "pair"), None),
    )
    out_specs = (P("parts", "wide", ("narrow", "pair")), P("parts", "wide", ("narrow", "pair")))
    return jax.shard_map(local, mesh=mesh, in_specs=in_specs, out_specs=out_specs, check_vma=False)
```

```python
import functools

import jax
import jax.numpy as jnp
from jax import lax
from jax.experimental import pallas as pl
from jax.experimental.pallas import tpu as pltpu
from jax.sharding import PartitionSpec as P

F32, BF16 = jnp.float32, jnp.bfloat16
VMEM = pl.BlockSpec(memory_space=pltpu.VMEM)
TAPS = 4


def call(kernel, outs, in_specs, scratch=(), vmem=16, flops=10**6):
    nbytes = sum(o.size * o.dtype.itemsize for o in jax.tree.leaves(outs))
    return pl.pallas_call(
        kernel,
        out_shape=outs,
        in_specs=in_specs,
        out_specs=jax.tree.map(lambda _: VMEM, outs),
        scratch_shapes=list(scratch),
        compiler_params=pltpu.CompilerParams(vmem_limit_bytes=int(vmem * 2**20)),
        cost_estimate=pl.CostEstimate(flops=flops, bytes_accessed=nbytes, transcendentals=0),
    )


def leaky_relu(values):
    return jnp.maximum(values, 0.1 * values)


def split(index, size):
    whole = ((index.astype(F32) + 0.5) * (1.0 / size)).astype(jnp.int32)
    return whole, index - whole * size


def iota(shape, axis):
    return lax.broadcasted_iota(jnp.int32, shape, axis)


def rounds(count, cores):
    if count == 4:
        schedules = [
            [(1, 2, 3, 0), (2, 3, 0, 1), (3, 0, 1, 2)],
            [(1, 3, 0, 2), (3, 2, 1, 0), (2, 0, 3, 1)],
        ]
    else:
        schedules = [[tuple((i + shift) % count for i in range(count)) for shift in range(1, count)]]
    return [
        tuple(schedules[core % len(schedules)][r][i] for i in range(count) for core in range(cores))
        for r in range(count - 1)
    ]


def sources(route, cores):
    back = [0] * len(route)
    for place, target in enumerate(route):
        back[target * cores + place % cores] = place // cores
    return tuple(back)


def entry(table, axes):
    index = lax.axis_index(axes)
    value = jnp.int32(table[0])
    for i in range(1, len(table)):
        value = jnp.where(index == i, jnp.int32(table[i]), value)
    return value


def column_groups(channels, span):
    most = max(1, 256 // (2 * channels) // 2 * 2)
    return [(first, min(most, span - first)) for first in range(0, span, most)]


def pack_kernel(routes, low_ref, *refs):
    windows, (block_ref, rows_ref, sems) = refs[: len(routes) + 1], refs[len(routes) + 1 :]
    _, channels, width, rows = low_ref.shape
    parts = sems.shape[0]
    each = channels // parts
    pieces = []
    for i in range(parts):
        piece = pl.ds(i * each, each)
        pieces.append(pltpu.make_async_copy(low_ref.at[0, piece], block_ref.at[piece], sems.at[i]))
        pieces[-1].start()
    edge = jnp.zeros((8, rows), F32)
    rows_ref[0:8, :] = edge
    rows_ref[8 + channels * width : 16 + channels * width, :] = edge
    for i in range(parts):
        pieces[i].wait()
        values = block_ref[i * each : (i + 1) * each].astype(F32).reshape(each * width, rows)
        rows_ref[8 + i * each * width : 8 + (i + 1) * each * width, :] = values
    own = width // (len(routes) + 1)
    me = lax.axis_index("wide")
    for window, target in zip(windows, [me] + [entry(route, ("wide", "pair")) for route in routes]):
        first = target * own + 7
        columns = [rows_ref[pl.ds(first + i, channels, stride=width), :] for i in range(own + 2)]
        window[...] = jnp.concatenate(columns, axis=0).astype(BF16)


def prepare_kernel(
    wide,
    own_out,
    groups,
    aw_ref,
    ab_ref,
    cw_ref,
    cb_ref,
    hw_ref,
    measured_ref,
    sparse_ref,
    *refs,
):
    firsts, (a2_ref, b1_ref, b2_ref, h_ref, select_ref, target_ref) = refs[:-6], refs[-6:]
    channels = aw_ref.shape[1]
    span = 2 * own_out + 2
    size, outs = span * channels, own_out * channels
    rows, columns = split(iota((size, channels), 0), channels)
    pick = (columns == iota((size, channels), 1)).astype(F32)
    pick16 = pick.astype(BF16)
    out_channel, _ = split(iota((outs, channels), 0), own_out)
    pick_out = (out_channel == iota((outs, channels), 1)).astype(F32)
    pick_out16 = pick_out.astype(BF16)

    def spread(left, weight, right):
        half = lax.dot_general(left, weight, (((1,), (1,)), ((), ())), preferred_element_type=F32)
        return lax.dot_general(half.astype(BF16), right, (((1,), (1,)), ((), ())), preferred_element_type=F32)

    for first_ref in firsts:
        many = first_ref.shape[0] // 2
        taken = many // channels
        which, channel = split(iota((2 * many, channels), 0), channels)
        is_channel = channel == iota((2 * many, channels), 1)
        sides = [is_channel & (which >= side * taken) & (which < (side + 1) * taken) for side in range(2)]
        sides = [side.astype(F32).astype(BF16) for side in sides]
        row_column = split(iota((many, 2 * many), 0), channels)[0]
        column_column = split(iota((many, 2 * many), 1), channels)[0]
        same = (row_column == column_column) | (row_column + taken == column_column)
        for e in range(2):
            full = spread(pick16[:many], aw_ref[e], sides[0]) + spread(pick16[:many], aw_ref[e + 2], sides[1])
            first_ref[e * many : (e + 1) * many, :] = jnp.where(same, full, 0.0).astype(BF16)

    in_column = split(iota((outs, size), 1), channels)[0]
    out_column = split(iota((outs, size), 0), own_out)[1]
    me = lax.axis_index("wide")
    absolute = in_column + me * (2 * own_out) - 1
    inside = (absolute >= 0) & (absolute < 2 * own_out * wide)
    total = jnp.zeros((outs, size), F32)
    for tap in range(TAPS):
        here = (in_column == 2 * out_column + tap) & inside
        total = jnp.where(here, spread(pick_out16, cw_ref[tap], pick16), total)
    a2_ref[...] = total.astype(BF16)

    def along(left, vector_ref, out_ref):
        summed = jnp.sum(left * vector_ref[...].astype(F32), axis=1, keepdims=True)
        out_ref[...] = jnp.broadcast_to(summed, out_ref.shape)

    along(pick, ab_ref, b1_ref)
    along(pick_out, cb_ref, b2_ref)
    along(pick_out, hw_ref, h_ref)

    sparse_count = measured_ref.shape[0]
    wanted = (select_ref.shape[0], sparse_count)
    pick_view = (split(iota(wanted, 0), own_out)[0] == iota(wanted, 1)).astype(F32)
    along(pick_view, sparse_ref, select_ref)
    for k in range(sparse_count):
        target_ref[k * own_out : (k + 1) * own_out, :] = measured_ref[k]


def turn_kernel(rw_ref, _, turned_ref):
    turned = rw_ref[...].T
    high = turned.astype(BF16)
    turned_ref[:, : high.shape[1]] = high
    turned_ref[:, high.shape[1] :] = (turned - high.astype(F32)).astype(BF16)


def net_kernel(routes, own_out, groups, *refs):
    wide = len(routes) + 1
    windows, firsts, refs = refs[:wide], refs[wide : wide + len(groups)], refs[wide + len(groups) :]
    a2_ref, b1_ref, b2_ref, h_ref, select_ref, target_ref, predicted_ref, residual_ref, views_ref = refs
    size, lanes = windows[0].shape
    outs = a2_ref.shape[0]
    channels = outs // own_out
    me = lax.axis_index("wide")
    cores = lax.axis_size("pair")
    origins = [me] + [entry(sources(route, cores), ("wide", "pair")) for route in routes]
    for window, source in zip(windows, origins):
        views_ref[:, pl.ds(pl.multiple_of((source + 1) * lanes, lanes), lanes)] = window[...]
    views_ref[:, :lanes] = views_ref[:, wide * lanes :]

    many = 2 if wide % 2 == 0 else 1
    wider = lambda ref, times: jnp.concatenate([ref[...]] * times, axis=1)
    b1 = wider(b1_ref, many)
    b2, h = wider(b2_ref, 2 * many), wider(h_ref, 2 * many)
    select = select_ref[...]
    picked = jnp.zeros(select.shape, F32)
    for view in range(0, wide, many):
        previous = slice(view * lanes, (view + many) * lanes)
        current = slice((view + 1) * lanes, (view + 1 + many) * lanes)
        pieces = ([], [])
        for (first, taken), first_ref in zip(groups, firsts):
            rows = slice(first * channels, (first + taken) * channels)
            half = taken * channels
            stacked = jnp.concatenate([views_ref[rows, current], views_ref[rows, previous]], axis=0)
            summed = jnp.dot(first_ref[...], stacked, preferred_element_type=F32)
            for e in range(2):
                pieces[e].append(leaky_relu(summed[e * half : (e + 1) * half] + b1[rows]).astype(BF16))
        both = jnp.concatenate([jnp.concatenate(piece, axis=0) for piece in pieces], axis=1)
        hidden = leaky_relu(jnp.dot(a2_ref[...], both, preferred_element_type=F32) + b2) * h
        value = jnp.sum(hidden.reshape(outs // 8, 8, hidden.shape[1]), axis=0)
        apart = own_out
        while apart < 8:
            value += pltpu.roll(value, apart, 0)
            apart *= 2
        for e in range(2):
            for i in range(many):
                out_view = 2 * (view + i) + e
                at = (e * many + i) * lanes
                tile = value[:, at : at + lanes]
                predicted_ref[out_view] = tile[:own_out]
                repeated = jnp.concatenate([tile] * (select.shape[0] // 8), axis=0)
                picked = jnp.where(select == out_view, repeated, picked)
    residual_ref[...] = (picked - target_ref[...]).astype(BF16)


def adjoint_kernel(shifts, own_out, *refs):
    residuals, refs = refs[: len(shifts)], refs[len(shifts) :]
    turned_ref, predicted_ref, out_ref, copied_ref = refs
    copied_ref[...] = predicted_ref[...]
    lanes = residuals[0].shape[1]
    weights = []
    for narrow_shift, pair_shift in shifts:
        narrow, pair = came_from("narrow", narrow_shift), came_from("pair", pair_shift)
        block = narrow * lax.axis_size("pair") + pair
        weights.append(turned_ref[pl.ds(pl.multiple_of(block * lanes, lanes), lanes), :])
    values = jnp.concatenate([ref[...] for ref in residuals], axis=1)
    both = jnp.dot(values, jnp.concatenate(weights, axis=0), preferred_element_type=F32)
    total = both[:, :lanes] + both[:, lanes:]
    for k in range(out_ref.shape[0]):
        out_ref[k] = total[k * own_out : (k + 1) * own_out]


def came_from(axis, distance):
    count = lax.axis_size(axis)
    return lax.rem(lax.axis_index(axis) - distance + count, count)


def send_both(block, narrow_distance, pair_distance):
    narrow, pair = lax.axis_size("narrow"), lax.axis_size("pair")
    route = []
    for i in range(narrow):
        for j in range(pair):
            target = (i + narrow_distance) % narrow * pair + (j + pair_distance) % pair
            route.append((i * pair + j, target))
    return lax.ppermute(block, ("narrow", "pair"), route)


def local(
    low_sino,
    angle_weight,
    angle_bias,
    column_weight,
    column_bias,
    head_weight,
    sparse_views,
    measured,
    row_weights,
):
    wide, narrow, pair = (lax.axis_size(axis) for axis in ("wide", "narrow", "pair"))
    _, channels, width, lanes = low_sino.shape
    own_out = width // wide // 2
    span = 2 * own_out + 2
    size, outs = span * channels, own_out * channels
    sparse_count = measured.shape[0]
    rows = row_weights.shape[1]
    flat = (sparse_count * own_out, lanes)
    shape = jax.ShapeDtypeStruct
    big = 16 if width <= 64 else 48

    small = (
        angle_weight,
        angle_bias[None],
        column_weight,
        column_bias[None],
        head_weight[None],
        measured,
        sparse_views,
    )
    routes = rounds(wide, pair)
    groups = column_groups(channels, span)
    windows = call(
        functools.partial(pack_kernel, routes),
        [shape((size, lanes), BF16)] * wide,
        [pl.BlockSpec(memory_space=pltpu.HBM)],
        [
            pltpu.VMEM((channels, width, lanes), BF16),
            pltpu.VMEM((16 + channels * width, lanes), F32),
            pltpu.SemaphoreType.DMA((4,)),
        ],
        vmem=53.6 if width <= 64 else 48,
    )(low_sino)
    windows = [windows[0]] + [
        lax.ppermute(window, ("wide", "pair"), [(p, t * pair + p % pair) for p, t in enumerate(route)])
        for window, route in zip(windows[1:], routes)
    ]

    widths = sorted({taken for _, taken in groups})
    *firsts, a2, b1, b2, head, select, target = call(
        functools.partial(prepare_kernel, wide, own_out, groups),
        [shape((2 * taken * channels, 2 * taken * channels), BF16) for taken in widths]
        + [
            shape((outs, size), BF16),
            shape((size, lanes), F32),
            shape((outs, lanes), F32),
            shape((outs, lanes), F32),
            shape(flat, F32),
            shape(flat, F32),
        ],
        [VMEM] * 7,
        vmem=big,
    )(*small)
    firsts = [firsts[widths.index(taken)] for _, taken in groups]

    predicted, residual = call(
        functools.partial(net_kernel, routes, own_out, groups),
        [shape((2 * wide, own_out, lanes), F32), shape(flat, BF16)],
        [VMEM] * (wide + len(groups) + 6),
        [pltpu.VMEM((size, (wide + 1) * lanes), BF16)],
        vmem=big,
    )(*windows, *firsts, a2, b1, b2, head, select, target)

    turned = call(turn_kernel, shape((rows, 2 * lanes), BF16), [VMEM] * 2, vmem=big)(row_weights, residual)
    shifts = [(0, t) for t in range(1, pair)] + [(s, 0) for s in range(1, narrow)]
    shifts += [(s, t) for s in range(1, narrow) for t in range(1, pair)]
    blocks = [residual] + [send_both(residual, s, t) for s, t in shifts]
    shifts.insert(0, (0, 0))
    adjoint, predicted = call(
        functools.partial(adjoint_kernel, shifts, own_out),
        [shape((sparse_count, own_out, lanes), F32), shape(predicted.shape, F32)],
        [VMEM] * (len(blocks) + 2),
        vmem=big,
    )(*blocks, turned, predicted)
    return (predicted, adjoint)


def solution(mesh):
    in_specs = (
        P(("parts", "wide"), None, None, ("narrow", "pair")),
        P(),
        P(),
        P(),
        P(),
        P(),
        P(("parts", "narrow"), None),
        P("parts", "wide", ("narrow", "pair")),
        P(("narrow", "pair"), None),
    )
    out_specs = (P("parts", "wide", ("narrow", "pair")), P("parts", "wide", ("narrow", "pair")))
    return jax.shard_map(local, mesh=mesh, in_specs=in_specs, out_specs=out_specs, check_vma=False)
```

```python
import functools

import jax
import jax.numpy as jnp
from jax import lax
from jax.experimental import pallas as pl
from jax.experimental.pallas import tpu as pltpu
from jax.sharding import PartitionSpec as P

F32, BF16 = jnp.float32, jnp.bfloat16
VMEM = pl.BlockSpec(memory_space=pltpu.VMEM)
TAPS = 4


def call(kernel, outs, in_specs, scratch=(), vmem=16, flops=10**6):
    nbytes = sum(o.size * o.dtype.itemsize for o in jax.tree.leaves(outs))
    return pl.pallas_call(
        kernel,
        out_shape=outs,
        in_specs=in_specs,
        out_specs=jax.tree.map(lambda _: VMEM, outs),
        scratch_shapes=list(scratch),
        compiler_params=pltpu.CompilerParams(vmem_limit_bytes=int(vmem * 2**20)),
        cost_estimate=pl.CostEstimate(flops=flops, bytes_accessed=nbytes, transcendentals=0),
    )


def leaky_relu(values):
    return jnp.maximum(values, 0.1 * values)


def split(index, size):
    whole = ((index.astype(F32) + 0.5) * (1.0 / size)).astype(jnp.int32)
    return whole, index - whole * size


def iota(shape, axis):
    return lax.broadcasted_iota(jnp.int32, shape, axis)


def rounds(count, cores):
    if count == 4:
        schedules = [
            [(1, 3, 0, 2), (3, 2, 1, 0), (2, 0, 3, 1)],
            [(2, 3, 1, 0), (3, 2, 0, 1), (1, 0, 3, 2)],
        ]
    else:
        schedules = [[tuple((i + shift) % count for i in range(count)) for shift in range(1, count)]]
    return [
        tuple(schedules[core % len(schedules)][r][i] for i in range(count) for core in range(cores))
        for r in range(count - 1)
    ]


def sources(route, cores):
    back = [0] * len(route)
    for place, target in enumerate(route):
        back[target * cores + place % cores] = place // cores
    return tuple(back)


def entry(table, axes):
    index = lax.axis_index(axes)
    value = jnp.int32(table[0])
    for i in range(1, len(table)):
        value = jnp.where(index == i, jnp.int32(table[i]), value)
    return value


def column_groups(channels, span):
    most = max(1, 256 // (2 * channels) // 2 * 2)
    return [(first, min(most, span - first)) for first in range(0, span, most)]


def pack_kernel(routes, low_ref, *refs):
    windows, (block_ref, rows_ref, sems) = refs[: len(routes) + 1], refs[len(routes) + 1 :]
    _, channels, width, rows = low_ref.shape
    parts = sems.shape[0]
    each = channels // parts
    pieces = []
    for i in range(parts):
        piece = pl.ds(i * each, each)
        pieces.append(pltpu.make_async_copy(low_ref.at[0, piece], block_ref.at[piece], sems.at[i]))
        pieces[-1].start()
    edge = jnp.zeros((8, rows), F32)
    rows_ref[0:8, :] = edge
    rows_ref[8 + channels * width : 16 + channels * width, :] = edge
    for i in range(parts):
        pieces[i].wait()
        values = block_ref[i * each : (i + 1) * each].astype(F32).reshape(each * width, rows)
        rows_ref[8 + i * each * width : 8 + (i + 1) * each * width, :] = values
    own = width // (len(routes) + 1)
    me = lax.axis_index("wide")
    for window, target in zip(windows, [me] + [entry(route, ("wide", "pair")) for route in routes]):
        first = target * own + 7
        columns = [rows_ref[pl.ds(first + i, channels, stride=width), :] for i in range(own + 2)]
        window[...] = jnp.concatenate(columns, axis=0).astype(BF16)


def prepare_kernel(
    wide,
    own_out,
    groups,
    aw_ref,
    ab_ref,
    cw_ref,
    cb_ref,
    hw_ref,
    measured_ref,
    sparse_ref,
    *refs,
):
    firsts, (a2_ref, b1_ref, b2_ref, h_ref, select_ref, target_ref) = refs[:-6], refs[-6:]
    channels = aw_ref.shape[1]
    span = 2 * own_out + 2
    size, outs = span * channels, own_out * channels
    rows, columns = split(iota((size, channels), 0), channels)
    pick = (columns == iota((size, channels), 1)).astype(F32)
    pick16 = pick.astype(BF16)
    out_channel, _ = split(iota((outs, channels), 0), own_out)
    pick_out = (out_channel == iota((outs, channels), 1)).astype(F32)
    pick_out16 = pick_out.astype(BF16)

    def spread(left, weight, right):
        half = lax.dot_general(left, weight, (((1,), (1,)), ((), ())), preferred_element_type=F32)
        return lax.dot_general(half.astype(BF16), right, (((1,), (1,)), ((), ())), preferred_element_type=F32)

    for first_ref in firsts:
        many = first_ref.shape[0] // 2
        taken = many // channels
        which, channel = split(iota((2 * many, channels), 0), channels)
        is_channel = channel == iota((2 * many, channels), 1)
        sides = [is_channel & (which >= side * taken) & (which < (side + 1) * taken) for side in range(2)]
        sides = [side.astype(F32).astype(BF16) for side in sides]
        row_column = split(iota((many, 2 * many), 0), channels)[0]
        column_column = split(iota((many, 2 * many), 1), channels)[0]
        same = (row_column == column_column) | (row_column + taken == column_column)
        for e in range(2):
            full = spread(pick16[:many], aw_ref[e], sides[0]) + spread(pick16[:many], aw_ref[e + 2], sides[1])
            first_ref[e * many : (e + 1) * many, :] = jnp.where(same, full, 0.0).astype(BF16)

    in_column = split(iota((outs, size), 1), channels)[0]
    out_column = split(iota((outs, size), 0), own_out)[1]
    me = lax.axis_index("wide")
    absolute = in_column + me * (2 * own_out) - 1
    inside = (absolute >= 0) & (absolute < 2 * own_out * wide)
    total = jnp.zeros((outs, size), F32)
    for tap in range(TAPS):
        here = (in_column == 2 * out_column + tap) & inside
        total = jnp.where(here, spread(pick_out16, cw_ref[tap], pick16), total)
    a2_ref[...] = total.astype(BF16)

    def along(left, vector_ref, out_ref):
        summed = jnp.sum(left * vector_ref[...].astype(F32), axis=1, keepdims=True)
        out_ref[...] = jnp.broadcast_to(summed, out_ref.shape)

    along(pick, ab_ref, b1_ref)
    along(pick_out, cb_ref, b2_ref)
    along(pick_out, hw_ref, h_ref)

    sparse_count = measured_ref.shape[0]
    wanted = (select_ref.shape[0], sparse_count)
    pick_view = (split(iota(wanted, 0), own_out)[0] == iota(wanted, 1)).astype(F32)
    along(pick_view, sparse_ref, select_ref)
    for k in range(sparse_count):
        target_ref[k * own_out : (k + 1) * own_out, :] = measured_ref[k]


def turn_kernel(rw_ref, _, turned_ref):
    turned = rw_ref[...].T
    high = turned.astype(BF16)
    turned_ref[:, : high.shape[1]] = high
    turned_ref[:, high.shape[1] :] = (turned - high.astype(F32)).astype(BF16)


def net_kernel(routes, own_out, groups, *refs):
    wide = len(routes) + 1
    windows, firsts, refs = refs[:wide], refs[wide : wide + len(groups)], refs[wide + len(groups) :]
    a2_ref, b1_ref, b2_ref, h_ref, select_ref, target_ref, predicted_ref, residual_ref, views_ref = refs
    size, lanes = windows[0].shape
    outs = a2_ref.shape[0]
    channels = outs // own_out
    me = lax.axis_index("wide")
    cores = lax.axis_size("pair")
    origins = [me] + [entry(sources(route, cores), ("wide", "pair")) for route in routes]
    for window, source in zip(windows, origins):
        views_ref[:, pl.ds(pl.multiple_of((source + 1) * lanes, lanes), lanes)] = window[...]
    views_ref[:, :lanes] = views_ref[:, wide * lanes :]

    many = 2 if wide % 2 == 0 else 1
    wider = lambda ref, times: jnp.concatenate([ref[...]] * times, axis=1)
    b1 = wider(b1_ref, many)
    b2, h = wider(b2_ref, 2 * many), wider(h_ref, 2 * many)
    select = select_ref[...]
    picked = jnp.zeros(select.shape, F32)
    for view in range(0, wide, many):
        previous = slice(view * lanes, (view + many) * lanes)
        current = slice((view + 1) * lanes, (view + 1 + many) * lanes)
        pieces = ([], [])
        for (first, taken), first_ref in zip(groups, firsts):
            rows = slice(first * channels, (first + taken) * channels)
            half = taken * channels
            stacked = jnp.concatenate([views_ref[rows, current], views_ref[rows, previous]], axis=0)
            summed = jnp.dot(first_ref[...], stacked, preferred_element_type=F32)
            for e in range(2):
                pieces[e].append(leaky_relu(summed[e * half : (e + 1) * half] + b1[rows]).astype(BF16))
        both = jnp.concatenate([jnp.concatenate(piece, axis=0) for piece in pieces], axis=1)
        hidden = leaky_relu(jnp.dot(a2_ref[...], both, preferred_element_type=F32) + b2) * h
        value = jnp.sum(hidden.reshape(outs // 8, 8, hidden.shape[1]), axis=0)
        apart = own_out
        while apart < 8:
            value += pltpu.roll(value, apart, 0)
            apart *= 2
        for e in range(2):
            for i in range(many):
                out_view = 2 * (view + i) + e
                at = (e * many + i) * lanes
                tile = value[:, at : at + lanes]
                predicted_ref[out_view] = tile[:own_out]
                repeated = jnp.concatenate([tile] * (select.shape[0] // 8), axis=0)
                picked = jnp.where(select == out_view, repeated, picked)
    residual_ref[...] = (picked - target_ref[...]).astype(BF16)


def adjoint_kernel(shifts, own_out, *refs):
    residuals, refs = refs[: len(shifts)], refs[len(shifts) :]
    turned_ref, predicted_ref, out_ref, copied_ref = refs
    copied_ref[...] = predicted_ref[...]
    lanes = residuals[0].shape[1]
    weights = []
    for narrow_shift, pair_shift in shifts:
        narrow, pair = came_from("narrow", narrow_shift), came_from("pair", pair_shift)
        block = narrow * lax.axis_size("pair") + pair
        weights.append(turned_ref[pl.ds(pl.multiple_of(block * lanes, lanes), lanes), :])
    values = jnp.concatenate([ref[...] for ref in residuals], axis=1)
    both = jnp.dot(values, jnp.concatenate(weights, axis=0), preferred_element_type=F32)
    total = both[:, :lanes] + both[:, lanes:]
    for k in range(out_ref.shape[0]):
        out_ref[k] = total[k * own_out : (k + 1) * own_out]


def came_from(axis, distance):
    count = lax.axis_size(axis)
    return lax.rem(lax.axis_index(axis) - distance + count, count)


def send_both(block, narrow_distance, pair_distance):
    narrow, pair = lax.axis_size("narrow"), lax.axis_size("pair")
    route = []
    for i in range(narrow):
        for j in range(pair):
            target = (i + narrow_distance) % narrow * pair + (j + pair_distance) % pair
            route.append((i * pair + j, target))
    return lax.ppermute(block, ("narrow", "pair"), route)


def local(
    low_sino,
    angle_weight,
    angle_bias,
    column_weight,
    column_bias,
    head_weight,
    sparse_views,
    measured,
    row_weights,
):
    wide, narrow, pair = (lax.axis_size(axis) for axis in ("wide", "narrow", "pair"))
    _, channels, width, lanes = low_sino.shape
    own_out = width // wide // 2
    span = 2 * own_out + 2
    size, outs = span * channels, own_out * channels
    sparse_count = measured.shape[0]
    rows = row_weights.shape[1]
    flat = (sparse_count * own_out, lanes)
    shape = jax.ShapeDtypeStruct
    big = 16 if width <= 64 else 48

    small = (
        angle_weight,
        angle_bias[None],
        column_weight,
        column_bias[None],
        head_weight[None],
        measured,
        sparse_views,
    )
    routes = rounds(wide, pair)
    groups = column_groups(channels, span)
    windows = call(
        functools.partial(pack_kernel, routes),
        [shape((size, lanes), BF16)] * wide,
        [pl.BlockSpec(memory_space=pltpu.HBM)],
        [
            pltpu.VMEM((channels, width, lanes), BF16),
            pltpu.VMEM((16 + channels * width, lanes), F32),
            pltpu.SemaphoreType.DMA((4,)),
        ],
        vmem=53.6 if width <= 64 else 48,
    )(low_sino)
    windows = [windows[0]] + [
        lax.ppermute(window, ("wide", "pair"), [(p, t * pair + p % pair) for p, t in enumerate(route)])
        for window, route in zip(windows[1:], routes)
    ]

    widths = sorted({taken for _, taken in groups})
    *firsts, a2, b1, b2, head, select, target = call(
        functools.partial(prepare_kernel, wide, own_out, groups),
        [shape((2 * taken * channels, 2 * taken * channels), BF16) for taken in widths]
        + [
            shape((outs, size), BF16),
            shape((size, lanes), F32),
            shape((outs, lanes), F32),
            shape((outs, lanes), F32),
            shape(flat, F32),
            shape(flat, F32),
        ],
        [VMEM] * 7,
        vmem=big,
    )(*small)
    firsts = [firsts[widths.index(taken)] for _, taken in groups]

    predicted, residual = call(
        functools.partial(net_kernel, routes, own_out, groups),
        [shape((2 * wide, own_out, lanes), F32), shape(flat, BF16)],
        [VMEM] * (wide + len(groups) + 6),
        [pltpu.VMEM((size, (wide + 1) * lanes), BF16)],
        vmem=big,
    )(*windows, *firsts, a2, b1, b2, head, select, target)

    turned = call(turn_kernel, shape((rows, 2 * lanes), BF16), [VMEM] * 2, vmem=big)(row_weights, residual)
    shifts = [(0, t) for t in range(1, pair)] + [(s, 0) for s in range(1, narrow)]
    shifts += [(s, t) for s in range(1, narrow) for t in range(1, pair)]
    blocks = [residual] + [send_both(residual, s, t) for s, t in shifts]
    shifts.insert(0, (0, 0))
    adjoint, predicted = call(
        functools.partial(adjoint_kernel, shifts, own_out),
        [shape((sparse_count, own_out, lanes), F32), shape(predicted.shape, F32)],
        [VMEM] * (len(blocks) + 2),
        vmem=big,
    )(*blocks, turned, predicted)
    return (predicted, adjoint)


def solution(mesh):
    in_specs = (
        P(("parts", "wide"), None, None, ("narrow", "pair")),
        P(),
        P(),
        P(),
        P(),
        P(),
        P(("parts", "narrow"), None),
        P("parts", "wide", ("narrow", "pair")),
        P(("narrow", "pair"), None),
    )
    out_specs = (P("parts", "wide", ("narrow", "pair")), P("parts", "wide", ("narrow", "pair")))
    return jax.shard_map(local, mesh=mesh, in_specs=in_specs, out_specs=out_specs, check_vma=False)
```

```python
import functools

import jax
import jax.numpy as jnp
from jax import lax
from jax.experimental import pallas as pl
from jax.experimental.pallas import tpu as pltpu
from jax.sharding import PartitionSpec as P

F32, BF16 = jnp.float32, jnp.bfloat16
VMEM = pl.BlockSpec(memory_space=pltpu.VMEM)
TAPS = 4


def call(kernel, outs, in_specs, scratch=(), vmem=16, flops=10**6):
    nbytes = sum(o.size * o.dtype.itemsize for o in jax.tree.leaves(outs))
    return pl.pallas_call(
        kernel,
        out_shape=outs,
        in_specs=in_specs,
        out_specs=jax.tree.map(lambda _: VMEM, outs),
        scratch_shapes=list(scratch),
        compiler_params=pltpu.CompilerParams(vmem_limit_bytes=int(vmem * 2**20)),
        cost_estimate=pl.CostEstimate(flops=flops, bytes_accessed=nbytes, transcendentals=0),
    )


def leaky_relu(values):
    return jnp.maximum(values, 0.1 * values)


def split(index, size):
    whole = ((index.astype(F32) + 0.5) * (1.0 / size)).astype(jnp.int32)
    return whole, index - whole * size


def iota(shape, axis):
    return lax.broadcasted_iota(jnp.int32, shape, axis)


def rounds(count, cores):
    if count == 4:
        schedules = [
            [(1, 3, 0, 2), (3, 2, 1, 0), (2, 0, 3, 1)],
            [(2, 3, 1, 0), (3, 2, 0, 1), (1, 0, 3, 2)],
        ]
    else:
        schedules = [[tuple((i + shift) % count for i in range(count)) for shift in range(1, count)]]
    return [
        tuple(schedules[core % len(schedules)][r][i] for i in range(count) for core in range(cores))
        for r in range(count - 1)
    ]


def sources(route, cores):
    back = [0] * len(route)
    for place, target in enumerate(route):
        back[target * cores + place % cores] = place // cores
    return tuple(back)


def entry(table, axes):
    index = lax.axis_index(axes)
    value = jnp.int32(table[0])
    for i in range(1, len(table)):
        value = jnp.where(index == i, jnp.int32(table[i]), value)
    return value


def column_groups(channels, span):
    most = max(1, 256 // (2 * channels) // 2 * 2)
    return [(first, min(most, span - first)) for first in range(0, span, most)]


def pack_kernel(routes, low_ref, *refs):
    windows, (block_ref, rows_ref, sems) = refs[: len(routes) + 1], refs[len(routes) + 1 :]
    _, channels, width, rows = low_ref.shape
    own = width // (len(routes) + 1)
    span = own + 2
    copies = []
    for g in range(channels // 8):
        group = pl.ds(8 * g, 8)
        copies.append(pltpu.make_async_copy(low_ref.at[0, group], block_ref.at[group], sems.at[g]))
        copies[-1].start()
    me = lax.axis_index("wide")
    firsts = [target * own + 7 for target in [me] + [entry(route, ("wide", "pair")) for route in routes]]
    edge = jnp.zeros((8, rows), F32)
    for g, copy in enumerate(copies):
        rows_ref[g, 0:8, :] = edge
        rows_ref[g, 8 + 8 * width : 16 + 8 * width, :] = edge
        copy.wait()
        values = block_ref[8 * g : 8 * g + 8].astype(F32).reshape(8 * width, rows)
        rows_ref[g, 8 : 8 + 8 * width, :] = values
        for window, first in zip(windows, firsts):
            columns = [rows_ref[g, pl.ds(first + i, 8, stride=width), :] for i in range(span)]
            window[8 * g * span : 8 * (g + 1) * span, :] = jnp.concatenate(columns, axis=0).astype(BF16)


def prepare_kernel(
    wide,
    own_out,
    groups,
    aw_ref,
    ab_ref,
    cw_ref,
    cb_ref,
    hw_ref,
    measured_ref,
    sparse_ref,
    *refs,
):
    firsts, (a2_ref, b1_ref, b2_ref, h_ref, select_ref, target_ref) = refs[:-6], refs[-6:]
    channels = aw_ref.shape[1]
    span = 2 * own_out + 2
    size, outs = span * channels, own_out * channels
    rows, columns = split(iota((size, channels), 0), channels)
    pick = (columns == iota((size, channels), 1)).astype(F32)
    pick16 = pick.astype(BF16)
    out_channel, _ = split(iota((outs, channels), 0), own_out)
    pick_out = (out_channel == iota((outs, channels), 1)).astype(F32)
    pick_out16 = pick_out.astype(BF16)

    def spread(left, weight, right):
        half = lax.dot_general(left, weight, (((1,), (1,)), ((), ())), preferred_element_type=F32)
        return lax.dot_general(half.astype(BF16), right, (((1,), (1,)), ((), ())), preferred_element_type=F32)

    for first_ref in firsts:
        many = first_ref.shape[0] // 2
        taken = many // channels

        def place(shape, axis):
            side, within = split(iota(shape, axis), many)
            group, within = split(within, 8 * taken)
            column, channel = split(within, 8)
            return side, column, 8 * group + channel

        side, _, channel = place((2 * many, channels), 0)
        is_channel = channel == iota((2 * many, channels), 1)
        sides = [(is_channel & (side == i)).astype(F32).astype(BF16) for i in range(2)]
        same = split(iota((many, 2 * many), 0), channels)[0] == place((many, 2 * many), 1)[1]
        for e in range(2):
            full = spread(pick16[:many], aw_ref[e], sides[0]) + spread(pick16[:many], aw_ref[e + 2], sides[1])
            first_ref[e * many : (e + 1) * many, :] = jnp.where(same, full, 0.0).astype(BF16)

    in_column = split(iota((outs, size), 1), channels)[0]
    out_column = split(iota((outs, size), 0), own_out)[1]
    me = lax.axis_index("wide")
    absolute = in_column + me * (2 * own_out) - 1
    inside = (absolute >= 0) & (absolute < 2 * own_out * wide)
    total = jnp.zeros((outs, size), F32)
    for tap in range(TAPS):
        here = (in_column == 2 * out_column + tap) & inside
        total = jnp.where(here, spread(pick_out16, cw_ref[tap], pick16), total)
    a2_ref[...] = total.astype(BF16)

    def along(left, vector_ref, out_ref):
        summed = jnp.sum(left * vector_ref[...].astype(F32), axis=1, keepdims=True)
        out_ref[...] = jnp.broadcast_to(summed, out_ref.shape)

    along(pick, ab_ref, b1_ref)
    along(pick_out, cb_ref, b2_ref)
    along(pick_out, hw_ref, h_ref)

    sparse_count = measured_ref.shape[0]
    wanted = (select_ref.shape[0], sparse_count)
    pick_view = (split(iota(wanted, 0), own_out)[0] == iota(wanted, 1)).astype(F32)
    along(pick_view, sparse_ref, select_ref)
    for k in range(sparse_count):
        target_ref[k * own_out : (k + 1) * own_out, :] = measured_ref[k]


def turn_kernel(rw_ref, _, turned_ref):
    turned = rw_ref[...].T
    high = turned.astype(BF16)
    turned_ref[:, : high.shape[1]] = high
    turned_ref[:, high.shape[1] :] = (turned - high.astype(F32)).astype(BF16)


def net_kernel(routes, own_out, groups, *refs):
    wide = len(routes) + 1
    windows, firsts, refs = refs[:wide], refs[wide : wide + len(groups)], refs[wide + len(groups) :]
    a2_ref, b1_ref, b2_ref, h_ref, select_ref, target_ref, predicted_ref, residual_ref, views_ref = refs
    size, lanes = windows[0].shape
    outs = a2_ref.shape[0]
    channels = outs // own_out
    span = size // channels
    me = lax.axis_index("wide")
    cores = lax.axis_size("pair")
    origins = [me] + [entry(sources(route, cores), ("wide", "pair")) for route in routes]
    for window, source in zip(windows, origins):
        views_ref[:, pl.ds(pl.multiple_of((source + 1) * lanes, lanes), lanes)] = window[...]
    views_ref[:, :lanes] = views_ref[:, wide * lanes :]

    many = 2 if wide % 2 == 0 else 1
    wider = lambda ref, times: jnp.concatenate([ref[...]] * times, axis=1)
    b1 = wider(b1_ref, many)
    b2, h = wider(b2_ref, 2 * many), wider(h_ref, 2 * many)
    select = select_ref[...]
    picked = jnp.zeros(select.shape, F32)
    for view in range(0, wide, many):
        previous = slice(view * lanes, (view + many) * lanes)
        current = slice((view + 1) * lanes, (view + 1 + many) * lanes)
        pieces = ([], [])
        for (first, taken), first_ref in zip(groups, firsts):
            rows = slice(first * channels, (first + taken) * channels)
            half = taken * channels
            parts = [
                views_ref[8 * (g * span + first) : 8 * (g * span + first + taken), lane]
                for lane in (current, previous)
                for g in range(channels // 8)
            ]
            stacked = jnp.concatenate(parts, axis=0)
            summed = jnp.dot(first_ref[...], stacked, preferred_element_type=F32)
            for e in range(2):
                pieces[e].append(leaky_relu(summed[e * half : (e + 1) * half] + b1[rows]).astype(BF16))
        both = jnp.concatenate([jnp.concatenate(piece, axis=0) for piece in pieces], axis=1)
        hidden = leaky_relu(jnp.dot(a2_ref[...], both, preferred_element_type=F32) + b2) * h
        value = jnp.sum(hidden.reshape(outs // 8, 8, hidden.shape[1]), axis=0)
        apart = own_out
        while apart < 8:
            value += pltpu.roll(value, apart, 0)
            apart *= 2
        for e in range(2):
            for i in range(many):
                out_view = 2 * (view + i) + e
                at = (e * many + i) * lanes
                tile = value[:, at : at + lanes]
                predicted_ref[out_view] = tile[:own_out]
                repeated = jnp.concatenate([tile] * (select.shape[0] // 8), axis=0)
                picked = jnp.where(select == out_view, repeated, picked)
    residual_ref[...] = (picked - target_ref[...]).astype(BF16)


def adjoint_kernel(shifts, own_out, *refs):
    residuals, refs = refs[: len(shifts)], refs[len(shifts) :]
    turned_ref, predicted_ref, out_ref, copied_ref = refs
    copied_ref[...] = predicted_ref[...]
    lanes = residuals[0].shape[1]
    weights = []
    for narrow_shift, pair_shift in shifts:
        narrow, pair = came_from("narrow", narrow_shift), came_from("pair", pair_shift)
        block = narrow * lax.axis_size("pair") + pair
        weights.append(turned_ref[pl.ds(pl.multiple_of(block * lanes, lanes), lanes), :])
    values = jnp.concatenate([ref[...] for ref in residuals], axis=1)
    both = jnp.dot(values, jnp.concatenate(weights, axis=0), preferred_element_type=F32)
    total = both[:, :lanes] + both[:, lanes:]
    for k in range(out_ref.shape[0]):
        out_ref[k] = total[k * own_out : (k + 1) * own_out]


def came_from(axis, distance):
    count = lax.axis_size(axis)
    return lax.rem(lax.axis_index(axis) - distance + count, count)


def send_both(block, narrow_distance, pair_distance):
    narrow, pair = lax.axis_size("narrow"), lax.axis_size("pair")
    route = []
    for i in range(narrow):
        for j in range(pair):
            target = (i + narrow_distance) % narrow * pair + (j + pair_distance) % pair
            route.append((i * pair + j, target))
    return lax.ppermute(block, ("narrow", "pair"), route)


def local(
    low_sino,
    angle_weight,
    angle_bias,
    column_weight,
    column_bias,
    head_weight,
    sparse_views,
    measured,
    row_weights,
):
    wide, narrow, pair = (lax.axis_size(axis) for axis in ("wide", "narrow", "pair"))
    _, channels, width, lanes = low_sino.shape
    own_out = width // wide // 2
    span = 2 * own_out + 2
    size, outs = span * channels, own_out * channels
    sparse_count = measured.shape[0]
    rows = row_weights.shape[1]
    flat = (sparse_count * own_out, lanes)
    shape = jax.ShapeDtypeStruct
    big = 16 if width <= 64 else 48

    small = (
        angle_weight,
        angle_bias[None],
        column_weight,
        column_bias[None],
        head_weight[None],
        measured,
        sparse_views,
    )
    routes = rounds(wide, pair)
    groups = column_groups(channels, span)
    windows = call(
        functools.partial(pack_kernel, routes),
        [shape((size, lanes), BF16)] * wide,
        [pl.BlockSpec(memory_space=pltpu.HBM)],
        [
            pltpu.VMEM((channels, width, lanes), BF16),
            pltpu.VMEM((channels // 8, 16 + 8 * width, lanes), F32),
            pltpu.SemaphoreType.DMA((channels // 8,)),
        ],
        vmem=53.6 if width <= 64 else 48,
    )(low_sino)
    windows = [windows[0]] + [
        lax.ppermute(window, ("wide", "pair"), [(p, t * pair + p % pair) for p, t in enumerate(route)])
        for window, route in zip(windows[1:], routes)
    ]

    widths = sorted({taken for _, taken in groups})
    *firsts, a2, b1, b2, head, select, target = call(
        functools.partial(prepare_kernel, wide, own_out, groups),
        [shape((2 * taken * channels, 2 * taken * channels), BF16) for taken in widths]
        + [
            shape((outs, size), BF16),
            shape((size, lanes), F32),
            shape((outs, lanes), F32),
            shape((outs, lanes), F32),
            shape(flat, F32),
            shape(flat, F32),
        ],
        [VMEM] * 7,
        vmem=big,
    )(*small)
    firsts = [firsts[widths.index(taken)] for _, taken in groups]

    predicted, residual = call(
        functools.partial(net_kernel, routes, own_out, groups),
        [shape((2 * wide, own_out, lanes), F32), shape(flat, BF16)],
        [VMEM] * (wide + len(groups) + 6),
        [pltpu.VMEM((size, (wide + 1) * lanes), BF16)],
        vmem=big,
    )(*windows, *firsts, a2, b1, b2, head, select, target)

    turned = call(turn_kernel, shape((rows, 2 * lanes), BF16), [VMEM] * 2, vmem=big)(row_weights, residual)
    shifts = [(0, t) for t in range(1, pair)] + [(s, 0) for s in range(1, narrow)]
    shifts += [(s, t) for s in range(1, narrow) for t in range(1, pair)]
    blocks = [residual] + [send_both(residual, s, t) for s, t in shifts]
    shifts.insert(0, (0, 0))
    adjoint, predicted = call(
        functools.partial(adjoint_kernel, shifts, own_out),
        [shape((sparse_count, own_out, lanes), F32), shape(predicted.shape, F32)],
        [VMEM] * (len(blocks) + 2),
        vmem=big,
    )(*blocks, turned, predicted)
    return (predicted, adjoint)


def solution(mesh):
    in_specs = (
        P(("parts", "wide"), None, None, ("narrow", "pair")),
        P(),
        P(),
        P(),
        P(),
        P(),
        P(("parts", "narrow"), None),
        P("parts", "wide", ("narrow", "pair")),
        P(("narrow", "pair"), None),
    )
    out_specs = (P("parts", "wide", ("narrow", "pair")), P("parts", "wide", ("narrow", "pair")))
    return jax.shard_map(local, mesh=mesh, in_specs=in_specs, out_specs=out_specs, check_vma=False)
```

```python
import functools

import jax
import jax.numpy as jnp
from jax import lax
from jax.experimental import pallas as pl
from jax.experimental.pallas import tpu as pltpu
from jax.sharding import PartitionSpec as P

F32, BF16 = jnp.float32, jnp.bfloat16
VMEM = pl.BlockSpec(memory_space=pltpu.VMEM)
TAPS = 4


def call(kernel, outs, in_specs, scratch=(), vmem=16, flops=10**6):
    nbytes = sum(o.size * o.dtype.itemsize for o in jax.tree.leaves(outs))
    return pl.pallas_call(
        kernel,
        out_shape=outs,
        in_specs=in_specs,
        out_specs=jax.tree.map(lambda _: VMEM, outs),
        scratch_shapes=list(scratch),
        compiler_params=pltpu.CompilerParams(vmem_limit_bytes=int(vmem * 2**20)),
        cost_estimate=pl.CostEstimate(flops=flops, bytes_accessed=nbytes, transcendentals=0),
    )


def leaky_relu(values):
    return jnp.maximum(values, 0.1 * values)


def split(index, size):
    whole = ((index.astype(F32) + 0.5) * (1.0 / size)).astype(jnp.int32)
    return whole, index - whole * size


def iota(shape, axis):
    return lax.broadcasted_iota(jnp.int32, shape, axis)


def rounds(count, cores):
    if count == 4:
        schedules = [
            [(1, 3, 0, 2), (3, 2, 1, 0), (2, 0, 3, 1)],
            [(2, 3, 1, 0), (3, 2, 0, 1), (1, 0, 3, 2)],
        ]
    else:
        schedules = [[tuple((i + shift) % count for i in range(count)) for shift in range(1, count)]]
    return [
        tuple(schedules[core % len(schedules)][r][i] for i in range(count) for core in range(cores))
        for r in range(count - 1)
    ]


def sources(route, cores):
    back = [0] * len(route)
    for place, target in enumerate(route):
        back[target * cores + place % cores] = place // cores
    return tuple(back)


def entry(table, axes):
    index = lax.axis_index(axes)
    value = jnp.int32(table[0])
    for i in range(1, len(table)):
        value = jnp.where(index == i, jnp.int32(table[i]), value)
    return value


def column_groups(channels, span):
    most = max(1, 256 // (2 * channels) // 2 * 2)
    return [(first, min(most, span - first)) for first in range(0, span, most)]


def pack_kernel(routes, low_ref, *refs):
    windows, (block_ref, rows_ref, sems) = refs[: len(routes) + 1], refs[len(routes) + 1 :]
    _, channels, width, rows = low_ref.shape
    parts = sems.shape[0]
    each = channels // parts
    pieces = []
    for i in range(parts):
        piece = pl.ds(i * each, each)
        pieces.append(pltpu.make_async_copy(low_ref.at[0, piece], block_ref.at[piece], sems.at[i]))
        pieces[-1].start()
    edge = jnp.zeros((8, rows), F32)
    rows_ref[0:8, :] = edge
    rows_ref[8 + channels * width : 16 + channels * width, :] = edge
    for i in range(parts):
        pieces[i].wait()
        values = block_ref[i * each : (i + 1) * each].astype(F32).reshape(each * width, rows)
        rows_ref[8 + i * each * width : 8 + (i + 1) * each * width, :] = values
    own = width // (len(routes) + 1)
    me = lax.axis_index("wide")
    for window, target in zip(windows, [me] + [entry(route, ("wide", "pair")) for route in routes]):
        first = target * own + 7
        columns = [rows_ref[pl.ds(first + i, channels, stride=width), :] for i in range(own + 2)]
        window[...] = jnp.concatenate(columns, axis=0).astype(BF16)


def prepare_kernel(
    wide,
    own_out,
    groups,
    aw_ref,
    ab_ref,
    cw_ref,
    cb_ref,
    hw_ref,
    measured_ref,
    sparse_ref,
    *refs,
):
    firsts, (a2_ref, b1_ref, b2_ref, h_ref, select_ref, target_ref) = refs[:-6], refs[-6:]
    channels = aw_ref.shape[1]
    span = 2 * own_out + 2
    size, outs = span * channels, own_out * channels
    rows, columns = split(iota((size, channels), 0), channels)
    pick = (columns == iota((size, channels), 1)).astype(F32)
    pick16 = pick.astype(BF16)
    out_channel, _ = split(iota((outs, channels), 0), own_out)
    pick_out = (out_channel == iota((outs, channels), 1)).astype(F32)
    pick_out16 = pick_out.astype(BF16)

    def spread(left, weight, right):
        half = lax.dot_general(left, weight, (((1,), (1,)), ((), ())), preferred_element_type=F32)
        return lax.dot_general(half.astype(BF16), right, (((1,), (1,)), ((), ())), preferred_element_type=F32)

    for first_ref in firsts:
        many = first_ref.shape[0] // 2
        taken = many // channels
        which, channel = split(iota((2 * many, channels), 0), channels)
        is_channel = channel == iota((2 * many, channels), 1)
        sides = [is_channel & (which >= side * taken) & (which < (side + 1) * taken) for side in range(2)]
        sides = [side.astype(F32).astype(BF16) for side in sides]
        row_column = split(iota((many, 2 * many), 0), channels)[0]
        column_column = split(iota((many, 2 * many), 1), channels)[0]
        same = (row_column == column_column) | (row_column + taken == column_column)
        for e in range(2):
            full = spread(pick16[:many], aw_ref[e], sides[0]) + spread(pick16[:many], aw_ref[e + 2], sides[1])
            first_ref[e * many : (e + 1) * many, :] = jnp.where(same, full, 0.0).astype(BF16)

    in_column = split(iota((outs, size), 1), channels)[0]
    out_column = split(iota((outs, size), 0), own_out)[1]
    me = lax.axis_index("wide")
    absolute = in_column + me * (2 * own_out) - 1
    inside = (absolute >= 0) & (absolute < 2 * own_out * wide)
    total = jnp.zeros((outs, size), F32)
    for tap in range(TAPS):
        here = (in_column == 2 * out_column + tap) & inside
        total = jnp.where(here, spread(pick_out16, cw_ref[tap], pick16), total)
    a2_ref[...] = total.astype(BF16)

    def along(left, vector_ref, out_ref):
        summed = jnp.sum(left * vector_ref[...].astype(F32), axis=1, keepdims=True)
        out_ref[...] = jnp.broadcast_to(summed, out_ref.shape)

    along(pick, ab_ref, b1_ref)
    along(pick_out, cb_ref, b2_ref)
    along(pick_out, hw_ref, h_ref)

    sparse_count = measured_ref.shape[0]
    wanted = (select_ref.shape[0], sparse_count)
    pick_view = (split(iota(wanted, 0), own_out)[0] == iota(wanted, 1)).astype(F32)
    along(pick_view, sparse_ref, select_ref)
    for k in range(sparse_count):
        target_ref[k * own_out : (k + 1) * own_out, :] = measured_ref[k]


def turn_kernel(rw_ref, _, turned_ref):
    turned = rw_ref[...].T
    high = turned.astype(BF16)
    turned_ref[:, : high.shape[1]] = high
    turned_ref[:, high.shape[1] :] = (turned - high.astype(F32)).astype(BF16)


def origin(route):
    return entry(sources(route, lax.axis_size("pair")), ("wide", "pair"))


def first_and_second_layer(current, previous, groups, firsts, a2_ref, b1, b2, h, own_out):
    outs = a2_ref.shape[0]
    channels = outs // own_out
    pieces = ([], [])
    for (first, taken), first_ref in zip(groups, firsts):
        rows = slice(first * channels, (first + taken) * channels)
        half = taken * channels
        stacked = jnp.concatenate([current[rows], previous[rows]], axis=0)
        summed = jnp.dot(first_ref[...], stacked, preferred_element_type=F32)
        for e in range(2):
            pieces[e].append(leaky_relu(summed[e * half : (e + 1) * half] + b1[rows]).astype(BF16))
    both = jnp.concatenate([jnp.concatenate(piece, axis=0) for piece in pieces], axis=1)
    hidden = leaky_relu(jnp.dot(a2_ref[...], both, preferred_element_type=F32) + b2) * h
    value = jnp.sum(hidden.reshape(outs // 8, 8, hidden.shape[1]), axis=0)
    apart = own_out
    while apart < 8:
        value += pltpu.roll(value, apart, 0)
        apart *= 2
    return value


def wider(ref, times):
    return jnp.concatenate([ref[...]] * times, axis=1)


def choose(select, view, tile, picked):
    repeated = jnp.concatenate([tile] * (select.shape[0] // 8), axis=0)
    return jnp.where(select == view.astype(F32), repeated, picked)


def early_kernel(routes, own_out, groups, *refs):
    wide = len(routes) + 1
    windows, firsts, refs = refs[: wide - 1], refs[wide - 1 : wide - 1 + len(groups)], refs[wide - 1 + len(groups) :]
    a2_ref, b1_ref, b2_ref, h_ref, select_ref, tiles_ref, picked_ref, next_ref, before_ref, views_ref = refs
    lanes = windows[0].shape[1]
    me = lax.axis_index("wide")
    missing = origin(routes[-1])
    for window, source in zip(windows, [me] + [origin(route) for route in routes[:-1]]):
        slot = lax.rem(source - missing + wide, wide) - 1
        views_ref[:, pl.ds(pl.multiple_of(slot * lanes, lanes), lanes)] = window[...]
    next_ref[...] = views_ref[:, :lanes]
    before_ref[...] = views_ref[:, (wide - 2) * lanes :]
    many = 2 if wide % 2 == 0 else 1
    b1, b2, h = wider(b1_ref, many), wider(b2_ref, 2 * many), wider(h_ref, 2 * many)
    select = select_ref[...]
    picked = jnp.zeros(select.shape, F32)
    for pair in range(0, wide - 2, many):
        previous = views_ref[:, pair * lanes : (pair + many) * lanes]
        current = views_ref[:, (pair + 1) * lanes : (pair + 1 + many) * lanes]
        value = first_and_second_layer(current, previous, groups, firsts, a2_ref, b1, b2, h, own_out)
        for e in range(2):
            for i in range(many):
                tile = value[:, (e * many + i) * lanes : (e * many + i + 1) * lanes]
                tiles_ref[2 * (pair + i) + e] = tile
                view = 2 * lax.rem(missing + 2 + pair + i, wide) + e
                picked = choose(select, view, tile, picked)
    picked_ref[...] = picked


def late_kernel(routes, own_out, groups, *refs):
    wide = len(routes) + 1
    window_ref, next_ref, before_ref, *firsts = refs[: 3 + len(groups)]
    a2_ref, b1_ref, b2_ref, h_ref, select_ref, target_ref, picked_ref, tiles_ref, residual_ref = refs[3 + len(groups) :]
    lanes = window_ref.shape[1]
    missing = origin(routes[-1])
    current = jnp.concatenate([window_ref[...], next_ref[...]], axis=1)
    previous = jnp.concatenate([before_ref[...], window_ref[...]], axis=1)
    b1, b2, h = wider(b1_ref, 2), wider(b2_ref, 4), wider(h_ref, 4)
    value = first_and_second_layer(current, previous, groups, firsts, a2_ref, b1, b2, h, own_out)
    select, picked = select_ref[...], picked_ref[...]
    for e in range(2):
        for i in range(2):
            tile = value[:, (2 * e + i) * lanes : (2 * e + i + 1) * lanes]
            tiles_ref[2 * i + e] = tile
            picked = choose(select, 2 * lax.rem(missing + i, wide) + e, tile, picked)
    residual_ref[...] = (picked - target_ref[...]).astype(BF16)


def adjoint_kernel(routes, shifts, own_out, *refs):
    residuals, refs = refs[: len(shifts)], refs[len(shifts) :]
    turned_ref, early_ref, late_ref, out_ref, predicted_ref = refs
    wide = len(routes) + 1
    missing = origin(routes[-1])
    for pair in range(wide):
        view = lax.rem(missing + pair, wide)
        for e in range(2):
            tile = late_ref[2 * pair + e] if pair < 2 else early_ref[2 * (pair - 2) + e]
            predicted_ref[2 * view + e] = tile[:own_out]
    lanes = residuals[0].shape[1]
    weights = []
    for narrow_shift, pair_shift in shifts:
        narrow, pair = came_from("narrow", narrow_shift), came_from("pair", pair_shift)
        block = narrow * lax.axis_size("pair") + pair
        weights.append(turned_ref[pl.ds(pl.multiple_of(block * lanes, lanes), lanes), :])
    values = jnp.concatenate([ref[...] for ref in residuals], axis=1)
    both = jnp.dot(values, jnp.concatenate(weights, axis=0), preferred_element_type=F32)
    total = both[:, :lanes] + both[:, lanes:]
    for k in range(out_ref.shape[0]):
        out_ref[k] = total[k * own_out : (k + 1) * own_out]


def came_from(axis, distance):
    count = lax.axis_size(axis)
    return lax.rem(lax.axis_index(axis) - distance + count, count)


def send_both(block, narrow_distance, pair_distance):
    narrow, pair = lax.axis_size("narrow"), lax.axis_size("pair")
    route = []
    for i in range(narrow):
        for j in range(pair):
            target = (i + narrow_distance) % narrow * pair + (j + pair_distance) % pair
            route.append((i * pair + j, target))
    return lax.ppermute(block, ("narrow", "pair"), route)


def local(
    low_sino,
    angle_weight,
    angle_bias,
    column_weight,
    column_bias,
    head_weight,
    sparse_views,
    measured,
    row_weights,
):
    wide, narrow, pair = (lax.axis_size(axis) for axis in ("wide", "narrow", "pair"))
    _, channels, width, lanes = low_sino.shape
    own_out = width // wide // 2
    span = 2 * own_out + 2
    size, outs = span * channels, own_out * channels
    sparse_count = measured.shape[0]
    rows = row_weights.shape[1]
    flat = (sparse_count * own_out, lanes)
    shape = jax.ShapeDtypeStruct
    big = 16 if width <= 64 else 48

    small = (
        angle_weight,
        angle_bias[None],
        column_weight,
        column_bias[None],
        head_weight[None],
        measured,
        sparse_views,
    )
    routes = rounds(wide, pair)
    groups = column_groups(channels, span)
    windows = call(
        functools.partial(pack_kernel, routes),
        [shape((size, lanes), BF16)] * wide,
        [pl.BlockSpec(memory_space=pltpu.HBM)],
        [
            pltpu.VMEM((channels, width, lanes), BF16),
            pltpu.VMEM((16 + channels * width, lanes), F32),
            pltpu.SemaphoreType.DMA((4,)),
        ],
        vmem=53.6 if width <= 64 else 48,
    )(low_sino)
    windows = [windows[0]] + [
        lax.ppermute(window, ("wide", "pair"), [(p, t * pair + p % pair) for p, t in enumerate(route)])
        for window, route in zip(windows[1:], routes)
    ]

    widths = sorted({taken for _, taken in groups})
    *firsts, a2, b1, b2, head, select, target = call(
        functools.partial(prepare_kernel, wide, own_out, groups),
        [shape((2 * taken * channels, 2 * taken * channels), BF16) for taken in widths]
        + [
            shape((outs, size), BF16),
            shape((size, lanes), F32),
            shape((outs, lanes), F32),
            shape((outs, lanes), F32),
            shape(flat, F32),
            shape(flat, F32),
        ],
        [VMEM] * 7,
        vmem=big,
    )(*small)
    firsts = [firsts[widths.index(taken)] for _, taken in groups]

    window = shape((size, lanes), BF16)
    early_tiles, picked, following, before = call(
        functools.partial(early_kernel, routes, own_out, groups),
        [shape((2 * wide - 4, 8, lanes), F32), shape(flat, F32), window, window],
        [VMEM] * (wide + len(groups) + 4),
        [pltpu.VMEM((size, (wide - 1) * lanes), BF16)],
        vmem=big,
    )(*windows[:-1], *firsts, a2, b1, b2, head, select)
    late_tiles, residual = call(
        functools.partial(late_kernel, routes, own_out, groups),
        [shape((4, 8, lanes), F32), shape(flat, BF16)],
        [VMEM] * (len(groups) + 10),
        vmem=big,
    )(windows[-1], following, before, *firsts, a2, b1, b2, head, select, target, picked)

    turned = call(turn_kernel, shape((rows, 2 * lanes), BF16), [VMEM] * 2, vmem=big)(row_weights, residual)
    shifts = [(0, t) for t in range(1, pair)] + [(s, 0) for s in range(1, narrow)]
    shifts += [(s, t) for s in range(1, narrow) for t in range(1, pair)]
    blocks = [residual] + [send_both(residual, s, t) for s, t in shifts]
    shifts.insert(0, (0, 0))
    adjoint, predicted = call(
        functools.partial(adjoint_kernel, routes, shifts, own_out),
        [shape((sparse_count, own_out, lanes), F32), shape((2 * wide, own_out, lanes), F32)],
        [VMEM] * (len(blocks) + 3),
        vmem=big,
    )(*blocks, turned, early_tiles, late_tiles)
    return (predicted, adjoint)


def solution(mesh):
    in_specs = (
        P(("parts", "wide"), None, None, ("narrow", "pair")),
        P(),
        P(),
        P(),
        P(),
        P(),
        P(("parts", "narrow"), None),
        P("parts", "wide", ("narrow", "pair")),
        P(("narrow", "pair"), None),
    )
    out_specs = (P("parts", "wide", ("narrow", "pair")), P("parts", "wide", ("narrow", "pair")))
    return jax.shard_map(local, mesh=mesh, in_specs=in_specs, out_specs=out_specs, check_vma=False)
```

```python
import functools

import jax
import jax.numpy as jnp
from jax import lax
from jax.experimental import pallas as pl
from jax.experimental.pallas import tpu as pltpu
from jax.sharding import PartitionSpec as P

F32, BF16 = jnp.float32, jnp.bfloat16
VMEM = pl.BlockSpec(memory_space=pltpu.VMEM)
TAPS = 4


def call(kernel, outs, in_specs, scratch=(), vmem=16, flops=10**6):
    nbytes = sum(o.size * o.dtype.itemsize for o in jax.tree.leaves(outs))
    return pl.pallas_call(
        kernel,
        out_shape=outs,
        in_specs=in_specs,
        out_specs=jax.tree.map(lambda _: VMEM, outs),
        scratch_shapes=list(scratch),
        compiler_params=pltpu.CompilerParams(vmem_limit_bytes=int(vmem * 2**20)),
        cost_estimate=pl.CostEstimate(flops=flops, bytes_accessed=nbytes, transcendentals=0),
    )


def leaky_relu(values):
    return jnp.maximum(values, 0.1 * values)


def split(index, size):
    whole = ((index.astype(F32) + 0.5) * (1.0 / size)).astype(jnp.int32)
    return whole, index - whole * size


def iota(shape, axis):
    return lax.broadcasted_iota(jnp.int32, shape, axis)


def rounds(count, cores):
    if count == 4:
        schedules = [
            [(3, 2, 1, 0), (1, 0, 3, 2), (2, 3, 0, 1)],
            [(1, 3, 0, 2), (3, 2, 1, 0), (2, 0, 3, 1)],
        ]
    else:
        schedules = [[tuple((i + shift) % count for i in range(count)) for shift in range(1, count)]]
    return [
        tuple(schedules[core % len(schedules)][r][i] for i in range(count) for core in range(cores))
        for r in range(count - 1)
    ]


def sources(route, cores):
    back = [0] * len(route)
    for place, target in enumerate(route):
        back[target * cores + place % cores] = place // cores
    return tuple(back)


def entry(table, axes):
    index = lax.axis_index(axes)
    value = jnp.int32(table[0])
    for i in range(1, len(table)):
        value = jnp.where(index == i, jnp.int32(table[i]), value)
    return value


def column_groups(channels, span):
    most = max(1, 256 // (2 * channels) // 2 * 2)
    return [(first, min(most, span - first)) for first in range(0, span, most)]


def pack_kernel(routes, low_ref, *refs):
    windows, (block_ref, rows_ref, sems) = refs[: len(routes) + 1], refs[len(routes) + 1 :]
    _, channels, width, rows = low_ref.shape
    parts = sems.shape[0]
    each = channels // parts
    pieces = []
    for i in range(parts):
        piece = pl.ds(i * each, each)
        pieces.append(pltpu.make_async_copy(low_ref.at[0, piece], block_ref.at[piece], sems.at[i]))
        pieces[-1].start()
    edge = jnp.zeros((8, rows), F32)
    rows_ref[0:8, :] = edge
    rows_ref[8 + channels * width : 16 + channels * width, :] = edge
    for i in range(parts):
        pieces[i].wait()
        values = block_ref[i * each : (i + 1) * each].astype(F32).reshape(each * width, rows)
        rows_ref[8 + i * each * width : 8 + (i + 1) * each * width, :] = values
    own = width // (len(routes) + 1)
    me = lax.axis_index("wide")
    for window, target in zip(windows, [me] + [entry(route, ("wide", "pair")) for route in routes]):
        first = target * own + 7
        columns = [rows_ref[pl.ds(first + i, channels, stride=width), :] for i in range(own + 2)]
        window[...] = jnp.concatenate(columns, axis=0).astype(BF16)


def prepare_kernel(
    wide,
    own_out,
    groups,
    aw_ref,
    ab_ref,
    cw_ref,
    cb_ref,
    hw_ref,
    measured_ref,
    sparse_ref,
    *refs,
):
    firsts, (a2_ref, b1_ref, b2_ref, h_ref, select_ref, target_ref) = refs[:-6], refs[-6:]
    channels = aw_ref.shape[1]
    span = 2 * own_out + 2
    size, outs = span * channels, own_out * channels
    rows, columns = split(iota((size, channels), 0), channels)
    pick = (columns == iota((size, channels), 1)).astype(F32)
    pick16 = pick.astype(BF16)
    out_channel, _ = split(iota((outs, channels), 0), own_out)
    pick_out = (out_channel == iota((outs, channels), 1)).astype(F32)
    pick_out16 = pick_out.astype(BF16)

    def spread(left, weight, right):
        half = lax.dot_general(left, weight, (((1,), (1,)), ((), ())), preferred_element_type=F32)
        return lax.dot_general(half.astype(BF16), right, (((1,), (1,)), ((), ())), preferred_element_type=F32)

    for first_ref in firsts:
        many = first_ref.shape[0] // 2
        taken = many // channels
        which, channel = split(iota((2 * many, channels), 0), channels)
        is_channel = channel == iota((2 * many, channels), 1)
        sides = [is_channel & (which >= side * taken) & (which < (side + 1) * taken) for side in range(2)]
        sides = [side.astype(F32).astype(BF16) for side in sides]
        row_column = split(iota((many, 2 * many), 0), channels)[0]
        column_column = split(iota((many, 2 * many), 1), channels)[0]
        same = (row_column == column_column) | (row_column + taken == column_column)
        for e in range(2):
            full = spread(pick16[:many], aw_ref[e], sides[0]) + spread(pick16[:many], aw_ref[e + 2], sides[1])
            first_ref[e * many : (e + 1) * many, :] = jnp.where(same, full, 0.0).astype(BF16)

    in_column = split(iota((outs, size), 1), channels)[0]
    out_column = split(iota((outs, size), 0), own_out)[1]
    me = lax.axis_index("wide")
    absolute = in_column + me * (2 * own_out) - 1
    inside = (absolute >= 0) & (absolute < 2 * own_out * wide)
    total = jnp.zeros((outs, size), F32)
    for tap in range(TAPS):
        here = (in_column == 2 * out_column + tap) & inside
        total = jnp.where(here, spread(pick_out16, cw_ref[tap], pick16), total)
    a2_ref[...] = total.astype(BF16)

    def along(left, vector_ref, out_ref):
        summed = jnp.sum(left * vector_ref[...].astype(F32), axis=1, keepdims=True)
        out_ref[...] = jnp.broadcast_to(summed, out_ref.shape)

    along(pick, ab_ref, b1_ref)
    along(pick_out, cb_ref, b2_ref)
    along(pick_out, hw_ref, h_ref)

    sparse_count = measured_ref.shape[0]
    wanted = (select_ref.shape[0], sparse_count)
    pick_view = (split(iota(wanted, 0), own_out)[0] == iota(wanted, 1)).astype(F32)
    along(pick_view, sparse_ref, select_ref)
    for k in range(sparse_count):
        target_ref[k * own_out : (k + 1) * own_out, :] = measured_ref[k]


def turn_kernel(rw_ref, _, turned_ref):
    turned = rw_ref[...].T
    high = turned.astype(BF16)
    turned_ref[:, : high.shape[1]] = high
    turned_ref[:, high.shape[1] :] = (turned - high.astype(F32)).astype(BF16)


def origin(route):
    return entry(sources(route, lax.axis_size("pair")), ("wide", "pair"))


def first_and_second_layer(current, previous, groups, firsts, a2_ref, b1, b2, h, own_out):
    outs = a2_ref.shape[0]
    channels = outs // own_out
    pieces = ([], [])
    for (first, taken), first_ref in zip(groups, firsts):
        rows = slice(first * channels, (first + taken) * channels)
        half = taken * channels
        stacked = jnp.concatenate([current[rows], previous[rows]], axis=0)
        summed = jnp.dot(first_ref[...], stacked, preferred_element_type=F32)
        for e in range(2):
            pieces[e].append(leaky_relu(summed[e * half : (e + 1) * half] + b1[rows]).astype(BF16))
    both = jnp.concatenate([jnp.concatenate(piece, axis=0) for piece in pieces], axis=1)
    hidden = leaky_relu(jnp.dot(a2_ref[...], both, preferred_element_type=F32) + b2) * h
    value = jnp.sum(hidden.reshape(outs // 8, 8, hidden.shape[1]), axis=0)
    apart = own_out
    while apart < 8:
        value += pltpu.roll(value, apart, 0)
        apart *= 2
    return value


def wider(ref, times):
    return jnp.concatenate([ref[...]] * times, axis=1)


def choose(select, view, tile, picked):
    repeated = jnp.concatenate([tile] * (select.shape[0] // 8), axis=0)
    return jnp.where(select == view.astype(F32), repeated, picked)


def early_kernel(routes, own_out, groups, *refs):
    wide = len(routes) + 1
    windows, firsts, refs = refs[: wide - 1], refs[wide - 1 : wide - 1 + len(groups)], refs[wide - 1 + len(groups) :]
    a2_ref, b1_ref, b2_ref, h_ref, select_ref, tiles_ref, picked_ref, next_ref, before_ref, views_ref = refs
    lanes = windows[0].shape[1]
    me = lax.axis_index("wide")
    missing = origin(routes[-1])
    for window, source in zip(windows, [me] + [origin(route) for route in routes[:-1]]):
        slot = lax.rem(source - missing + wide, wide) - 1
        views_ref[:, pl.ds(pl.multiple_of(slot * lanes, lanes), lanes)] = window[...]
    next_ref[...] = views_ref[:, :lanes]
    before_ref[...] = views_ref[:, (wide - 2) * lanes :]
    many = 2 if wide % 2 == 0 else 1
    b1, b2, h = wider(b1_ref, many), wider(b2_ref, 2 * many), wider(h_ref, 2 * many)
    select = select_ref[...]
    picked = jnp.zeros(select.shape, F32)
    for pair in range(0, wide - 2, many):
        previous = views_ref[:, pair * lanes : (pair + many) * lanes]
        current = views_ref[:, (pair + 1) * lanes : (pair + 1 + many) * lanes]
        value = first_and_second_layer(current, previous, groups, firsts, a2_ref, b1, b2, h, own_out)
        for e in range(2):
            for i in range(many):
                tile = value[:, (e * many + i) * lanes : (e * many + i + 1) * lanes]
                tiles_ref[2 * (pair + i) + e] = tile
                view = 2 * lax.rem(missing + 2 + pair + i, wide) + e
                picked = choose(select, view, tile, picked)
    picked_ref[...] = picked


def late_kernel(routes, own_out, groups, *refs):
    wide = len(routes) + 1
    window_ref, next_ref, before_ref, *firsts = refs[: 3 + len(groups)]
    a2_ref, b1_ref, b2_ref, h_ref, select_ref, target_ref, picked_ref, tiles_ref, residual_ref = refs[3 + len(groups) :]
    lanes = window_ref.shape[1]
    missing = origin(routes[-1])
    current = jnp.concatenate([window_ref[...], next_ref[...]], axis=1)
    previous = jnp.concatenate([before_ref[...], window_ref[...]], axis=1)
    b1, b2, h = wider(b1_ref, 2), wider(b2_ref, 4), wider(h_ref, 4)
    value = first_and_second_layer(current, previous, groups, firsts, a2_ref, b1, b2, h, own_out)
    select, picked = select_ref[...], picked_ref[...]
    for e in range(2):
        for i in range(2):
            tile = value[:, (2 * e + i) * lanes : (2 * e + i + 1) * lanes]
            tiles_ref[2 * i + e] = tile
            picked = choose(select, 2 * lax.rem(missing + i, wide) + e, tile, picked)
    residual_ref[...] = (picked - target_ref[...]).astype(BF16)


def adjoint_kernel(routes, shifts, own_out, *refs):
    residuals, refs = refs[: len(shifts)], refs[len(shifts) :]
    turned_ref, early_ref, late_ref, out_ref, predicted_ref = refs
    wide = len(routes) + 1
    missing = origin(routes[-1])
    for pair in range(wide):
        view = lax.rem(missing + pair, wide)
        for e in range(2):
            tile = late_ref[2 * pair + e] if pair < 2 else early_ref[2 * (pair - 2) + e]
            predicted_ref[2 * view + e] = tile[:own_out]
    lanes = residuals[0].shape[1]
    weights = []
    for narrow_shift, pair_shift in shifts:
        narrow, pair = came_from("narrow", narrow_shift), came_from("pair", pair_shift)
        block = narrow * lax.axis_size("pair") + pair
        weights.append(turned_ref[pl.ds(pl.multiple_of(block * lanes, lanes), lanes), :])
    values = jnp.concatenate([ref[...] for ref in residuals], axis=1)
    both = jnp.dot(values, jnp.concatenate(weights, axis=0), preferred_element_type=F32)
    total = both[:, :lanes] + both[:, lanes:]
    for k in range(out_ref.shape[0]):
        out_ref[k] = total[k * own_out : (k + 1) * own_out]


def came_from(axis, distance):
    count = lax.axis_size(axis)
    return lax.rem(lax.axis_index(axis) - distance + count, count)


def send_both(block, narrow_distance, pair_distance):
    narrow, pair = lax.axis_size("narrow"), lax.axis_size("pair")
    route = []
    for i in range(narrow):
        for j in range(pair):
            target = (i + narrow_distance) % narrow * pair + (j + pair_distance) % pair
            route.append((i * pair + j, target))
    return lax.ppermute(block, ("narrow", "pair"), route)


def local(
    low_sino,
    angle_weight,
    angle_bias,
    column_weight,
    column_bias,
    head_weight,
    sparse_views,
    measured,
    row_weights,
):
    wide, narrow, pair = (lax.axis_size(axis) for axis in ("wide", "narrow", "pair"))
    _, channels, width, lanes = low_sino.shape
    own_out = width // wide // 2
    span = 2 * own_out + 2
    size, outs = span * channels, own_out * channels
    sparse_count = measured.shape[0]
    rows = row_weights.shape[1]
    flat = (sparse_count * own_out, lanes)
    shape = jax.ShapeDtypeStruct
    big = 16 if width <= 64 else 48

    small = (
        angle_weight,
        angle_bias[None],
        column_weight,
        column_bias[None],
        head_weight[None],
        measured,
        sparse_views,
    )
    routes = rounds(wide, pair)
    groups = column_groups(channels, span)
    windows = call(
        functools.partial(pack_kernel, routes),
        [shape((size, lanes), BF16)] * wide,
        [pl.BlockSpec(memory_space=pltpu.HBM)],
        [
            pltpu.VMEM((channels, width, lanes), BF16),
            pltpu.VMEM((16 + channels * width, lanes), F32),
            pltpu.SemaphoreType.DMA((4,)),
        ],
        vmem=53.6 if width <= 64 else 48,
    )(low_sino)
    windows = [windows[0]] + [
        lax.ppermute(window, ("wide", "pair"), [(p, t * pair + p % pair) for p, t in enumerate(route)])
        for window, route in zip(windows[1:], routes)
    ]

    widths = sorted({taken for _, taken in groups})
    *firsts, a2, b1, b2, head, select, target = call(
        functools.partial(prepare_kernel, wide, own_out, groups),
        [shape((2 * taken * channels, 2 * taken * channels), BF16) for taken in widths]
        + [
            shape((outs, size), BF16),
            shape((size, lanes), F32),
            shape((outs, lanes), F32),
            shape((outs, lanes), F32),
            shape(flat, F32),
            shape(flat, F32),
        ],
        [VMEM] * 7,
        vmem=big,
    )(*small)
    firsts = [firsts[widths.index(taken)] for _, taken in groups]

    window = shape((size, lanes), BF16)
    early_tiles, picked, following, before = call(
        functools.partial(early_kernel, routes, own_out, groups),
        [shape((2 * wide - 4, 8, lanes), F32), shape(flat, F32), window, window],
        [VMEM] * (wide + len(groups) + 4),
        [pltpu.VMEM((size, (wide - 1) * lanes), BF16)],
        vmem=big,
    )(*windows[:-1], *firsts, a2, b1, b2, head, select)
    late_tiles, residual = call(
        functools.partial(late_kernel, routes, own_out, groups),
        [shape((4, 8, lanes), F32), shape(flat, BF16)],
        [VMEM] * (len(groups) + 10),
        vmem=big,
    )(windows[-1], following, before, *firsts, a2, b1, b2, head, select, target, picked)

    turned = call(turn_kernel, shape((rows, 2 * lanes), BF16), [VMEM] * 2, vmem=big)(row_weights, residual)
    shifts = [(0, t) for t in range(1, pair)] + [(s, 0) for s in range(1, narrow)]
    shifts += [(s, t) for s in range(1, narrow) for t in range(1, pair)]
    blocks = [residual] + [send_both(residual, s, t) for s, t in shifts]
    shifts.insert(0, (0, 0))
    adjoint, predicted = call(
        functools.partial(adjoint_kernel, routes, shifts, own_out),
        [shape((sparse_count, own_out, lanes), F32), shape((2 * wide, own_out, lanes), F32)],
        [VMEM] * (len(blocks) + 3),
        vmem=big,
    )(*blocks, turned, early_tiles, late_tiles)
    return (predicted, adjoint)


def solution(mesh):
    in_specs = (
        P(("parts", "wide"), None, None, ("narrow", "pair")),
        P(),
        P(),
        P(),
        P(),
        P(),
        P(("parts", "narrow"), None),
        P("parts", "wide", ("narrow", "pair")),
        P(("narrow", "pair"), None),
    )
    out_specs = (P("parts", "wide", ("narrow", "pair")), P("parts", "wide", ("narrow", "pair")))
    return jax.shard_map(local, mesh=mesh, in_specs=in_specs, out_specs=out_specs, check_vma=False)
```

```python
import functools

import jax
import jax.numpy as jnp
from jax import lax
from jax.experimental import pallas as pl
from jax.experimental.pallas import tpu as pltpu
from jax.sharding import PartitionSpec as P

F32, BF16 = jnp.float32, jnp.bfloat16
VMEM = pl.BlockSpec(memory_space=pltpu.VMEM)
TAPS = 4


def call(kernel, outs, in_specs, scratch=(), vmem=16, flops=10**6):
    nbytes = sum(o.size * o.dtype.itemsize for o in jax.tree.leaves(outs))
    return pl.pallas_call(
        kernel,
        out_shape=outs,
        in_specs=in_specs,
        out_specs=jax.tree.map(lambda _: VMEM, outs),
        scratch_shapes=list(scratch),
        compiler_params=pltpu.CompilerParams(vmem_limit_bytes=int(vmem * 2**20)),
        cost_estimate=pl.CostEstimate(flops=flops, bytes_accessed=nbytes, transcendentals=0),
    )


def leaky_relu(values):
    return jnp.maximum(values, 0.1 * values)


def split(index, size):
    whole = ((index.astype(F32) + 0.5) * (1.0 / size)).astype(jnp.int32)
    return whole, index - whole * size


def iota(shape, axis):
    return lax.broadcasted_iota(jnp.int32, shape, axis)


def rounds(count, cores):
    if count == 4:
        schedules = [
            [(1, 3, 0, 2), (3, 2, 1, 0), (2, 0, 3, 1)],
            [(2, 3, 1, 0), (3, 2, 0, 1), (1, 0, 3, 2)],
        ]
    else:
        schedules = [[tuple((i + shift) % count for i in range(count)) for shift in range(1, count)]]
    return [
        tuple(schedules[core % len(schedules)][r][i] for i in range(count) for core in range(cores))
        for r in range(count - 1)
    ]


def sources(route, cores):
    back = [0] * len(route)
    for place, target in enumerate(route):
        back[target * cores + place % cores] = place // cores
    return tuple(back)


def entry(table, axes):
    index = lax.axis_index(axes)
    value = jnp.int32(table[0])
    for i in range(1, len(table)):
        value = jnp.where(index == i, jnp.int32(table[i]), value)
    return value


def column_groups(channels, span):
    most = max(1, 256 // (2 * channels) // 2 * 2)
    return [(first, min(most, span - first)) for first in range(0, span, most)]


def pack_kernel(routes, low_ref, *refs):
    windows, (block_ref, rows_ref, sems) = refs[: len(routes) + 1], refs[len(routes) + 1 :]
    _, channels, width, rows = low_ref.shape
    parts = sems.shape[0]
    each = channels // parts
    pieces = []
    for i in range(parts):
        piece = pl.ds(i * each, each)
        pieces.append(pltpu.make_async_copy(low_ref.at[0, piece], block_ref.at[piece], sems.at[i]))
        pieces[-1].start()
    edge = jnp.zeros((8, rows), F32)
    rows_ref[0:8, :] = edge
    rows_ref[8 + channels * width : 16 + channels * width, :] = edge
    for i in range(parts):
        pieces[i].wait()
        values = block_ref[i * each : (i + 1) * each].astype(F32).reshape(each * width, rows)
        rows_ref[8 + i * each * width : 8 + (i + 1) * each * width, :] = values
    own = width // (len(routes) + 1)
    me = lax.axis_index("wide")
    for window, target in zip(windows, [me] + [entry(route, ("wide", "pair")) for route in routes]):
        first = target * own + 7
        columns = [rows_ref[pl.ds(first + i, channels, stride=width), :] for i in range(own + 2)]
        window[...] = jnp.concatenate(columns, axis=0).astype(BF16)


def prepare_kernel(
    wide,
    own_out,
    groups,
    aw_ref,
    ab_ref,
    cw_ref,
    cb_ref,
    hw_ref,
    measured_ref,
    sparse_ref,
    *refs,
):
    firsts, (a2_ref, b1_ref, b2_ref, h_ref, select_ref, target_ref) = refs[:-6], refs[-6:]
    channels = aw_ref.shape[1]
    span = 2 * own_out + 2
    size, outs = span * channels, own_out * channels
    rows, columns = split(iota((size, channels), 0), channels)
    pick = (columns == iota((size, channels), 1)).astype(F32)
    pick16 = pick.astype(BF16)
    out_channel, _ = split(iota((outs, channels), 0), own_out)
    pick_out = (out_channel == iota((outs, channels), 1)).astype(F32)
    pick_out16 = pick_out.astype(BF16)

    def spread(left, weight, right):
        half = lax.dot_general(left, weight, (((1,), (1,)), ((), ())), preferred_element_type=F32)
        return lax.dot_general(half.astype(BF16), right, (((1,), (1,)), ((), ())), preferred_element_type=F32)

    for first_ref in firsts:
        many = first_ref.shape[0] // 2
        taken = many // channels
        which, channel = split(iota((2 * many, channels), 0), channels)
        is_channel = channel == iota((2 * many, channels), 1)
        sides = [is_channel & (which >= side * taken) & (which < (side + 1) * taken) for side in range(2)]
        sides = [side.astype(F32).astype(BF16) for side in sides]
        row_column = split(iota((many, 2 * many), 0), channels)[0]
        column_column = split(iota((many, 2 * many), 1), channels)[0]
        same = (row_column == column_column) | (row_column + taken == column_column)
        for e in range(2):
            full = spread(pick16[:many], aw_ref[e], sides[0]) + spread(pick16[:many], aw_ref[e + 2], sides[1])
            first_ref[e * many : (e + 1) * many, :] = jnp.where(same, full, 0.0).astype(BF16)

    in_column = split(iota((outs, size), 1), channels)[0]
    out_column = split(iota((outs, size), 0), own_out)[1]
    me = lax.axis_index("wide")
    absolute = in_column + me * (2 * own_out) - 1
    inside = (absolute >= 0) & (absolute < 2 * own_out * wide)
    total = jnp.zeros((outs, size), F32)
    for tap in range(TAPS):
        here = (in_column == 2 * out_column + tap) & inside
        total = jnp.where(here, spread(pick_out16, cw_ref[tap], pick16), total)
    a2_ref[...] = total.astype(BF16)

    def along(left, vector_ref, out_ref):
        summed = jnp.sum(left * vector_ref[...].astype(F32), axis=1, keepdims=True)
        out_ref[...] = jnp.broadcast_to(summed, out_ref.shape)

    along(pick, ab_ref, b1_ref)
    along(pick_out, cb_ref, b2_ref)
    along(pick_out, hw_ref, h_ref)

    sparse_count = measured_ref.shape[0]
    wanted = (select_ref.shape[0], sparse_count)
    pick_view = (split(iota(wanted, 0), own_out)[0] == iota(wanted, 1)).astype(F32)
    along(pick_view, sparse_ref, select_ref)
    for k in range(sparse_count):
        target_ref[k * own_out : (k + 1) * own_out, :] = measured_ref[k]


def turn_kernel(rw_ref, _, turned_ref):
    turned = rw_ref[...].T
    high = turned.astype(BF16)
    turned_ref[:, : high.shape[1]] = high
    turned_ref[:, high.shape[1] :] = (turned - high.astype(F32)).astype(BF16)


def origin(route):
    return entry(sources(route, lax.axis_size("pair")), ("wide", "pair"))


def first_and_second_layer(current, previous, groups, firsts, a2_ref, b1, b2, h, own_out):
    outs = a2_ref.shape[0]
    channels = outs // own_out
    lanes = current.shape[1]
    summed = {}
    for width in sorted({taken for _, taken in groups}, reverse=True):
        alike = [i for i, (_, taken) in enumerate(groups) if taken == width]
        stacks = []
        for i in alike:
            rows = slice(groups[i][0] * channels, (groups[i][0] + width) * channels)
            stacks.append(jnp.concatenate([current[rows], previous[rows]], axis=0))
        wide_sum = jnp.dot(firsts[alike[0]][...], jnp.concatenate(stacks, axis=1), preferred_element_type=F32)
        for place, i in enumerate(alike):
            summed[i] = wide_sum[:, place * lanes : (place + 1) * lanes]
    pieces = ([], [])
    for i, (first, taken) in enumerate(groups):
        half = taken * channels
        for e in range(2):
            bias = b1[first * channels : (first + taken) * channels]
            pieces[e].append(leaky_relu(summed[i][e * half : (e + 1) * half] + bias).astype(BF16))
    both = jnp.concatenate([jnp.concatenate(piece, axis=0) for piece in pieces], axis=1)
    hidden = leaky_relu(jnp.dot(a2_ref[...], both, preferred_element_type=F32) + b2) * h
    value = jnp.sum(hidden.reshape(outs // 8, 8, hidden.shape[1]), axis=0)
    apart = own_out
    while apart < 8:
        value += pltpu.roll(value, apart, 0)
        apart *= 2
    return value


def wider(ref, times):
    return jnp.concatenate([ref[...]] * times, axis=1)


def choose(select, view, tile, picked):
    repeated = jnp.concatenate([tile] * (select.shape[0] // 8), axis=0)
    return jnp.where(select == view.astype(F32), repeated, picked)


def early_kernel(routes, own_out, groups, *refs):
    wide = len(routes) + 1
    windows, firsts, refs = refs[: wide - 1], refs[wide - 1 : wide - 1 + len(groups)], refs[wide - 1 + len(groups) :]
    a2_ref, b1_ref, b2_ref, h_ref, select_ref, tiles_ref, picked_ref, next_ref, before_ref, views_ref = refs
    lanes = windows[0].shape[1]
    me = lax.axis_index("wide")
    missing = origin(routes[-1])
    for window, source in zip(windows, [me] + [origin(route) for route in routes[:-1]]):
        slot = lax.rem(source - missing + wide, wide) - 1
        views_ref[:, pl.ds(pl.multiple_of(slot * lanes, lanes), lanes)] = window[...]
    next_ref[...] = views_ref[:, :lanes]
    before_ref[...] = views_ref[:, (wide - 2) * lanes :]
    many = 2 if wide % 2 == 0 else 1
    b1, b2, h = wider(b1_ref, many), wider(b2_ref, 2 * many), wider(h_ref, 2 * many)
    select = select_ref[...]
    picked = jnp.zeros(select.shape, F32)
    for pair in range(0, wide - 2, many):
        previous = views_ref[:, pair * lanes : (pair + many) * lanes]
        current = views_ref[:, (pair + 1) * lanes : (pair + 1 + many) * lanes]
        value = first_and_second_layer(current, previous, groups, firsts, a2_ref, b1, b2, h, own_out)
        for e in range(2):
            for i in range(many):
                tile = value[:, (e * many + i) * lanes : (e * many + i + 1) * lanes]
                tiles_ref[2 * (pair + i) + e] = tile
                view = 2 * lax.rem(missing + 2 + pair + i, wide) + e
                picked = choose(select, view, tile, picked)
    picked_ref[...] = picked


def late_kernel(routes, own_out, groups, *refs):
    wide = len(routes) + 1
    window_ref, next_ref, before_ref, *firsts = refs[: 3 + len(groups)]
    a2_ref, b1_ref, b2_ref, h_ref, select_ref, target_ref, picked_ref, tiles_ref, residual_ref = refs[3 + len(groups) :]
    lanes = window_ref.shape[1]
    missing = origin(routes[-1])
    current = jnp.concatenate([window_ref[...], next_ref[...]], axis=1)
    previous = jnp.concatenate([before_ref[...], window_ref[...]], axis=1)
    b1, b2, h = wider(b1_ref, 2), wider(b2_ref, 4), wider(h_ref, 4)
    value = first_and_second_layer(current, previous, groups, firsts, a2_ref, b1, b2, h, own_out)
    select, picked = select_ref[...], picked_ref[...]
    for e in range(2):
        for i in range(2):
            tile = value[:, (2 * e + i) * lanes : (2 * e + i + 1) * lanes]
            tiles_ref[2 * i + e] = tile
            picked = choose(select, 2 * lax.rem(missing + i, wide) + e, tile, picked)
    residual_ref[...] = (picked - target_ref[...]).astype(BF16)


def adjoint_kernel(routes, shifts, own_out, *refs):
    residuals, refs = refs[: len(shifts)], refs[len(shifts) :]
    turned_ref, early_ref, late_ref, out_ref, predicted_ref = refs
    wide = len(routes) + 1
    missing = origin(routes[-1])
    for pair in range(wide):
        view = lax.rem(missing + pair, wide)
        for e in range(2):
            tile = late_ref[2 * pair + e] if pair < 2 else early_ref[2 * (pair - 2) + e]
            predicted_ref[2 * view + e] = tile[:own_out]
    lanes = residuals[0].shape[1]
    weights = []
    for narrow_shift, pair_shift in shifts:
        narrow, pair = came_from("narrow", narrow_shift), came_from("pair", pair_shift)
        block = narrow * lax.axis_size("pair") + pair
        weights.append(turned_ref[pl.ds(pl.multiple_of(block * lanes, lanes), lanes), :])
    values = jnp.concatenate([ref[...] for ref in residuals], axis=1)
    both = jnp.dot(values, jnp.concatenate(weights, axis=0), preferred_element_type=F32)
    total = both[:, :lanes] + both[:, lanes:]
    for k in range(out_ref.shape[0]):
        out_ref[k] = total[k * own_out : (k + 1) * own_out]


def came_from(axis, distance):
    count = lax.axis_size(axis)
    return lax.rem(lax.axis_index(axis) - distance + count, count)


def send_both(block, narrow_distance, pair_distance):
    narrow, pair = lax.axis_size("narrow"), lax.axis_size("pair")
    route = []
    for i in range(narrow):
        for j in range(pair):
            target = (i + narrow_distance) % narrow * pair + (j + pair_distance) % pair
            route.append((i * pair + j, target))
    return lax.ppermute(block, ("narrow", "pair"), route)


def local(
    low_sino,
    angle_weight,
    angle_bias,
    column_weight,
    column_bias,
    head_weight,
    sparse_views,
    measured,
    row_weights,
):
    wide, narrow, pair = (lax.axis_size(axis) for axis in ("wide", "narrow", "pair"))
    _, channels, width, lanes = low_sino.shape
    own_out = width // wide // 2
    span = 2 * own_out + 2
    size, outs = span * channels, own_out * channels
    sparse_count = measured.shape[0]
    rows = row_weights.shape[1]
    flat = (sparse_count * own_out, lanes)
    shape = jax.ShapeDtypeStruct
    big = 16 if width <= 64 else 48

    small = (
        angle_weight,
        angle_bias[None],
        column_weight,
        column_bias[None],
        head_weight[None],
        measured,
        sparse_views,
    )
    routes = rounds(wide, pair)
    groups = column_groups(channels, span)
    windows = call(
        functools.partial(pack_kernel, routes),
        [shape((size, lanes), BF16)] * wide,
        [pl.BlockSpec(memory_space=pltpu.HBM)],
        [
            pltpu.VMEM((channels, width, lanes), BF16),
            pltpu.VMEM((16 + channels * width, lanes), F32),
            pltpu.SemaphoreType.DMA((4,)),
        ],
        vmem=53.6 if width <= 64 else 48,
    )(low_sino)
    windows = [windows[0]] + [
        lax.ppermute(window, ("wide", "pair"), [(p, t * pair + p % pair) for p, t in enumerate(route)])
        for window, route in zip(windows[1:], routes)
    ]

    widths = sorted({taken for _, taken in groups})
    *firsts, a2, b1, b2, head, select, target = call(
        functools.partial(prepare_kernel, wide, own_out, groups),
        [shape((2 * taken * channels, 2 * taken * channels), BF16) for taken in widths]
        + [
            shape((outs, size), BF16),
            shape((size, lanes), F32),
            shape((outs, lanes), F32),
            shape((outs, lanes), F32),
            shape(flat, F32),
            shape(flat, F32),
        ],
        [VMEM] * 7,
        vmem=big,
    )(*small)
    firsts = [firsts[widths.index(taken)] for _, taken in groups]

    window = shape((size, lanes), BF16)
    early_tiles, picked, following, before = call(
        functools.partial(early_kernel, routes, own_out, groups),
        [shape((2 * wide - 4, 8, lanes), F32), shape(flat, F32), window, window],
        [VMEM] * (wide + len(groups) + 4),
        [pltpu.VMEM((size, (wide - 1) * lanes), BF16)],
        vmem=big,
    )(*windows[:-1], *firsts, a2, b1, b2, head, select)
    late_tiles, residual = call(
        functools.partial(late_kernel, routes, own_out, groups),
        [shape((4, 8, lanes), F32), shape(flat, BF16)],
        [VMEM] * (len(groups) + 10),
        vmem=big,
    )(windows[-1], following, before, *firsts, a2, b1, b2, head, select, target, picked)

    turned = call(turn_kernel, shape((rows, 2 * lanes), BF16), [VMEM] * 2, vmem=big)(row_weights, residual)
    shifts = [(0, t) for t in range(1, pair)] + [(s, 0) for s in range(1, narrow)]
    shifts += [(s, t) for s in range(1, narrow) for t in range(1, pair)]
    blocks = [residual] + [send_both(residual, s, t) for s, t in shifts]
    shifts.insert(0, (0, 0))
    adjoint, predicted = call(
        functools.partial(adjoint_kernel, routes, shifts, own_out),
        [shape((sparse_count, own_out, lanes), F32), shape((2 * wide, own_out, lanes), F32)],
        [VMEM] * (len(blocks) + 3),
        vmem=big,
    )(*blocks, turned, early_tiles, late_tiles)
    return (predicted, adjoint)


def solution(mesh):
    in_specs = (
        P(("parts", "wide"), None, None, ("narrow", "pair")),
        P(),
        P(),
        P(),
        P(),
        P(),
        P(("parts", "narrow"), None),
        P("parts", "wide", ("narrow", "pair")),
        P(("narrow", "pair"), None),
    )
    out_specs = (P("parts", "wide", ("narrow", "pair")), P("parts", "wide", ("narrow", "pair")))
    return jax.shard_map(local, mesh=mesh, in_specs=in_specs, out_specs=out_specs, check_vma=False)
```

```python
import functools

import jax
import jax.numpy as jnp
from jax import lax
from jax.experimental import pallas as pl
from jax.experimental.pallas import tpu as pltpu
from jax.sharding import PartitionSpec as P

F32, BF16 = jnp.float32, jnp.bfloat16
VMEM = pl.BlockSpec(memory_space=pltpu.VMEM)
TAPS = 4


def call(kernel, outs, in_specs, scratch=(), vmem=16, flops=10**6):
    nbytes = sum(o.size * o.dtype.itemsize for o in jax.tree.leaves(outs))
    return pl.pallas_call(
        kernel,
        out_shape=outs,
        in_specs=in_specs,
        out_specs=jax.tree.map(lambda _: VMEM, outs),
        scratch_shapes=list(scratch),
        compiler_params=pltpu.CompilerParams(vmem_limit_bytes=int(vmem * 2**20)),
        cost_estimate=pl.CostEstimate(flops=flops, bytes_accessed=nbytes, transcendentals=0),
    )


def leaky_relu(values):
    return jnp.maximum(values, 0.1 * values)


def split(index, size):
    whole = ((index.astype(F32) + 0.5) * (1.0 / size)).astype(jnp.int32)
    return whole, index - whole * size


def iota(shape, axis):
    return lax.broadcasted_iota(jnp.int32, shape, axis)


def rounds(count, cores):
    if count == 4:
        schedules = [
            [(1, 3, 0, 2), (3, 2, 1, 0), (2, 0, 3, 1)],
            [(2, 3, 1, 0), (3, 2, 0, 1), (1, 0, 3, 2)],
        ]
    else:
        schedules = [[tuple((i + shift) % count for i in range(count)) for shift in range(1, count)]]
    return [
        tuple(schedules[core % len(schedules)][r][i] for i in range(count) for core in range(cores))
        for r in range(count - 1)
    ]


def sources(route, cores):
    back = [0] * len(route)
    for place, target in enumerate(route):
        back[target * cores + place % cores] = place // cores
    return tuple(back)


def entry(table, axes):
    index = lax.axis_index(axes)
    value = jnp.int32(table[0])
    for i in range(1, len(table)):
        value = jnp.where(index == i, jnp.int32(table[i]), value)
    return value


def column_groups(channels, span):
    most = max(1, 256 // (2 * channels) // 2 * 2)
    return [(first, min(most, span - first)) for first in range(0, span, most)]


def pack_kernel(routes, low_ref, *refs):
    windows, (block_ref, rows_ref, sems) = refs[: len(routes) + 1], refs[len(routes) + 1 :]
    _, channels, width, rows = low_ref.shape
    parts = sems.shape[0]
    each = channels // parts
    pieces = []
    for i in range(parts):
        piece = pl.ds(i * each, each)
        pieces.append(pltpu.make_async_copy(low_ref.at[0, piece], block_ref.at[piece], sems.at[i]))
        pieces[-1].start()
    edge = jnp.zeros((8, rows), F32)
    rows_ref[0:8, :] = edge
    rows_ref[8 + channels * width : 16 + channels * width, :] = edge
    for i in range(parts):
        pieces[i].wait()
        values = block_ref[i * each : (i + 1) * each].astype(F32).reshape(each * width, rows)
        rows_ref[8 + i * each * width : 8 + (i + 1) * each * width, :] = values
    own = width // (len(routes) + 1)
    me = lax.axis_index("wide")
    for window, target in zip(windows, [me] + [entry(route, ("wide", "pair")) for route in routes]):
        first = target * own + 7
        columns = [rows_ref[pl.ds(first + i, channels, stride=width), :] for i in range(own + 2)]
        window[...] = jnp.concatenate(columns, axis=0).astype(BF16)


def prepare_kernel(
    wide,
    own_out,
    groups,
    aw_ref,
    ab_ref,
    cw_ref,
    cb_ref,
    hw_ref,
    measured_ref,
    sparse_ref,
    *refs,
):
    firsts, (a2_ref, b1_ref, b2_ref, h_ref, select_ref, target_ref) = refs[:-6], refs[-6:]
    channels = aw_ref.shape[1]
    span = 2 * own_out + 2
    size, outs = span * channels, own_out * channels
    rows, columns = split(iota((size, channels), 0), channels)
    pick = (columns == iota((size, channels), 1)).astype(F32)
    pick16 = pick.astype(BF16)
    out_channel, _ = split(iota((outs, channels), 0), own_out)
    pick_out = (out_channel == iota((outs, channels), 1)).astype(F32)
    pick_out16 = pick_out.astype(BF16)

    def spread(left, weight, right):
        half = lax.dot_general(left, weight, (((1,), (1,)), ((), ())), preferred_element_type=F32)
        return lax.dot_general(half.astype(BF16), right, (((1,), (1,)), ((), ())), preferred_element_type=F32)

    for first_ref in firsts:
        many = first_ref.shape[0] // 2
        taken = many // channels
        which, channel = split(iota((2 * many, channels), 0), channels)
        is_channel = channel == iota((2 * many, channels), 1)
        sides = [is_channel & (which >= side * taken) & (which < (side + 1) * taken) for side in range(2)]
        sides = [side.astype(F32).astype(BF16) for side in sides]
        row_column = split(iota((many, 2 * many), 0), channels)[0]
        column_column = split(iota((many, 2 * many), 1), channels)[0]
        same = (row_column == column_column) | (row_column + taken == column_column)
        for e in range(2):
            full = spread(pick16[:many], aw_ref[e], sides[0]) + spread(pick16[:many], aw_ref[e + 2], sides[1])
            first_ref[e * many : (e + 1) * many, :] = jnp.where(same, full, 0.0).astype(BF16)

    in_column = split(iota((outs, size), 1), channels)[0]
    out_column = split(iota((outs, size), 0), own_out)[1]
    me = lax.axis_index("wide")
    absolute = in_column + me * (2 * own_out) - 1
    inside = (absolute >= 0) & (absolute < 2 * own_out * wide)
    total = jnp.zeros((outs, size), F32)
    for tap in range(TAPS):
        here = (in_column == 2 * out_column + tap) & inside
        total = jnp.where(here, spread(pick_out16, cw_ref[tap], pick16), total)
    a2_ref[...] = total.astype(BF16)

    def along(left, vector_ref, out_ref):
        summed = jnp.sum(left * vector_ref[...].astype(F32), axis=1, keepdims=True)
        out_ref[...] = jnp.broadcast_to(summed, out_ref.shape)

    along(pick, ab_ref, b1_ref)
    along(pick_out, cb_ref, b2_ref)
    along(pick_out, hw_ref, h_ref)

    sparse_count = measured_ref.shape[0]
    wanted = (select_ref.shape[0], sparse_count)
    pick_view = (split(iota(wanted, 0), own_out)[0] == iota(wanted, 1)).astype(F32)
    along(pick_view, sparse_ref, select_ref)
    for k in range(sparse_count):
        target_ref[k * own_out : (k + 1) * own_out, :] = measured_ref[k]


def turn_kernel(rw_ref, _, turned_ref):
    turned = rw_ref[...].T
    high = turned.astype(BF16)
    turned_ref[:, : high.shape[1]] = high
    turned_ref[:, high.shape[1] :] = (turned - high.astype(F32)).astype(BF16)


def origin(route):
    return entry(sources(route, lax.axis_size("pair")), ("wide", "pair"))


def first_and_second_layer(current, previous, groups, firsts, a2_ref, b1, b2, h, own_out):
    outs = a2_ref.shape[0]
    channels = outs // own_out
    pieces = ([], [])
    for (first, taken), first_ref in zip(groups, firsts):
        rows = slice(first * channels, (first + taken) * channels)
        half = taken * channels
        stacked = jnp.concatenate([current[rows], previous[rows]], axis=0)
        summed = jnp.dot(first_ref[...], stacked, preferred_element_type=F32)
        for e in range(2):
            pieces[e].append(leaky_relu(summed[e * half : (e + 1) * half] + b1[rows]).astype(BF16))
    both = jnp.concatenate([jnp.concatenate(piece, axis=0) for piece in pieces], axis=1)
    hidden = leaky_relu(jnp.dot(a2_ref[...], both, preferred_element_type=F32) + b2) * h
    value = jnp.sum(hidden.reshape(outs // 8, 8, hidden.shape[1]), axis=0)
    apart = own_out
    while apart < 8:
        value += pltpu.roll(value, apart, 0)
        apart *= 2
    return value


def wider(ref, times):
    return jnp.concatenate([ref[...]] * times, axis=1)


def choose(select, view, tile, picked):
    repeated = jnp.concatenate([tile] * (select.shape[0] // 8), axis=0)
    return jnp.where(select == view.astype(F32), repeated, picked)


def early_kernel(routes, own_out, groups, *refs):
    wide = len(routes) + 1
    windows, firsts, refs = refs[: wide - 1], refs[wide - 1 : wide - 1 + len(groups)], refs[wide - 1 + len(groups) :]
    a2_ref, b1_ref, b2_ref, h_ref, select_ref, tiles_ref, picked_ref, next_ref, before_ref, views_ref = refs
    lanes = windows[0].shape[1]
    me = lax.axis_index("wide")
    missing = origin(routes[-1])
    for window, source in zip(windows, [me] + [origin(route) for route in routes[:-1]]):
        slot = lax.rem(source - missing + wide, wide) - 1
        views_ref[:, pl.ds(pl.multiple_of(slot * lanes, lanes), lanes)] = window[...]
    next_ref[...] = views_ref[:, :lanes]
    before_ref[...] = views_ref[:, (wide - 2) * lanes :]
    many = 2 if wide % 2 == 0 else 1
    b1, b2, h = wider(b1_ref, many), wider(b2_ref, 2 * many), wider(h_ref, 2 * many)
    select = select_ref[...]
    picked = jnp.zeros(select.shape, F32)
    for pair in range(0, wide - 2, many):
        previous = views_ref[:, pair * lanes : (pair + many) * lanes]
        current = views_ref[:, (pair + 1) * lanes : (pair + 1 + many) * lanes]
        value = first_and_second_layer(current, previous, groups, firsts, a2_ref, b1, b2, h, own_out)
        for e in range(2):
            for i in range(many):
                tile = value[:, (e * many + i) * lanes : (e * many + i + 1) * lanes]
                tiles_ref[2 * (pair + i) + e] = tile
                view = 2 * lax.rem(missing + 2 + pair + i, wide) + e
                picked = choose(select, view, tile, picked)
    picked_ref[...] = picked


def late_kernel(routes, own_out, groups, *refs):
    wide = len(routes) + 1
    window_ref, next_ref, before_ref, *firsts = refs[: 3 + len(groups)]
    a2_ref, b1_ref, b2_ref, h_ref, select_ref, target_ref, picked_ref, tiles_ref, residual_ref = refs[3 + len(groups) :]
    lanes = window_ref.shape[1]
    missing = origin(routes[-1])
    current = jnp.concatenate([window_ref[...], next_ref[...]], axis=1)
    previous = jnp.concatenate([before_ref[...], window_ref[...]], axis=1)
    b1, b2, h = wider(b1_ref, 2), wider(b2_ref, 4), wider(h_ref, 4)
    value = first_and_second_layer(current, previous, groups, firsts, a2_ref, b1, b2, h, own_out)
    select, picked = select_ref[...], picked_ref[...]
    for e in range(2):
        for i in range(2):
            tile = value[:, (2 * e + i) * lanes : (2 * e + i + 1) * lanes]
            tiles_ref[2 * i + e] = tile
            picked = choose(select, 2 * lax.rem(missing + i, wide) + e, tile, picked)
    residual_ref[...] = (picked - target_ref[...]).astype(BF16)


def adjoint_kernel(routes, shifts, own_out, *refs):
    residuals, refs = refs[: len(shifts)], refs[len(shifts) :]
    turned_ref, early_ref, late_ref, out_ref, predicted_ref = refs
    wide = len(routes) + 1
    missing = origin(routes[-1])
    for pair in range(wide):
        view = lax.rem(missing + pair, wide)
        for e in range(2):
            tile = late_ref[2 * pair + e] if pair < 2 else early_ref[2 * (pair - 2) + e]
            predicted_ref[2 * view + e] = tile[:own_out]
    lanes = residuals[0].shape[1]
    weights = []
    for narrow_shift, pair_shift in shifts:
        narrow, pair = came_from("narrow", narrow_shift), came_from("pair", pair_shift)
        block = narrow * lax.axis_size("pair") + pair
        weights.append(turned_ref[pl.ds(pl.multiple_of(block * lanes, lanes), lanes), :])
    values = jnp.concatenate([ref[...] for ref in residuals], axis=1)
    both = jnp.dot(values, jnp.concatenate(weights, axis=0), preferred_element_type=F32)
    total = both[:, :lanes] + both[:, lanes:]
    for k in range(out_ref.shape[0]):
        out_ref[k] = total[k * own_out : (k + 1) * own_out]


def came_from(axis, distance):
    count = lax.axis_size(axis)
    return lax.rem(lax.axis_index(axis) - distance + count, count)


def send_both(block, narrow_distance, pair_distance):
    narrow, pair = lax.axis_size("narrow"), lax.axis_size("pair")
    route = []
    for i in range(narrow):
        for j in range(pair):
            target = (i + narrow_distance) % narrow * pair + (j + pair_distance) % pair
            route.append((i * pair + j, target))
    return lax.ppermute(block, ("narrow", "pair"), route)


def local(
    low_sino,
    angle_weight,
    angle_bias,
    column_weight,
    column_bias,
    head_weight,
    sparse_views,
    measured,
    row_weights,
):
    wide, narrow, pair = (lax.axis_size(axis) for axis in ("wide", "narrow", "pair"))
    _, channels, width, lanes = low_sino.shape
    own_out = width // wide // 2
    span = 2 * own_out + 2
    size, outs = span * channels, own_out * channels
    sparse_count = measured.shape[0]
    rows = row_weights.shape[1]
    flat = (sparse_count * own_out, lanes)
    shape = jax.ShapeDtypeStruct
    big = 16 if width <= 64 else 48

    small = (
        angle_weight,
        angle_bias[None],
        column_weight,
        column_bias[None],
        head_weight[None],
        measured,
        sparse_views,
    )
    routes = rounds(wide, pair)
    groups = column_groups(channels, span)
    windows = call(
        functools.partial(pack_kernel, routes),
        [shape((size, lanes), BF16)] * wide,
        [pl.BlockSpec(memory_space=pltpu.HBM)],
        [
            pltpu.VMEM((channels, width, lanes), BF16),
            pltpu.VMEM((16 + (channels + 1) * width, lanes), F32),
            pltpu.SemaphoreType.DMA((4,)),
        ],
        vmem=53.6 if width <= 64 else 48,
    )(low_sino)
    windows = [windows[0]] + [
        lax.ppermute(window, ("wide", "pair"), [(p, t * pair + p % pair) for p, t in enumerate(route)])
        for window, route in zip(windows[1:], routes)
    ]

    widths = sorted({taken for _, taken in groups})
    *firsts, a2, b1, b2, head, select, target = call(
        functools.partial(prepare_kernel, wide, own_out, groups),
        [shape((2 * taken * channels, 2 * taken * channels), BF16) for taken in widths]
        + [
            shape((outs, size), BF16),
            shape((size, lanes), F32),
            shape((outs, lanes), F32),
            shape((outs, lanes), F32),
            shape(flat, F32),
            shape(flat, F32),
        ],
        [VMEM] * 7,
        vmem=big,
    )(*small)
    firsts = [firsts[widths.index(taken)] for _, taken in groups]

    window = shape((size, lanes), BF16)
    early_tiles, picked, following, before = call(
        functools.partial(early_kernel, routes, own_out, groups),
        [shape((2 * wide - 4, 8, lanes), F32), shape(flat, F32), window, window],
        [VMEM] * (wide + len(groups) + 4),
        [pltpu.VMEM((size, (wide - 1) * lanes), BF16)],
        vmem=big,
    )(*windows[:-1], *firsts, a2, b1, b2, head, select)
    late_tiles, residual = call(
        functools.partial(late_kernel, routes, own_out, groups),
        [shape((4, 8, lanes), F32), shape(flat, BF16)],
        [VMEM] * (len(groups) + 10),
        vmem=big,
    )(windows[-1], following, before, *firsts, a2, b1, b2, head, select, target, picked)

    turned = call(turn_kernel, shape((rows, 2 * lanes), BF16), [VMEM] * 2, vmem=big)(row_weights, residual)
    shifts = [(0, t) for t in range(1, pair)] + [(s, 0) for s in range(1, narrow)]
    shifts += [(s, t) for s in range(1, narrow) for t in range(1, pair)]
    blocks = [residual] + [send_both(residual, s, t) for s, t in shifts]
    shifts.insert(0, (0, 0))
    adjoint, predicted = call(
        functools.partial(adjoint_kernel, routes, shifts, own_out),
        [shape((sparse_count, own_out, lanes), F32), shape((2 * wide, own_out, lanes), F32)],
        [VMEM] * (len(blocks) + 3),
        vmem=big,
    )(*blocks, turned, early_tiles, late_tiles)
    return (predicted, adjoint)


def solution(mesh):
    in_specs = (
        P(("parts", "wide"), None, None, ("narrow", "pair")),
        P(),
        P(),
        P(),
        P(),
        P(),
        P(("parts", "narrow"), None),
        P("parts", "wide", ("narrow", "pair")),
        P(("narrow", "pair"), None),
    )
    out_specs = (P("parts", "wide", ("narrow", "pair")), P("parts", "wide", ("narrow", "pair")))
    return jax.shard_map(local, mesh=mesh, in_specs=in_specs, out_specs=out_specs, check_vma=False)
```

```python
import functools

import jax
import jax.numpy as jnp
from jax import lax
from jax.experimental import pallas as pl
from jax.experimental.pallas import tpu as pltpu
from jax.sharding import PartitionSpec as P

F32, BF16 = jnp.float32, jnp.bfloat16
VMEM = pl.BlockSpec(memory_space=pltpu.VMEM)
TAPS = 4


def call(kernel, outs, in_specs, scratch=(), vmem=16, flops=10**6):
    nbytes = sum(o.size * o.dtype.itemsize for o in jax.tree.leaves(outs))
    return pl.pallas_call(
        kernel,
        out_shape=outs,
        in_specs=in_specs,
        out_specs=jax.tree.map(lambda _: VMEM, outs),
        scratch_shapes=list(scratch),
        compiler_params=pltpu.CompilerParams(vmem_limit_bytes=int(vmem * 2**20)),
        cost_estimate=pl.CostEstimate(flops=flops, bytes_accessed=nbytes, transcendentals=0),
    )


def leaky_relu(values):
    return jnp.maximum(values, 0.1 * values)


def split(index, size):
    whole = ((index.astype(F32) + 0.5) * (1.0 / size)).astype(jnp.int32)
    return whole, index - whole * size


def iota(shape, axis):
    return lax.broadcasted_iota(jnp.int32, shape, axis)


def rounds(count, cores):
    if count == 4:
        schedules = [
            [(1, 3, 0, 2), (3, 2, 1, 0), (2, 0, 3, 1)],
            [(2, 3, 1, 0), (3, 2, 0, 1), (1, 0, 3, 2)],
        ]
    else:
        schedules = [[tuple((i + shift) % count for i in range(count)) for shift in range(1, count)]]
    return [
        tuple(schedules[core % len(schedules)][r][i] for i in range(count) for core in range(cores))
        for r in range(count - 1)
    ]


def sources(route, cores):
    back = [0] * len(route)
    for place, target in enumerate(route):
        back[target * cores + place % cores] = place // cores
    return tuple(back)


def entry(table, axes):
    index = lax.axis_index(axes)
    value = jnp.int32(table[0])
    for i in range(1, len(table)):
        value = jnp.where(index == i, jnp.int32(table[i]), value)
    return value


def column_groups(channels, span):
    most = max(1, 256 // (2 * channels) // 2 * 2)
    return [(first, min(most, span - first)) for first in range(0, span, most)]


def pack_kernel(routes, low_ref, *refs):
    windows, (block_ref, rows_ref, sems) = refs[: len(routes) + 1], refs[len(routes) + 1 :]
    _, channels, width, rows = low_ref.shape
    parts = sems.shape[0]
    each = channels // parts
    pieces = []
    for i in range(parts):
        piece = pl.ds(i * each, each)
        pieces.append(pltpu.make_async_copy(low_ref.at[0, piece], block_ref.at[piece], sems.at[i]))
        pieces[-1].start()
    edge = jnp.zeros((8, rows), F32)
    rows_ref[0:8, :] = edge
    rows_ref[8 + channels * width : 16 + channels * width, :] = edge
    for i in range(parts):
        pieces[i].wait()
        values = block_ref[i * each : (i + 1) * each].astype(F32).reshape(each * width, rows)
        rows_ref[8 + i * each * width : 8 + (i + 1) * each * width, :] = values
    own = width // (len(routes) + 1)
    me = lax.axis_index("wide")
    for window, target in zip(windows, [me] + [entry(route, ("wide", "pair")) for route in routes]):
        first = target * own + 7
        columns = [rows_ref[pl.ds(first + i, channels, stride=width), :] for i in range(own + 2)]
        window[...] = jnp.concatenate(columns, axis=0).astype(BF16)


def prepare_kernel(
    wide,
    own_out,
    groups,
    aw_ref,
    ab_ref,
    cw_ref,
    cb_ref,
    hw_ref,
    measured_ref,
    sparse_ref,
    *refs,
):
    firsts, (a2_ref, b1_ref, b2_ref, h_ref, select_ref, target_ref) = refs[:-6], refs[-6:]
    channels = aw_ref.shape[1]
    span = 2 * own_out + 2
    size, outs = span * channels, own_out * channels
    rows, columns = split(iota((size, channels), 0), channels)
    pick = (columns == iota((size, channels), 1)).astype(F32)
    pick16 = pick.astype(BF16)
    out_channel, _ = split(iota((outs, channels), 0), own_out)
    pick_out = (out_channel == iota((outs, channels), 1)).astype(F32)
    pick_out16 = pick_out.astype(BF16)

    def spread(left, weight, right):
        half = lax.dot_general(left, weight, (((1,), (1,)), ((), ())), preferred_element_type=F32)
        return lax.dot_general(half.astype(BF16), right, (((1,), (1,)), ((), ())), preferred_element_type=F32)

    for first_ref in firsts:
        many = first_ref.shape[0] // 2
        taken = many // channels
        which, channel = split(iota((2 * many, channels), 0), channels)
        is_channel = channel == iota((2 * many, channels), 1)
        sides = [is_channel & (which >= side * taken) & (which < (side + 1) * taken) for side in range(2)]
        sides = [side.astype(F32).astype(BF16) for side in sides]
        row_column = split(iota((many, 2 * many), 0), channels)[0]
        column_column = split(iota((many, 2 * many), 1), channels)[0]
        same = (row_column == column_column) | (row_column + taken == column_column)
        for e in range(2):
            full = spread(pick16[:many], aw_ref[e], sides[0]) + spread(pick16[:many], aw_ref[e + 2], sides[1])
            first_ref[e * many : (e + 1) * many, :] = jnp.where(same, full, 0.0).astype(BF16)

    in_column = split(iota((outs, size), 1), channels)[0]
    out_column = split(iota((outs, size), 0), own_out)[1]
    me = lax.axis_index("wide")
    absolute = in_column + me * (2 * own_out) - 1
    inside = (absolute >= 0) & (absolute < 2 * own_out * wide)
    total = jnp.zeros((outs, size), F32)
    for tap in range(TAPS):
        here = (in_column == 2 * out_column + tap) & inside
        total = jnp.where(here, spread(pick_out16, cw_ref[tap], pick16), total)
    a2_ref[...] = total.astype(BF16)

    def along(left, vector_ref, out_ref):
        summed = jnp.sum(left * vector_ref[...].astype(F32), axis=1, keepdims=True)
        out_ref[...] = jnp.broadcast_to(summed, out_ref.shape)

    along(pick, ab_ref, b1_ref)
    along(pick_out, cb_ref, b2_ref)
    along(pick_out, hw_ref, h_ref)

    sparse_count = measured_ref.shape[0]
    wanted = (select_ref.shape[0], sparse_count)
    pick_view = (split(iota(wanted, 0), own_out)[0] == iota(wanted, 1)).astype(F32)
    along(pick_view, sparse_ref, select_ref)
    for k in range(sparse_count):
        target_ref[k * own_out : (k + 1) * own_out, :] = measured_ref[k]


def turn_kernel(rw_ref, _, turned_ref):
    turned = rw_ref[...].T
    high = turned.astype(BF16)
    turned_ref[:, : high.shape[1]] = high
    turned_ref[:, high.shape[1] :] = (turned - high.astype(F32)).astype(BF16)


def origin(route):
    return entry(sources(route, lax.axis_size("pair")), ("wide", "pair"))


def first_and_second_layer(current, previous, groups, firsts, a2_ref, b1, b2, h, own_out):
    outs = a2_ref.shape[0]
    channels = outs // own_out
    pieces = ([], [])
    for (first, taken), first_ref in zip(groups, firsts):
        rows = slice(first * channels, (first + taken) * channels)
        half = taken * channels
        stacked = jnp.concatenate([current[rows], previous[rows]], axis=0)
        summed = jnp.dot(first_ref[...], stacked, preferred_element_type=F32)
        for e in range(2):
            pieces[e].append(leaky_relu(summed[e * half : (e + 1) * half] + b1[rows]).astype(BF16))
    both = jnp.concatenate([jnp.concatenate(piece, axis=0) for piece in pieces], axis=1)
    hidden = leaky_relu(jnp.dot(a2_ref[...], both, preferred_element_type=F32) + b2) * h
    value = jnp.sum(hidden.reshape(outs // 8, 8, hidden.shape[1]), axis=0)
    apart = own_out
    while apart < 8:
        value += pltpu.roll(value, apart, 0)
        apart *= 2
    return value


def wider(ref, times):
    return jnp.concatenate([ref[...]] * times, axis=1)


def choose(select, view, tile, picked):
    repeated = jnp.concatenate([tile] * (select.shape[0] // 8), axis=0)
    return jnp.where(select == view.astype(F32), repeated, picked)


def early_kernel(routes, own_out, groups, *refs):
    wide = len(routes) + 1
    windows, firsts, refs = refs[: wide - 1], refs[wide - 1 : wide - 1 + len(groups)], refs[wide - 1 + len(groups) :]
    a2_ref, b1_ref, b2_ref, h_ref, select_ref, tiles_ref, picked_ref, next_ref, before_ref, views_ref = refs
    lanes = windows[0].shape[1]
    me = lax.axis_index("wide")
    missing = origin(routes[-1])
    for window, source in zip(windows, [me] + [origin(route) for route in routes[:-1]]):
        slot = lax.rem(source - missing + wide, wide) - 1
        views_ref[:, pl.ds(pl.multiple_of(slot * lanes, lanes), lanes)] = window[...]
    next_ref[...] = views_ref[:, :lanes]
    before_ref[...] = views_ref[:, (wide - 2) * lanes :]
    many = 2 if wide % 2 == 0 else 1
    b1, b2, h = wider(b1_ref, many), wider(b2_ref, 2 * many), wider(h_ref, 2 * many)
    select = select_ref[...]
    picked = jnp.zeros(select.shape, F32)
    for pair in range(0, wide - 2, many):
        previous = views_ref[:, pair * lanes : (pair + many) * lanes]
        current = views_ref[:, (pair + 1) * lanes : (pair + 1 + many) * lanes]
        value = first_and_second_layer(current, previous, groups, firsts, a2_ref, b1, b2, h, own_out)
        for e in range(2):
            for i in range(many):
                tile = value[:, (e * many + i) * lanes : (e * many + i + 1) * lanes]
                tiles_ref[2 * (pair + i) + e] = tile
                view = 2 * lax.rem(missing + 2 + pair + i, wide) + e
                picked = choose(select, view, tile, picked)
    picked_ref[...] = picked


def late_kernel(routes, own_out, groups, *refs):
    wide = len(routes) + 1
    window_ref, next_ref, before_ref, *firsts = refs[: 3 + len(groups)]
    a2_ref, b1_ref, b2_ref, h_ref, select_ref, target_ref, picked_ref, tiles_ref, residual_ref = refs[3 + len(groups) :]
    lanes = window_ref.shape[1]
    missing = origin(routes[-1])
    current = jnp.concatenate([window_ref[...], next_ref[...]], axis=1)
    previous = jnp.concatenate([before_ref[...], window_ref[...]], axis=1)
    b1, b2, h = wider(b1_ref, 2), wider(b2_ref, 4), wider(h_ref, 4)
    value = first_and_second_layer(current, previous, groups, firsts, a2_ref, b1, b2, h, own_out)
    select, picked = select_ref[...], picked_ref[...]
    for e in range(2):
        for i in range(2):
            tile = value[:, (2 * e + i) * lanes : (2 * e + i + 1) * lanes]
            tiles_ref[2 * i + e] = tile
            picked = choose(select, 2 * lax.rem(missing + i, wide) + e, tile, picked)
    residual_ref[...] = (picked - target_ref[...]).astype(BF16)


def adjoint_kernel(routes, shifts, straight, own_out, *refs):
    many, across = len(shifts), len(straight)
    cores = lax.axis_size("pair")
    evens, odds = refs[cores : cores + across], refs[many + across : many + 2 * across]
    near, diagonal, refs = refs[:cores], refs[cores + across : many + across], refs[many + 2 * across :]
    residuals = [ref[...] for ref in near + diagonal]
    is_odd = lax.rem(lax.axis_index("pair"), 2) == 1
    residuals += [jnp.where(is_odd, odd[...], even[...]) for even, odd in zip(evens, odds)]
    shifts = shifts + straight
    turned_ref, early_ref, late_ref, out_ref, predicted_ref = refs
    wide = len(routes) + 1
    missing = origin(routes[-1])
    for pair in range(wide):
        view = lax.rem(missing + pair, wide)
        for e in range(2):
            tile = late_ref[2 * pair + e] if pair < 2 else early_ref[2 * (pair - 2) + e]
            predicted_ref[2 * view + e] = tile[:own_out]
    lanes = residuals[0].shape[1]
    weights = []
    for narrow_shift, pair_shift in shifts:
        narrow, pair = came_from("narrow", narrow_shift), came_from("pair", pair_shift)
        block = narrow * lax.axis_size("pair") + pair
        weights.append(turned_ref[pl.ds(pl.multiple_of(block * lanes, lanes), lanes), :])
    values = jnp.concatenate(residuals, axis=1)
    both = jnp.dot(values, jnp.concatenate(weights, axis=0), preferred_element_type=F32)
    total = both[:, :lanes] + both[:, lanes:]
    for k in range(out_ref.shape[0]):
        out_ref[k] = total[k * own_out : (k + 1) * own_out]


def came_from(axis, distance):
    count = lax.axis_size(axis)
    return lax.rem(lax.axis_index(axis) - distance + count, count)


def send_both(block, narrow_distance, pair_distance, parity=None):
    narrow, pair = lax.axis_size("narrow"), lax.axis_size("pair")
    route = []
    for i in range(narrow):
        for j in range(pair):
            target = (i + narrow_distance) % narrow * pair + (j + pair_distance) % pair
            if parity is not None and j % 2 != parity:
                target = i * pair + j
            route.append((i * pair + j, target))
    return lax.ppermute(block, ("narrow", "pair"), route)


def local(
    low_sino,
    angle_weight,
    angle_bias,
    column_weight,
    column_bias,
    head_weight,
    sparse_views,
    measured,
    row_weights,
):
    wide, narrow, pair = (lax.axis_size(axis) for axis in ("wide", "narrow", "pair"))
    _, channels, width, lanes = low_sino.shape
    own_out = width // wide // 2
    span = 2 * own_out + 2
    size, outs = span * channels, own_out * channels
    sparse_count = measured.shape[0]
    rows = row_weights.shape[1]
    flat = (sparse_count * own_out, lanes)
    shape = jax.ShapeDtypeStruct
    big = 16 if width <= 64 else 48

    small = (
        angle_weight,
        angle_bias[None],
        column_weight,
        column_bias[None],
        head_weight[None],
        measured,
        sparse_views,
    )
    routes = rounds(wide, pair)
    groups = column_groups(channels, span)
    windows = call(
        functools.partial(pack_kernel, routes),
        [shape((size, lanes), BF16)] * wide,
        [pl.BlockSpec(memory_space=pltpu.HBM)],
        [
            pltpu.VMEM((channels, width, lanes), BF16),
            pltpu.VMEM((16 + (channels + 1) * width, lanes), F32),
            pltpu.SemaphoreType.DMA((4,)),
        ],
        vmem=53.6 if width <= 64 else 48,
    )(low_sino)
    windows = [windows[0]] + [
        lax.ppermute(window, ("wide", "pair"), [(p, t * pair + p % pair) for p, t in enumerate(route)])
        for window, route in zip(windows[1:], routes)
    ]

    widths = sorted({taken for _, taken in groups})
    *firsts, a2, b1, b2, head, select, target = call(
        functools.partial(prepare_kernel, wide, own_out, groups),
        [shape((2 * taken * channels, 2 * taken * channels), BF16) for taken in widths]
        + [
            shape((outs, size), BF16),
            shape((size, lanes), F32),
            shape((outs, lanes), F32),
            shape((outs, lanes), F32),
            shape(flat, F32),
            shape(flat, F32),
        ],
        [VMEM] * 7,
        vmem=big,
    )(*small)
    firsts = [firsts[widths.index(taken)] for _, taken in groups]

    window = shape((size, lanes), BF16)
    early_tiles, picked, following, before = call(
        functools.partial(early_kernel, routes, own_out, groups),
        [shape((2 * wide - 4, 8, lanes), F32), shape(flat, F32), window, window],
        [VMEM] * (wide + len(groups) + 4),
        [pltpu.VMEM((size, (wide - 1) * lanes), BF16)],
        vmem=big,
    )(*windows[:-1], *firsts, a2, b1, b2, head, select)
    late_tiles, residual = call(
        functools.partial(late_kernel, routes, own_out, groups),
        [shape((4, 8, lanes), F32), shape(flat, BF16)],
        [VMEM] * (len(groups) + 10),
        vmem=big,
    )(windows[-1], following, before, *firsts, a2, b1, b2, head, select, target, picked)

    turned = call(turn_kernel, shape((rows, 2 * lanes), BF16), [VMEM] * 2, vmem=big)(row_weights, residual)
    across = range(1, narrow)
    shifts = [(0, t) for t in range(1, pair)] + [(s, t) for s in across for t in range(1, pair)]
    straight = [(s, 0) for s in across]
    near = [send_both(residual, 0, t) for t in range(1, pair)]
    even = [send_both(residual, s, 0, 0) for s in across]
    diagonal = [send_both(residual, s, t) for s in across for t in range(1, pair)]
    odd = [send_both(residual, s, 0, 1) for s in across]
    blocks = [residual] + near + even + diagonal + odd
    shifts.insert(0, (0, 0))
    adjoint, predicted = call(
        functools.partial(adjoint_kernel, routes, shifts, straight, own_out),
        [shape((sparse_count, own_out, lanes), F32), shape((2 * wide, own_out, lanes), F32)],
        [VMEM] * (len(blocks) + 3),
        vmem=big,
    )(*blocks, turned, early_tiles, late_tiles)
    return (predicted, adjoint)


def solution(mesh):
    in_specs = (
        P(("parts", "wide"), None, None, ("narrow", "pair")),
        P(),
        P(),
        P(),
        P(),
        P(),
        P(("parts", "narrow"), None),
        P("parts", "wide", ("narrow", "pair")),
        P(("narrow", "pair"), None),
    )
    out_specs = (P("parts", "wide", ("narrow", "pair")), P("parts", "wide", ("narrow", "pair")))
    return jax.shard_map(local, mesh=mesh, in_specs=in_specs, out_specs=out_specs, check_vma=False)
```

```python
import functools

import jax
import jax.numpy as jnp
from jax import lax
from jax.experimental import pallas as pl
from jax.experimental.pallas import tpu as pltpu
from jax.sharding import PartitionSpec as P

F32, BF16 = jnp.float32, jnp.bfloat16
VMEM = pl.BlockSpec(memory_space=pltpu.VMEM)
TAPS = 4


def call(kernel, outs, in_specs, scratch=(), vmem=16, flops=10**6):
    nbytes = sum(o.size * o.dtype.itemsize for o in jax.tree.leaves(outs))
    return pl.pallas_call(
        kernel,
        out_shape=outs,
        in_specs=in_specs,
        out_specs=jax.tree.map(lambda _: VMEM, outs),
        scratch_shapes=list(scratch),
        compiler_params=pltpu.CompilerParams(vmem_limit_bytes=int(vmem * 2**20)),
        cost_estimate=pl.CostEstimate(flops=flops, bytes_accessed=nbytes, transcendentals=0),
    )


def leaky_relu(values):
    return jnp.maximum(values, 0.1 * values)


def split(index, size):
    whole = ((index.astype(F32) + 0.5) * (1.0 / size)).astype(jnp.int32)
    return whole, index - whole * size


def iota(shape, axis):
    return lax.broadcasted_iota(jnp.int32, shape, axis)


def rounds(count, cores):
    if count == 4:
        schedules = [
            [(1, 3, 0, 2), (3, 2, 1, 0), (2, 0, 3, 1)],
            [(2, 3, 1, 0), (3, 2, 0, 1), (1, 0, 3, 2)],
        ]
    else:
        schedules = [[tuple((i + shift) % count for i in range(count)) for shift in range(1, count)]]
    return [
        tuple(schedules[core % len(schedules)][r][i] for i in range(count) for core in range(cores))
        for r in range(count - 1)
    ]


def sources(route, cores):
    back = [0] * len(route)
    for place, target in enumerate(route):
        back[target * cores + place % cores] = place // cores
    return tuple(back)


def entry(table, axes):
    index = lax.axis_index(axes)
    value = jnp.int32(table[0])
    for i in range(1, len(table)):
        value = jnp.where(index == i, jnp.int32(table[i]), value)
    return value


def column_groups(channels, span):
    most = max(1, 256 // (2 * channels) // 2 * 2)
    return [(first, min(most, span - first)) for first in range(0, span, most)]


def pack_window(window_ref, rows_ref, channels, width, span, target):
    first = target * (span - 2) + 7
    columns = [rows_ref[pl.ds(first + i, channels, stride=width), :] for i in range(span)]
    window_ref[...] = jnp.concatenate(columns, axis=0).astype(BF16)


def clear_edges(rows_ref, count):
    edge = jnp.zeros((8, rows_ref.shape[1]), F32)
    rows_ref[0:8, :] = edge
    rows_ref[8 + count : 16 + count, :] = edge


def pack_kernel(routes, low_ref, *refs):
    windows, (block_ref, rows_ref, sems) = refs[: len(routes)], refs[len(routes) :]
    _, channels, width, rows = low_ref.shape
    parts = sems.shape[0]
    each = channels // parts
    pieces = []
    for i in range(parts):
        piece = pl.ds(i * each, each)
        pieces.append(pltpu.make_async_copy(low_ref.at[0, piece], block_ref.at[piece], sems.at[i]))
        pieces[-1].start()
    clear_edges(rows_ref, channels * width)
    targets = [entry(route, ("wide", "pair")) for route in routes]
    for i in range(parts):
        pieces[i].wait()
        values = block_ref[i * each : (i + 1) * each].astype(F32).reshape(each * width, rows)
        rows_ref[8 + i * each * width : 8 + (i + 1) * each * width, :] = values
    for window, target in zip(windows, targets):
        pack_window(window, rows_ref, channels, width, width // (len(routes) + 1) + 2, target)


def prepare_kernel(
    wide,
    own_out,
    groups,
    aw_ref,
    ab_ref,
    cw_ref,
    cb_ref,
    hw_ref,
    measured_ref,
    sparse_ref,
    block_ref,
    *refs,
):
    firsts, refs = refs[:-8], refs[-8:]
    a2_ref, b1_ref, b2_ref, h_ref, select_ref, target_ref, own_ref, rows_ref = refs
    channels, width, lanes = block_ref.shape
    span = 2 * own_out + 2
    clear_edges(rows_ref, channels * width)
    rows_ref[8 : 8 + channels * width, :] = block_ref[...].astype(F32).reshape(channels * width, lanes)
    pack_window(own_ref, rows_ref, channels, width, span, lax.axis_index("wide"))
    size, outs = span * channels, own_out * channels
    rows, columns = split(iota((size, channels), 0), channels)
    pick = (columns == iota((size, channels), 1)).astype(F32)
    pick16 = pick.astype(BF16)
    out_channel, _ = split(iota((outs, channels), 0), own_out)
    pick_out = (out_channel == iota((outs, channels), 1)).astype(F32)
    pick_out16 = pick_out.astype(BF16)

    def spread(left, weight, right):
        half = lax.dot_general(left, weight, (((1,), (1,)), ((), ())), preferred_element_type=F32)
        return lax.dot_general(half.astype(BF16), right, (((1,), (1,)), ((), ())), preferred_element_type=F32)

    for first_ref in firsts:
        many = first_ref.shape[0] // 2
        taken = many // channels
        which, channel = split(iota((2 * many, channels), 0), channels)
        is_channel = channel == iota((2 * many, channels), 1)
        sides = [is_channel & (which >= side * taken) & (which < (side + 1) * taken) for side in range(2)]
        sides = [side.astype(F32).astype(BF16) for side in sides]
        row_column = split(iota((many, 2 * many), 0), channels)[0]
        column_column = split(iota((many, 2 * many), 1), channels)[0]
        same = (row_column == column_column) | (row_column + taken == column_column)
        for e in range(2):
            full = spread(pick16[:many], aw_ref[e], sides[0]) + spread(pick16[:many], aw_ref[e + 2], sides[1])
            first_ref[e * many : (e + 1) * many, :] = jnp.where(same, full, 0.0).astype(BF16)

    in_column = split(iota((outs, size), 1), channels)[0]
    out_column = split(iota((outs, size), 0), own_out)[1]
    me = lax.axis_index("wide")
    absolute = in_column + me * (2 * own_out) - 1
    inside = (absolute >= 0) & (absolute < 2 * own_out * wide)
    total = jnp.zeros((outs, size), F32)
    for tap in range(TAPS):
        here = (in_column == 2 * out_column + tap) & inside
        total = jnp.where(here, spread(pick_out16, cw_ref[tap], pick16), total)
    a2_ref[...] = total.astype(BF16)

    def along(left, vector_ref, out_ref):
        summed = jnp.sum(left * vector_ref[...].astype(F32), axis=1, keepdims=True)
        out_ref[...] = jnp.broadcast_to(summed, out_ref.shape)

    along(pick, ab_ref, b1_ref)
    along(pick_out, cb_ref, b2_ref)
    along(pick_out, hw_ref, h_ref)

    sparse_count = measured_ref.shape[0]
    wanted = (select_ref.shape[0], sparse_count)
    pick_view = (split(iota(wanted, 0), own_out)[0] == iota(wanted, 1)).astype(F32)
    along(pick_view, sparse_ref, select_ref)
    for k in range(sparse_count):
        target_ref[k * own_out : (k + 1) * own_out, :] = measured_ref[k]


def turn_kernel(routes, rw_ref, early_ref, late_ref, turned_ref, predicted_ref):
    wide = len(routes) + 1
    missing = origin(routes[-1])
    for pair in range(wide):
        view = lax.rem(missing + pair, wide)
        for e in range(2):
            tile = late_ref[2 * pair + e] if pair < 2 else early_ref[2 * (pair - 2) + e]
            predicted_ref[2 * view + e] = tile[: predicted_ref.shape[1]]
    turned = rw_ref[...].T
    high = turned.astype(BF16)
    turned_ref[:, : high.shape[1]] = high
    turned_ref[:, high.shape[1] :] = (turned - high.astype(F32)).astype(BF16)


def origin(route):
    return entry(sources(route, lax.axis_size("pair")), ("wide", "pair"))


def first_and_second_layer(current, previous, groups, firsts, a2_ref, b1, b2, h, own_out):
    outs = a2_ref.shape[0]
    channels = outs // own_out
    pieces = ([], [])
    for (first, taken), first_ref in zip(groups, firsts):
        rows = slice(first * channels, (first + taken) * channels)
        half = taken * channels
        stacked = jnp.concatenate([current[rows], previous[rows]], axis=0)
        summed = jnp.dot(first_ref[...], stacked, preferred_element_type=F32)
        for e in range(2):
            pieces[e].append(leaky_relu(summed[e * half : (e + 1) * half] + b1[rows]).astype(BF16))
    both = jnp.concatenate([jnp.concatenate(piece, axis=0) for piece in pieces], axis=1)
    hidden = leaky_relu(jnp.dot(a2_ref[...], both, preferred_element_type=F32) + b2) * h
    value = jnp.sum(hidden.reshape(outs // 8, 8, hidden.shape[1]), axis=0)
    apart = own_out
    while apart < 8:
        value += pltpu.roll(value, apart, 0)
        apart *= 2
    return value


def wider(ref, times):
    return jnp.concatenate([ref[...]] * times, axis=1)


def choose(select, view, tile, picked):
    repeated = jnp.concatenate([tile] * (select.shape[0] // 8), axis=0)
    return jnp.where(select == view.astype(F32), repeated, picked)


def early_kernel(routes, own_out, groups, *refs):
    wide = len(routes) + 1
    windows, firsts, refs = refs[: wide - 1], refs[wide - 1 : wide - 1 + len(groups)], refs[wide - 1 + len(groups) :]
    a2_ref, b1_ref, b2_ref, h_ref, select_ref, tiles_ref, picked_ref, next_ref, before_ref, views_ref = refs
    lanes = windows[0].shape[1]
    me = lax.axis_index("wide")
    missing = origin(routes[-1])
    for window, source in zip(windows, [me] + [origin(route) for route in routes[:-1]]):
        slot = lax.rem(source - missing + wide, wide) - 1
        views_ref[:, pl.ds(pl.multiple_of(slot * lanes, lanes), lanes)] = window[...]
    next_ref[...] = views_ref[:, :lanes]
    before_ref[...] = views_ref[:, (wide - 2) * lanes :]
    many = 2 if wide % 2 == 0 else 1
    b1, b2, h = wider(b1_ref, many), wider(b2_ref, 2 * many), wider(h_ref, 2 * many)
    select = select_ref[...]
    picked = jnp.zeros(select.shape, F32)
    for pair in range(0, wide - 2, many):
        previous = views_ref[:, pair * lanes : (pair + many) * lanes]
        current = views_ref[:, (pair + 1) * lanes : (pair + 1 + many) * lanes]
        value = first_and_second_layer(current, previous, groups, firsts, a2_ref, b1, b2, h, own_out)
        for e in range(2):
            for i in range(many):
                tile = value[:, (e * many + i) * lanes : (e * many + i + 1) * lanes]
                tiles_ref[2 * (pair + i) + e] = tile
                view = 2 * lax.rem(missing + 2 + pair + i, wide) + e
                picked = choose(select, view, tile, picked)
    picked_ref[...] = picked


def late_kernel(routes, own_out, groups, *refs):
    wide = len(routes) + 1
    window_ref, next_ref, before_ref, *firsts = refs[: 3 + len(groups)]
    a2_ref, b1_ref, b2_ref, h_ref, select_ref, target_ref, picked_ref, tiles_ref, residual_ref = refs[3 + len(groups) :]
    lanes = window_ref.shape[1]
    missing = origin(routes[-1])
    current = jnp.concatenate([window_ref[...], next_ref[...]], axis=1)
    previous = jnp.concatenate([before_ref[...], window_ref[...]], axis=1)
    b1, b2, h = wider(b1_ref, 2), wider(b2_ref, 4), wider(h_ref, 4)
    value = first_and_second_layer(current, previous, groups, firsts, a2_ref, b1, b2, h, own_out)
    select, picked = select_ref[...], picked_ref[...]
    for e in range(2):
        for i in range(2):
            tile = value[:, (2 * e + i) * lanes : (2 * e + i + 1) * lanes]
            tiles_ref[2 * i + e] = tile
            picked = choose(select, 2 * lax.rem(missing + i, wide) + e, tile, picked)
    residual_ref[...] = (picked - target_ref[...]).astype(BF16)


def adjoint_kernel(shifts, own_out, *refs):
    residuals, refs = refs[: len(shifts)], refs[len(shifts) :]
    turned_ref, out_ref = refs
    lanes = residuals[0].shape[1]
    weights = []
    for narrow_shift, pair_shift in shifts:
        narrow, pair = came_from("narrow", narrow_shift), came_from("pair", pair_shift)
        block = narrow * lax.axis_size("pair") + pair
        weights.append(turned_ref[pl.ds(pl.multiple_of(block * lanes, lanes), lanes), :])
    values = jnp.concatenate([ref[...] for ref in residuals], axis=1)
    both = jnp.dot(values, jnp.concatenate(weights, axis=0), preferred_element_type=F32)
    total = both[:, :lanes] + both[:, lanes:]
    for k in range(out_ref.shape[0]):
        out_ref[k] = total[k * own_out : (k + 1) * own_out]


def came_from(axis, distance):
    count = lax.axis_size(axis)
    return lax.rem(lax.axis_index(axis) - distance + count, count)


def send_both(block, narrow_distance, pair_distance):
    narrow, pair = lax.axis_size("narrow"), lax.axis_size("pair")
    route = []
    for i in range(narrow):
        for j in range(pair):
            target = (i + narrow_distance) % narrow * pair + (j + pair_distance) % pair
            route.append((i * pair + j, target))
    return lax.ppermute(block, ("narrow", "pair"), route)


def local(
    low_sino,
    angle_weight,
    angle_bias,
    column_weight,
    column_bias,
    head_weight,
    sparse_views,
    measured,
    row_weights,
):
    wide, narrow, pair = (lax.axis_size(axis) for axis in ("wide", "narrow", "pair"))
    _, channels, width, lanes = low_sino.shape
    own_out = width // wide // 2
    span = 2 * own_out + 2
    size, outs = span * channels, own_out * channels
    sparse_count = measured.shape[0]
    rows = row_weights.shape[1]
    flat = (sparse_count * own_out, lanes)
    shape = jax.ShapeDtypeStruct
    big = 16 if width <= 64 else 48

    small = (
        angle_weight,
        angle_bias[None],
        column_weight,
        column_bias[None],
        head_weight[None],
        measured,
        sparse_views,
    )
    routes = rounds(wide, pair)
    groups = column_groups(channels, span)
    rows_scratch = pltpu.VMEM((16 + (channels + 1) * width, lanes), F32)
    *windows, block = call(
        functools.partial(pack_kernel, routes),
        [shape((size, lanes), BF16)] * (wide - 1) + [shape(low_sino.shape[1:], BF16)],
        [pl.BlockSpec(memory_space=pltpu.HBM)],
        [rows_scratch, pltpu.SemaphoreType.DMA((4,))],
        vmem=53.5 if width <= 64 else 48,
    )(low_sino)
    windows = [
        lax.ppermute(window, ("wide", "pair"), [(p, t * pair + p % pair) for p, t in enumerate(route)])
        for window, route in zip(windows, routes)
    ]

    widths = sorted({taken for _, taken in groups})
    *firsts, a2, b1, b2, head, select, target, own = call(
        functools.partial(prepare_kernel, wide, own_out, groups),
        [shape((2 * taken * channels, 2 * taken * channels), BF16) for taken in widths]
        + [
            shape((outs, size), BF16),
            shape((size, lanes), F32),
            shape((outs, lanes), F32),
            shape((outs, lanes), F32),
            shape(flat, F32),
            shape(flat, F32),
            shape((size, lanes), BF16),
        ],
        [VMEM] * 8,
        [rows_scratch],
        vmem=big,
    )(*small, block)
    windows.insert(0, own)
    firsts = [firsts[widths.index(taken)] for _, taken in groups]

    window = shape((size, lanes), BF16)
    early_tiles, picked, following, before = call(
        functools.partial(early_kernel, routes, own_out, groups),
        [shape((2 * wide - 4, 8, lanes), F32), shape(flat, F32), window, window],
        [VMEM] * (wide + len(groups) + 4),
        [pltpu.VMEM((size, (wide - 1) * lanes), BF16)],
        vmem=big,
    )(*windows[:-1], *firsts, a2, b1, b2, head, select)
    late_tiles, residual = call(
        functools.partial(late_kernel, routes, own_out, groups),
        [shape((4, 8, lanes), F32), shape(flat, BF16)],
        [VMEM] * (len(groups) + 10),
        vmem=big,
    )(windows[-1], following, before, *firsts, a2, b1, b2, head, select, target, picked)

    turned, predicted = call(
        functools.partial(turn_kernel, routes),
        [shape((rows, 2 * lanes), BF16), shape((2 * wide, own_out, lanes), F32)],
        [VMEM] * 3,
        vmem=big,
    )(row_weights, early_tiles, late_tiles)
    shifts = [(0, t) for t in range(1, pair)] + [(s, 0) for s in range(1, narrow)]
    shifts += [(s, t) for s in range(1, narrow) for t in range(1, pair)]
    blocks = [residual] + [send_both(residual, s, t) for s, t in shifts]
    shifts.insert(0, (0, 0))
    adjoint = call(
        functools.partial(adjoint_kernel, shifts, own_out),
        shape((sparse_count, own_out, lanes), F32),
        [VMEM] * (len(blocks) + 1),
        vmem=big,
    )(*blocks, turned)
    return (predicted, adjoint)


def solution(mesh):
    in_specs = (
        P(("parts", "wide"), None, None, ("narrow", "pair")),
        P(),
        P(),
        P(),
        P(),
        P(),
        P(("parts", "narrow"), None),
        P("parts", "wide", ("narrow", "pair")),
        P(("narrow", "pair"), None),
    )
    out_specs = (P("parts", "wide", ("narrow", "pair")), P("parts", "wide", ("narrow", "pair")))
    return jax.shard_map(local, mesh=mesh, in_specs=in_specs, out_specs=out_specs, check_vma=False)
```

```python
import functools

import jax
import jax.numpy as jnp
from jax import lax
from jax.experimental import pallas as pl
from jax.experimental.pallas import tpu as pltpu
from jax.sharding import PartitionSpec as P

F32, BF16 = jnp.float32, jnp.bfloat16
VMEM = pl.BlockSpec(memory_space=pltpu.VMEM)
TAPS = 4


def call(kernel, outs, in_specs, scratch=(), vmem=16, flops=10**6):
    nbytes = sum(o.size * o.dtype.itemsize for o in jax.tree.leaves(outs))
    return pl.pallas_call(
        kernel,
        out_shape=outs,
        in_specs=in_specs,
        out_specs=jax.tree.map(lambda _: VMEM, outs),
        scratch_shapes=list(scratch),
        compiler_params=pltpu.CompilerParams(vmem_limit_bytes=int(vmem * 2**20)),
        cost_estimate=pl.CostEstimate(flops=flops, bytes_accessed=nbytes, transcendentals=0),
    )


def leaky_relu(values):
    return jnp.maximum(values, 0.1 * values)


def split(index, size):
    whole = ((index.astype(F32) + 0.5) * (1.0 / size)).astype(jnp.int32)
    return whole, index - whole * size


def iota(shape, axis):
    return lax.broadcasted_iota(jnp.int32, shape, axis)


def rounds(count, cores):
    if count == 4:
        schedules = [
            [(1, 3, 0, 2), (3, 2, 1, 0), (2, 0, 3, 1)],
            [(2, 3, 1, 0), (3, 2, 0, 1), (1, 0, 3, 2)],
        ]
    else:
        schedules = [[tuple((i + shift) % count for i in range(count)) for shift in range(1, count)]]
    return [
        tuple(schedules[core % len(schedules)][r][i] for i in range(count) for core in range(cores))
        for r in range(count - 1)
    ]


def sources(route, cores):
    back = [0] * len(route)
    for place, target in enumerate(route):
        back[target * cores + place % cores] = place // cores
    return tuple(back)


def entry(table, axes):
    index = lax.axis_index(axes)
    value = jnp.int32(table[0])
    for i in range(1, len(table)):
        value = jnp.where(index == i, jnp.int32(table[i]), value)
    return value


def column_groups(channels, span):
    most = max(1, 256 // (2 * channels) // 2 * 2)
    return [(first, min(most, span - first)) for first in range(0, span, most)]


def pack_window(window_ref, rows_ref, channels, width, span, target):
    first = target * (span - 2) + 7
    columns = [rows_ref[pl.ds(first + i, channels, stride=width), :] for i in range(span)]
    window_ref[...] = jnp.concatenate(columns, axis=0).astype(BF16)


def clear_edges(rows_ref, count):
    edge = jnp.zeros((8, rows_ref.shape[1]), F32)
    rows_ref[0:8, :] = edge
    rows_ref[8 + count : 16 + count, :] = edge


def pack_kernel(routes, low_ref, *refs):
    windows, (block_ref, rows_ref, sems) = refs[: len(routes)], refs[len(routes) :]
    _, channels, width, rows = low_ref.shape
    parts = sems.shape[0]
    each = channels // parts
    pieces = []
    for i in range(parts):
        piece = pl.ds(i * each, each)
        pieces.append(pltpu.make_async_copy(low_ref.at[0, piece], block_ref.at[piece], sems.at[i]))
        pieces[-1].start()
    clear_edges(rows_ref, channels * width)
    targets = [entry(route, ("wide", "pair")) for route in routes]
    for i in range(parts):
        pieces[i].wait()
        values = block_ref[i * each : (i + 1) * each].astype(F32).reshape(each * width, rows)
        rows_ref[8 + i * each * width : 8 + (i + 1) * each * width, :] = values
    for window, target in zip(windows, targets):
        pack_window(window, rows_ref, channels, width, width // (len(routes) + 1) + 2, target)


def prepare_kernel(
    wide,
    own_out,
    groups,
    aw_ref,
    ab_ref,
    cw_ref,
    cb_ref,
    hw_ref,
    measured_ref,
    sparse_ref,
    block_ref,
    *refs,
):
    firsts, refs = refs[:-8], refs[-8:]
    a2_ref, b1_ref, b2_ref, h_ref, select_ref, target_ref, own_ref, rows_ref = refs
    channels, width, lanes = block_ref.shape
    span = 2 * own_out + 2
    clear_edges(rows_ref, channels * width)
    rows_ref[8 : 8 + channels * width, :] = block_ref[...].astype(F32).reshape(channels * width, lanes)
    pack_window(own_ref, rows_ref, channels, width, span, lax.axis_index("wide"))
    size, outs = span * channels, own_out * channels
    rows, columns = split(iota((size, channels), 0), channels)
    pick = (columns == iota((size, channels), 1)).astype(F32)
    pick16 = pick.astype(BF16)
    out_channel, _ = split(iota((outs, channels), 0), own_out)
    pick_out = (out_channel == iota((outs, channels), 1)).astype(F32)
    pick_out16 = pick_out.astype(BF16)

    def spread(left, weight, right):
        half = lax.dot_general(left, weight, (((1,), (1,)), ((), ())), preferred_element_type=F32)
        return lax.dot_general(half.astype(BF16), right, (((1,), (1,)), ((), ())), preferred_element_type=F32)

    for first_ref in firsts:
        many = first_ref.shape[0] // 2
        taken = many // channels
        which, channel = split(iota((2 * many, channels), 0), channels)
        is_channel = channel == iota((2 * many, channels), 1)
        sides = [is_channel & (which >= side * taken) & (which < (side + 1) * taken) for side in range(2)]
        sides = [side.astype(F32).astype(BF16) for side in sides]
        row_column = split(iota((many, 2 * many), 0), channels)[0]
        column_column = split(iota((many, 2 * many), 1), channels)[0]
        same = (row_column == column_column) | (row_column + taken == column_column)
        for e in range(2):
            full = spread(pick16[:many], aw_ref[e], sides[0]) + spread(pick16[:many], aw_ref[e + 2], sides[1])
            first_ref[e * many : (e + 1) * many, :] = jnp.where(same, full, 0.0).astype(BF16)

    in_column = split(iota((outs, size), 1), channels)[0]
    out_column = split(iota((outs, size), 0), own_out)[1]
    me = lax.axis_index("wide")
    absolute = in_column + me * (2 * own_out) - 1
    inside = (absolute >= 0) & (absolute < 2 * own_out * wide)
    total = jnp.zeros((outs, size), F32)
    for tap in range(TAPS):
        here = (in_column == 2 * out_column + tap) & inside
        total = jnp.where(here, spread(pick_out16, cw_ref[tap], pick16), total)
    a2_ref[...] = total.astype(BF16)

    def along(left, vector_ref, out_ref):
        summed = jnp.sum(left * vector_ref[...].astype(F32), axis=1, keepdims=True)
        out_ref[...] = jnp.broadcast_to(summed, out_ref.shape)

    along(pick, ab_ref, b1_ref)
    along(pick_out, cb_ref, b2_ref)
    along(pick_out, hw_ref, h_ref)

    sparse_count = measured_ref.shape[0]
    wanted = (select_ref.shape[0], sparse_count)
    pick_view = (split(iota(wanted, 0), own_out)[0] == iota(wanted, 1)).astype(F32)
    along(pick_view, sparse_ref, select_ref)
    for k in range(sparse_count):
        target_ref[k * own_out : (k + 1) * own_out, :] = measured_ref[k]


def turn_kernel(routes, rw_ref, early_ref, late_ref, turned_ref, predicted_ref):
    wide = len(routes) + 1
    missing = origin(routes[-1])
    for pair in range(wide):
        view = lax.rem(missing + pair, wide)
        for e in range(2):
            tile = late_ref[2 * pair + e] if pair < 2 else early_ref[2 * (pair - 2) + e]
            predicted_ref[2 * view + e] = tile[: predicted_ref.shape[1]]
    turned = rw_ref[...].T
    high = turned.astype(BF16)
    turned_ref[:, : high.shape[1]] = high
    turned_ref[:, high.shape[1] :] = (turned - high.astype(F32)).astype(BF16)


def origin(route):
    return entry(sources(route, lax.axis_size("pair")), ("wide", "pair"))


def first_and_second_layer(current, previous, groups, firsts, a2_ref, b1, b2, h, own_out):
    outs = a2_ref.shape[0]
    channels = outs // own_out
    pieces = ([], [])
    for (first, taken), first_ref in zip(groups, firsts):
        rows = slice(first * channels, (first + taken) * channels)
        half = taken * channels
        stacked = jnp.concatenate([current[rows], previous[rows]], axis=0)
        summed = jnp.dot(first_ref[...], stacked, preferred_element_type=F32)
        for e in range(2):
            pieces[e].append(leaky_relu(summed[e * half : (e + 1) * half] + b1[rows]).astype(BF16))
    both = jnp.concatenate([jnp.concatenate(piece, axis=0) for piece in pieces], axis=1)
    hidden = leaky_relu(jnp.dot(a2_ref[...], both, preferred_element_type=F32) + b2) * h
    value = jnp.sum(hidden.reshape(outs // 8, 8, hidden.shape[1]), axis=0)
    apart = own_out
    while apart < 8:
        value += pltpu.roll(value, apart, 0)
        apart *= 2
    return value


def wider(ref, times):
    return jnp.concatenate([ref[...]] * times, axis=1)


def choose(select, view, tile, picked):
    repeated = jnp.concatenate([tile] * (select.shape[0] // 8), axis=0)
    return jnp.where(select == view.astype(F32), repeated, picked)


def early_kernel(routes, own_out, groups, *refs):
    wide = len(routes) + 1
    windows, firsts, refs = refs[: wide - 1], refs[wide - 1 : wide - 1 + len(groups)], refs[wide - 1 + len(groups) :]
    a2_ref, b1_ref, b2_ref, h_ref, select_ref, tiles_ref, picked_ref, next_ref, before_ref, views_ref = refs
    lanes = windows[0].shape[1]
    me = lax.axis_index("wide")
    missing = origin(routes[-1])
    slots = [lax.rem(source - missing + wide, wide) - 1 for source in [me] + [origin(route) for route in routes[:-1]]]
    if wide <= 4:
        values = [window[...] for window in windows]
        ordered = []
        for place in range(wide - 1):
            chosen = values[0]
            for value, slot in zip(values[1:], slots[1:]):
                chosen = jnp.where(slot == place, value, chosen)
            ordered.append(chosen)
        views = jnp.concatenate(ordered, axis=1)
    else:
        for window, slot in zip(windows, slots):
            views_ref[:, pl.ds(pl.multiple_of(slot * lanes, lanes), lanes)] = window[...]
        views = views_ref
    next_ref[...] = views[:, :lanes]
    before_ref[...] = views[:, (wide - 2) * lanes :]
    many = 2 if wide % 2 == 0 else 1
    b1, b2, h = wider(b1_ref, many), wider(b2_ref, 2 * many), wider(h_ref, 2 * many)
    select = select_ref[...]
    picked = jnp.zeros(select.shape, F32)
    for pair in range(0, wide - 2, many):
        previous = views[:, pair * lanes : (pair + many) * lanes]
        current = views[:, (pair + 1) * lanes : (pair + 1 + many) * lanes]
        value = first_and_second_layer(current, previous, groups, firsts, a2_ref, b1, b2, h, own_out)
        for e in range(2):
            for i in range(many):
                tile = value[:, (e * many + i) * lanes : (e * many + i + 1) * lanes]
                tiles_ref[2 * (pair + i) + e] = tile
                view = 2 * lax.rem(missing + 2 + pair + i, wide) + e
                picked = choose(select, view, tile, picked)
    picked_ref[...] = picked


def late_kernel(routes, own_out, groups, *refs):
    wide = len(routes) + 1
    window_ref, next_ref, before_ref, *firsts = refs[: 3 + len(groups)]
    a2_ref, b1_ref, b2_ref, h_ref, select_ref, target_ref, picked_ref, tiles_ref, residual_ref = refs[3 + len(groups) :]
    lanes = window_ref.shape[1]
    missing = origin(routes[-1])
    current = jnp.concatenate([window_ref[...], next_ref[...]], axis=1)
    previous = jnp.concatenate([before_ref[...], window_ref[...]], axis=1)
    b1, b2, h = wider(b1_ref, 2), wider(b2_ref, 4), wider(h_ref, 4)
    value = first_and_second_layer(current, previous, groups, firsts, a2_ref, b1, b2, h, own_out)
    select, picked = select_ref[...], picked_ref[...]
    for e in range(2):
        for i in range(2):
            tile = value[:, (2 * e + i) * lanes : (2 * e + i + 1) * lanes]
            tiles_ref[2 * i + e] = tile
            picked = choose(select, 2 * lax.rem(missing + i, wide) + e, tile, picked)
    residual_ref[...] = (picked - target_ref[...]).astype(BF16)


def adjoint_kernel(shifts, own_out, *refs):
    residuals, refs = refs[: len(shifts)], refs[len(shifts) :]
    turned_ref, out_ref = refs
    lanes = residuals[0].shape[1]
    weights = []
    for narrow_shift, pair_shift in shifts:
        narrow, pair = came_from("narrow", narrow_shift), came_from("pair", pair_shift)
        block = narrow * lax.axis_size("pair") + pair
        weights.append(turned_ref[pl.ds(pl.multiple_of(block * lanes, lanes), lanes), :])
    values = jnp.concatenate([ref[...] for ref in residuals], axis=1)
    both = jnp.dot(values, jnp.concatenate(weights, axis=0), preferred_element_type=F32)
    total = both[:, :lanes] + both[:, lanes:]
    for k in range(out_ref.shape[0]):
        out_ref[k] = total[k * own_out : (k + 1) * own_out]


def came_from(axis, distance):
    count = lax.axis_size(axis)
    return lax.rem(lax.axis_index(axis) - distance + count, count)


def send_both(block, narrow_distance, pair_distance):
    narrow, pair = lax.axis_size("narrow"), lax.axis_size("pair")
    route = []
    for i in range(narrow):
        for j in range(pair):
            target = (i + narrow_distance) % narrow * pair + (j + pair_distance) % pair
            route.append((i * pair + j, target))
    return lax.ppermute(block, ("narrow", "pair"), route)


def local(
    low_sino,
    angle_weight,
    angle_bias,
    column_weight,
    column_bias,
    head_weight,
    sparse_views,
    measured,
    row_weights,
):
    wide, narrow, pair = (lax.axis_size(axis) for axis in ("wide", "narrow", "pair"))
    _, channels, width, lanes = low_sino.shape
    own_out = width // wide // 2
    span = 2 * own_out + 2
    size, outs = span * channels, own_out * channels
    sparse_count = measured.shape[0]
    rows = row_weights.shape[1]
    flat = (sparse_count * own_out, lanes)
    shape = jax.ShapeDtypeStruct
    big = 16 if width <= 64 else 48

    small = (
        angle_weight,
        angle_bias[None],
        column_weight,
        column_bias[None],
        head_weight[None],
        measured,
        sparse_views,
    )
    routes = rounds(wide, pair)
    groups = column_groups(channels, span)
    rows_scratch = pltpu.VMEM((16 + (channels + 1) * width, lanes), F32)
    *windows, block = call(
        functools.partial(pack_kernel, routes),
        [shape((size, lanes), BF16)] * (wide - 1) + [shape(low_sino.shape[1:], BF16)],
        [pl.BlockSpec(memory_space=pltpu.HBM)],
        [rows_scratch, pltpu.SemaphoreType.DMA((4,))],
        vmem=53.5 if width <= 64 else 48,
    )(low_sino)
    windows = [
        lax.ppermute(window, ("wide", "pair"), [(p, t * pair + p % pair) for p, t in enumerate(route)])
        for window, route in zip(windows, routes)
    ]

    widths = sorted({taken for _, taken in groups})
    *firsts, a2, b1, b2, head, select, target, own = call(
        functools.partial(prepare_kernel, wide, own_out, groups),
        [shape((2 * taken * channels, 2 * taken * channels), BF16) for taken in widths]
        + [
            shape((outs, size), BF16),
            shape((size, lanes), F32),
            shape((outs, lanes), F32),
            shape((outs, lanes), F32),
            shape(flat, F32),
            shape(flat, F32),
            shape((size, lanes), BF16),
        ],
        [VMEM] * 8,
        [rows_scratch],
        vmem=big,
    )(*small, block)
    windows.insert(0, own)
    firsts = [firsts[widths.index(taken)] for _, taken in groups]

    window = shape((size, lanes), BF16)
    early_tiles, picked, following, before = call(
        functools.partial(early_kernel, routes, own_out, groups),
        [shape((2 * wide - 4, 8, lanes), F32), shape(flat, F32), window, window],
        [VMEM] * (wide + len(groups) + 4),
        [pltpu.VMEM((size, (wide - 1) * lanes), BF16)],
        vmem=big,
    )(*windows[:-1], *firsts, a2, b1, b2, head, select)
    late_tiles, residual = call(
        functools.partial(late_kernel, routes, own_out, groups),
        [shape((4, 8, lanes), F32), shape(flat, BF16)],
        [VMEM] * (len(groups) + 10),
        vmem=big,
    )(windows[-1], following, before, *firsts, a2, b1, b2, head, select, target, picked)

    turned, predicted = call(
        functools.partial(turn_kernel, routes),
        [shape((rows, 2 * lanes), BF16), shape((2 * wide, own_out, lanes), F32)],
        [VMEM] * 3,
        vmem=big,
    )(row_weights, early_tiles, late_tiles)
    shifts = [(0, t) for t in range(1, pair)] + [(s, 0) for s in range(1, narrow)]
    shifts += [(s, t) for s in range(1, narrow) for t in range(1, pair)]
    blocks = [residual] + [send_both(residual, s, t) for s, t in shifts]
    shifts.insert(0, (0, 0))
    adjoint = call(
        functools.partial(adjoint_kernel, shifts, own_out),
        shape((sparse_count, own_out, lanes), F32),
        [VMEM] * (len(blocks) + 1),
        vmem=big,
    )(*blocks, turned)
    return (predicted, adjoint)


def solution(mesh):
    in_specs = (
        P(("parts", "wide"), None, None, ("narrow", "pair")),
        P(),
        P(),
        P(),
        P(),
        P(),
        P(("parts", "narrow"), None),
        P("parts", "wide", ("narrow", "pair")),
        P(("narrow", "pair"), None),
    )
    out_specs = (P("parts", "wide", ("narrow", "pair")), P("parts", "wide", ("narrow", "pair")))
    return jax.shard_map(local, mesh=mesh, in_specs=in_specs, out_specs=out_specs, check_vma=False)
```

```python
import functools

import jax
import jax.numpy as jnp
from jax import lax
from jax.experimental import pallas as pl
from jax.experimental.pallas import tpu as pltpu
from jax.sharding import PartitionSpec as P

F32, BF16 = jnp.float32, jnp.bfloat16
VMEM = pl.BlockSpec(memory_space=pltpu.VMEM)
TAPS = 4


def call(kernel, outs, in_specs, scratch=(), vmem=16, flops=10**6):
    nbytes = sum(o.size * o.dtype.itemsize for o in jax.tree.leaves(outs))
    return pl.pallas_call(
        kernel,
        out_shape=outs,
        in_specs=in_specs,
        out_specs=jax.tree.map(lambda _: VMEM, outs),
        scratch_shapes=list(scratch),
        compiler_params=pltpu.CompilerParams(vmem_limit_bytes=int(vmem * 2**20)),
        cost_estimate=pl.CostEstimate(flops=flops, bytes_accessed=nbytes, transcendentals=0),
    )


def leaky_relu(values):
    return jnp.maximum(values, 0.1 * values)


def split(index, size):
    whole = ((index.astype(F32) + 0.5) * (1.0 / size)).astype(jnp.int32)
    return whole, index - whole * size


def iota(shape, axis):
    return lax.broadcasted_iota(jnp.int32, shape, axis)


def rounds(count, cores):
    if count == 4:
        schedules = [
            [(1, 3, 0, 2), (3, 2, 1, 0), (2, 0, 3, 1)],
            [(2, 3, 1, 0), (3, 2, 0, 1), (1, 0, 3, 2)],
        ]
    else:
        schedules = [[tuple((i + shift) % count for i in range(count)) for shift in range(1, count)]]
    return [
        tuple(schedules[core % len(schedules)][r][i] for i in range(count) for core in range(cores))
        for r in range(count - 1)
    ]


def sources(route, cores):
    back = [0] * len(route)
    for place, target in enumerate(route):
        back[target * cores + place % cores] = place // cores
    return tuple(back)


def entry(table, axes):
    index = lax.axis_index(axes)
    value = jnp.int32(table[0])
    for i in range(1, len(table)):
        value = jnp.where(index == i, jnp.int32(table[i]), value)
    return value


def column_groups(channels, span):
    most = max(1, 256 // (2 * channels) // 2 * 2)
    return [(first, min(most, span - first)) for first in range(0, span, most)]


def pack_window(window_ref, rows_ref, channels, width, span, target):
    first = target * (span - 2) + 7
    columns = [rows_ref[pl.ds(first + i, channels, stride=width), :] for i in range(span)]
    window_ref[...] = jnp.concatenate(columns, axis=0).astype(BF16)


def clear_edges(rows_ref, count):
    edge = jnp.zeros((8, rows_ref.shape[1]), F32)
    rows_ref[0:8, :] = edge
    rows_ref[8 + count : 16 + count, :] = edge


def pack_kernel(routes, low_ref, *refs):
    windows, (block_ref, rows_ref, sems) = refs[: len(routes)], refs[len(routes) :]
    _, channels, width, rows = low_ref.shape
    parts = sems.shape[0]
    each = channels // parts
    pieces = []
    for i in range(parts):
        piece = pl.ds(i * each, each)
        pieces.append(pltpu.make_async_copy(low_ref.at[0, piece], block_ref.at[piece], sems.at[i]))
        pieces[-1].start()
    clear_edges(rows_ref, channels * width)
    targets = [entry(route, ("wide", "pair")) for route in routes]
    for i in range(parts):
        pieces[i].wait()
        values = block_ref[i * each : (i + 1) * each].astype(F32).reshape(each * width, rows)
        rows_ref[8 + i * each * width : 8 + (i + 1) * each * width, :] = values
    for window, target in zip(windows, targets):
        pack_window(window, rows_ref, channels, width, width // (len(routes) + 1) + 2, target)


def prepare_kernel(
    wide,
    own_out,
    groups,
    aw_ref,
    ab_ref,
    cw_ref,
    cb_ref,
    hw_ref,
    measured_ref,
    sparse_ref,
    block_ref,
    *refs,
):
    firsts, refs = refs[:-8], refs[-8:]
    a2_ref, b1_ref, b2_ref, h_ref, select_ref, target_ref, own_ref, rows_ref = refs
    channels, width, lanes = block_ref.shape
    span = 2 * own_out + 2
    clear_edges(rows_ref, channels * width)
    rows_ref[8 : 8 + channels * width, :] = block_ref[...].astype(F32).reshape(channels * width, lanes)
    pack_window(own_ref, rows_ref, channels, width, span, lax.axis_index("wide"))
    size, outs = span * channels, own_out * channels
    rows, columns = split(iota((size, channels), 0), channels)
    pick = (columns == iota((size, channels), 1)).astype(F32)
    pick16 = pick.astype(BF16)
    out_channel, _ = split(iota((outs, channels), 0), own_out)
    pick_out = (out_channel == iota((outs, channels), 1)).astype(F32)
    pick_out16 = pick_out.astype(BF16)

    def spread(left, weight, right):
        half = lax.dot_general(left, weight, (((1,), (1,)), ((), ())), preferred_element_type=F32)
        return lax.dot_general(half.astype(BF16), right, (((1,), (1,)), ((), ())), preferred_element_type=F32)

    for first_ref in firsts:
        many = first_ref.shape[0] // 2
        taken = many // channels
        which, channel = split(iota((2 * many, channels), 0), channels)
        is_channel = channel == iota((2 * many, channels), 1)
        sides = [is_channel & (which >= side * taken) & (which < (side + 1) * taken) for side in range(2)]
        sides = [side.astype(F32).astype(BF16) for side in sides]
        row_column = split(iota((many, 2 * many), 0), channels)[0]
        column_column = split(iota((many, 2 * many), 1), channels)[0]
        same = (row_column == column_column) | (row_column + taken == column_column)
        for e in range(2):
            full = spread(pick16[:many], aw_ref[e], sides[0]) + spread(pick16[:many], aw_ref[e + 2], sides[1])
            first_ref[e * many : (e + 1) * many, :] = jnp.where(same, full, 0.0).astype(BF16)

    in_column = split(iota((outs, size), 1), channels)[0]
    out_column = split(iota((outs, size), 0), own_out)[1]
    me = lax.axis_index("wide")
    absolute = in_column + me * (2 * own_out) - 1
    inside = (absolute >= 0) & (absolute < 2 * own_out * wide)
    total = jnp.zeros((outs, size), F32)
    for tap in range(TAPS):
        here = (in_column == 2 * out_column + tap) & inside
        total = jnp.where(here, spread(pick_out16, cw_ref[tap], pick16), total)
    a2_ref[...] = total.astype(BF16)

    def along(left, vector_ref, out_ref):
        summed = jnp.sum(left * vector_ref[...].astype(F32), axis=1, keepdims=True)
        out_ref[...] = jnp.broadcast_to(summed, out_ref.shape)

    along(pick, ab_ref, b1_ref)
    along(pick_out, cb_ref, b2_ref)
    along(pick_out, hw_ref, h_ref)

    sparse_count = measured_ref.shape[0]
    wanted = (select_ref.shape[0], sparse_count)
    pick_view = (split(iota(wanted, 0), own_out)[0] == iota(wanted, 1)).astype(F32)
    along(pick_view, sparse_ref, select_ref)
    for k in range(sparse_count):
        target_ref[k * own_out : (k + 1) * own_out, :] = measured_ref[k]


def turn_kernel(routes, rw_ref, early_ref, late_ref, turned_ref, predicted_ref):
    wide = len(routes) + 1
    missing = origin(routes[-1])
    for pair in range(wide):
        view = lax.rem(missing + pair, wide)
        for e in range(2):
            tile = late_ref[2 * pair + e] if pair < 2 else early_ref[2 * (pair - 2) + e]
            predicted_ref[2 * view + e] = tile[: predicted_ref.shape[1]]
    turned = rw_ref[...].T
    high = turned.astype(BF16)
    turned_ref[:, : high.shape[1]] = high
    turned_ref[:, high.shape[1] :] = (turned - high.astype(F32)).astype(BF16)


def origin(route):
    return entry(sources(route, lax.axis_size("pair")), ("wide", "pair"))


def first_and_second_layer(current, previous, groups, firsts, a2_ref, b1, b2, h, own_out):
    outs = a2_ref.shape[0]
    channels = outs // own_out
    pieces = ([], [])
    for (first, taken), first_ref in zip(groups, firsts):
        rows = slice(first * channels, (first + taken) * channels)
        half = taken * channels
        stacked = jnp.concatenate([current[rows], previous[rows]], axis=0)
        summed = jnp.dot(first_ref[...], stacked, preferred_element_type=F32)
        for e in range(2):
            pieces[e].append(leaky_relu(summed[e * half : (e + 1) * half] + b1[rows]).astype(BF16))
    both = jnp.concatenate([jnp.concatenate(piece, axis=0) for piece in pieces], axis=1)
    hidden = leaky_relu(jnp.dot(a2_ref[...], both, preferred_element_type=F32) + b2) * h
    value = jnp.sum(hidden.reshape(outs // 8, 8, hidden.shape[1]), axis=0)
    apart = own_out
    while apart < 8:
        value += pltpu.roll(value, apart, 0)
        apart *= 2
    return value


def wider(ref, times):
    return jnp.concatenate([ref[...]] * times, axis=1)


def choose(select, view, tile, picked):
    repeated = jnp.concatenate([tile] * (select.shape[0] // 8), axis=0)
    return jnp.where(select == view.astype(F32), repeated, picked)


def early_kernel(routes, own_out, groups, *refs):
    wide = len(routes) + 1
    windows, firsts, refs = refs[: wide - 1], refs[wide - 1 : wide - 1 + len(groups)], refs[wide - 1 + len(groups) :]
    a2_ref, b1_ref, b2_ref, h_ref, select_ref, tiles_ref, picked_ref, next_ref, before_ref, views_ref = refs
    lanes = windows[0].shape[1]
    me = lax.axis_index("wide")
    missing = origin(routes[-1])
    slots = [lax.rem(source - missing + wide, wide) - 1 for source in [me] + [origin(route) for route in routes[:-1]]]
    if wide <= 4:
        values = [window[...] for window in windows]
        ordered = []
        for place in range(wide - 1):
            chosen = values[0]
            for value, slot in zip(values[1:], slots[1:]):
                chosen = jnp.where(slot == place, value, chosen)
            ordered.append(chosen)
        views = jnp.concatenate(ordered, axis=1)
    else:
        for window, slot in zip(windows, slots):
            views_ref[:, pl.ds(pl.multiple_of(slot * lanes, lanes), lanes)] = window[...]
        views = views_ref
    next_ref[...] = views[:, :lanes]
    before_ref[...] = views[:, (wide - 2) * lanes :]
    many = 2 if wide % 2 == 0 else 1
    b1, b2, h = wider(b1_ref, many), wider(b2_ref, 2 * many), wider(h_ref, 2 * many)
    select = select_ref[...]
    picked = jnp.zeros(select.shape, F32)
    for pair in range(0, wide - 2, many):
        previous = views[:, pair * lanes : (pair + many) * lanes]
        current = views[:, (pair + 1) * lanes : (pair + 1 + many) * lanes]
        value = first_and_second_layer(current, previous, groups, firsts, a2_ref, b1, b2, h, own_out)
        for e in range(2):
            for i in range(many):
                tile = value[:, (e * many + i) * lanes : (e * many + i + 1) * lanes]
                tiles_ref[2 * (pair + i) + e] = tile
                view = 2 * lax.rem(missing + 2 + pair + i, wide) + e
                picked = choose(select, view, tile, picked)
    picked_ref[...] = picked


def late_kernel(routes, own_out, groups, *refs):
    wide = len(routes) + 1
    window_ref, next_ref, before_ref, *firsts = refs[: 3 + len(groups)]
    a2_ref, b1_ref, b2_ref, h_ref, select_ref, target_ref, picked_ref, tiles_ref, residual_ref = refs[3 + len(groups) :]
    lanes = window_ref.shape[1]
    missing = origin(routes[-1])
    current = jnp.concatenate([window_ref[...], next_ref[...]], axis=1)
    previous = jnp.concatenate([before_ref[...], window_ref[...]], axis=1)
    b1, b2, h = wider(b1_ref, 2), wider(b2_ref, 4), wider(h_ref, 4)
    value = first_and_second_layer(current, previous, groups, firsts, a2_ref, b1, b2, h, own_out)
    select, picked = select_ref[...], picked_ref[...]
    for e in range(2):
        for i in range(2):
            tile = value[:, (2 * e + i) * lanes : (2 * e + i + 1) * lanes]
            tiles_ref[2 * i + e] = tile
            picked = choose(select, 2 * lax.rem(missing + i, wide) + e, tile, picked)
    residual_ref[...] = (picked - target_ref[...]).astype(BF16)


def adjoint_kernel(shifts, own_out, *refs):
    residuals, refs = refs[: len(shifts)], refs[len(shifts) :]
    turned_ref, out_ref = refs
    lanes = residuals[0].shape[1]
    weights = []
    for narrow_shift, pair_shift in shifts:
        narrow, pair = came_from("narrow", narrow_shift), came_from("pair", pair_shift)
        block = narrow * lax.axis_size("pair") + pair
        weights.append(turned_ref[pl.ds(pl.multiple_of(block * lanes, lanes), lanes), :])
    values = jnp.concatenate([ref[...] for ref in residuals], axis=1)
    both = jnp.dot(values, jnp.concatenate(weights, axis=0), preferred_element_type=F32)
    total = both[:, :lanes] + both[:, lanes:]
    for k in range(out_ref.shape[0]):
        out_ref[k] = total[k * own_out : (k + 1) * own_out]


def came_from(axis, distance):
    count = lax.axis_size(axis)
    return lax.rem(lax.axis_index(axis) - distance + count, count)


def send_both(block, narrow_distance, pair_distance):
    narrow, pair = lax.axis_size("narrow"), lax.axis_size("pair")
    route = []
    for i in range(narrow):
        for j in range(pair):
            target = (i + narrow_distance) % narrow * pair + (j + pair_distance) % pair
            route.append((i * pair + j, target))
    return lax.ppermute(block, ("narrow", "pair"), route)


def local(
    low_sino,
    angle_weight,
    angle_bias,
    column_weight,
    column_bias,
    head_weight,
    sparse_views,
    measured,
    row_weights,
):
    wide, narrow, pair = (lax.axis_size(axis) for axis in ("wide", "narrow", "pair"))
    _, channels, width, lanes = low_sino.shape
    own_out = width // wide // 2
    span = 2 * own_out + 2
    size, outs = span * channels, own_out * channels
    sparse_count = measured.shape[0]
    rows = row_weights.shape[1]
    flat = (sparse_count * own_out, lanes)
    shape = jax.ShapeDtypeStruct
    big = 16 if width <= 64 else 48

    small = (
        angle_weight,
        angle_bias[None],
        column_weight,
        column_bias[None],
        head_weight[None],
        measured,
        sparse_views,
    )
    routes = rounds(wide, pair)
    groups = column_groups(channels, span)
    rows_scratch = pltpu.VMEM((16 + (channels + 1) * width, lanes), F32)
    *windows, block = call(
        functools.partial(pack_kernel, routes),
        [shape((size, lanes), BF16)] * (wide - 1) + [shape(low_sino.shape[1:], BF16)],
        [pl.BlockSpec(memory_space=pltpu.HBM)],
        [rows_scratch, pltpu.SemaphoreType.DMA((8,))],
        vmem=53.5 if width <= 64 else 48,
    )(low_sino)
    windows = [
        lax.ppermute(window, ("wide", "pair"), [(p, t * pair + p % pair) for p, t in enumerate(route)])
        for window, route in zip(windows, routes)
    ]

    widths = sorted({taken for _, taken in groups})
    *firsts, a2, b1, b2, head, select, target, own = call(
        functools.partial(prepare_kernel, wide, own_out, groups),
        [shape((2 * taken * channels, 2 * taken * channels), BF16) for taken in widths]
        + [
            shape((outs, size), BF16),
            shape((size, lanes), F32),
            shape((outs, lanes), F32),
            shape((outs, lanes), F32),
            shape(flat, F32),
            shape(flat, F32),
            shape((size, lanes), BF16),
        ],
        [VMEM] * 8,
        [rows_scratch],
        vmem=big,
    )(*small, block)
    windows.insert(0, own)
    firsts = [firsts[widths.index(taken)] for _, taken in groups]

    window = shape((size, lanes), BF16)
    early_tiles, picked, following, before = call(
        functools.partial(early_kernel, routes, own_out, groups),
        [shape((2 * wide - 4, 8, lanes), F32), shape(flat, F32), window, window],
        [VMEM] * (wide + len(groups) + 4),
        [pltpu.VMEM((size, (wide - 1) * lanes), BF16)],
        vmem=big,
    )(*windows[:-1], *firsts, a2, b1, b2, head, select)
    late_tiles, residual = call(
        functools.partial(late_kernel, routes, own_out, groups),
        [shape((4, 8, lanes), F32), shape(flat, BF16)],
        [VMEM] * (len(groups) + 10),
        vmem=big,
    )(windows[-1], following, before, *firsts, a2, b1, b2, head, select, target, picked)

    turned, predicted = call(
        functools.partial(turn_kernel, routes),
        [shape((rows, 2 * lanes), BF16), shape((2 * wide, own_out, lanes), F32)],
        [VMEM] * 3,
        vmem=big,
    )(row_weights, early_tiles, late_tiles)
    shifts = [(0, t) for t in range(1, pair)] + [(s, 0) for s in range(1, narrow)]
    shifts += [(s, t) for s in range(1, narrow) for t in range(1, pair)]
    blocks = [residual] + [send_both(residual, s, t) for s, t in shifts]
    shifts.insert(0, (0, 0))
    adjoint = call(
        functools.partial(adjoint_kernel, shifts, own_out),
        shape((sparse_count, own_out, lanes), F32),
        [VMEM] * (len(blocks) + 1),
        vmem=big,
    )(*blocks, turned)
    return (predicted, adjoint)


def solution(mesh):
    in_specs = (
        P(("parts", "wide"), None, None, ("narrow", "pair")),
        P(),
        P(),
        P(),
        P(),
        P(),
        P(("parts", "narrow"), None),
        P("parts", "wide", ("narrow", "pair")),
        P(("narrow", "pair"), None),
    )
    out_specs = (P("parts", "wide", ("narrow", "pair")), P("parts", "wide", ("narrow", "pair")))
    return jax.shard_map(local, mesh=mesh, in_specs=in_specs, out_specs=out_specs, check_vma=False)
```

```python
import functools

import jax
import jax.numpy as jnp
from jax import lax
from jax.experimental import pallas as pl
from jax.experimental.pallas import tpu as pltpu
from jax.sharding import PartitionSpec as P

F32, BF16 = jnp.float32, jnp.bfloat16
VMEM = pl.BlockSpec(memory_space=pltpu.VMEM)
TAPS = 4


def call(kernel, outs, in_specs, scratch=(), vmem=16, flops=10**6):
    nbytes = sum(o.size * o.dtype.itemsize for o in jax.tree.leaves(outs))
    return pl.pallas_call(
        kernel,
        out_shape=outs,
        in_specs=in_specs,
        out_specs=jax.tree.map(lambda _: VMEM, outs),
        scratch_shapes=list(scratch),
        compiler_params=pltpu.CompilerParams(vmem_limit_bytes=int(vmem * 2**20)),
        cost_estimate=pl.CostEstimate(flops=flops, bytes_accessed=nbytes, transcendentals=0),
    )


def leaky_relu(values):
    return jnp.maximum(values, 0.1 * values)


def split(index, size):
    whole = ((index.astype(F32) + 0.5) * (1.0 / size)).astype(jnp.int32)
    return whole, index - whole * size


def iota(shape, axis):
    return lax.broadcasted_iota(jnp.int32, shape, axis)


def rounds(count, cores):
    if count == 4:
        schedules = [
            [(1, 3, 0, 2), (3, 2, 1, 0), (2, 0, 3, 1)],
            [(2, 3, 1, 0), (3, 2, 0, 1), (1, 0, 3, 2)],
        ]
    else:
        schedules = [[tuple((i + shift) % count for i in range(count)) for shift in range(1, count)]]
    return [
        tuple(schedules[core % len(schedules)][r][i] for i in range(count) for core in range(cores))
        for r in range(count - 1)
    ]


def sources(route, cores):
    back = [0] * len(route)
    for place, target in enumerate(route):
        back[target * cores + place % cores] = place // cores
    return tuple(back)


def entry(table, axes):
    index = lax.axis_index(axes)
    value = jnp.int32(table[0])
    for i in range(1, len(table)):
        value = jnp.where(index == i, jnp.int32(table[i]), value)
    return value


def column_groups(channels, span):
    most = max(1, 256 // (2 * channels) // 2 * 2)
    return [(first, min(most, span - first)) for first in range(0, span, most)]


def pack_window(window_ref, rows_ref, channels, width, span, target):
    first = target * (span - 2) + 7
    columns = [rows_ref[pl.ds(first + i, channels, stride=width), :] for i in range(span)]
    window_ref[...] = jnp.concatenate(columns, axis=0).astype(BF16)


def clear_edges(rows_ref, count):
    edge = jnp.zeros((8, rows_ref.shape[1]), F32)
    rows_ref[0:8, :] = edge
    rows_ref[8 + count : 16 + count, :] = edge


def pack_kernel(routes, low_ref, *refs):
    windows, (block_ref, rows_ref, sems) = refs[: len(routes)], refs[len(routes) :]
    _, channels, width, rows = low_ref.shape
    parts = sems.shape[0]
    each = channels // parts
    pieces = []
    for i in range(parts):
        piece = pl.ds(i * each, each)
        pieces.append(pltpu.make_async_copy(low_ref.at[0, piece], block_ref.at[piece], sems.at[i]))
        pieces[-1].start()
    clear_edges(rows_ref, channels * width)
    targets = [entry(route, ("wide", "pair")) for route in routes]
    for i in range(parts):
        pieces[i].wait()
        values = block_ref[i * each : (i + 1) * each].astype(F32).reshape(each * width, rows)
        rows_ref[8 + i * each * width : 8 + (i + 1) * each * width, :] = values
    for window, target in zip(windows, targets):
        pack_window(window, rows_ref, channels, width, width // (len(routes) + 1) + 2, target)


def prepare_kernel(
    wide,
    own_out,
    groups,
    aw_ref,
    ab_ref,
    cw_ref,
    cb_ref,
    hw_ref,
    measured_ref,
    sparse_ref,
    block_ref,
    *refs,
):
    firsts, refs = refs[:-8], refs[-8:]
    a2_ref, b1_ref, b2_ref, h_ref, select_ref, target_ref, own_ref, rows_ref = refs
    channels, width, lanes = block_ref.shape
    span = 2 * own_out + 2
    clear_edges(rows_ref, channels * width)
    rows_ref[8 : 8 + channels * width, :] = block_ref[...].astype(F32).reshape(channels * width, lanes)
    pack_window(own_ref, rows_ref, channels, width, span, lax.axis_index("wide"))
    size, outs = span * channels, own_out * channels
    rows, columns = split(iota((size, channels), 0), channels)
    pick = (columns == iota((size, channels), 1)).astype(F32)
    pick16 = pick.astype(BF16)
    out_channel, _ = split(iota((outs, channels), 0), own_out)
    pick_out = (out_channel == iota((outs, channels), 1)).astype(F32)
    pick_out16 = pick_out.astype(BF16)

    def spread(left, weight, right):
        half = lax.dot_general(left, weight, (((1,), (1,)), ((), ())), preferred_element_type=F32)
        return lax.dot_general(half.astype(BF16), right, (((1,), (1,)), ((), ())), preferred_element_type=F32)

    for first_ref in firsts:
        many = first_ref.shape[0] // 2
        taken = many // channels
        which, channel = split(iota((2 * many, channels), 0), channels)
        is_channel = channel == iota((2 * many, channels), 1)
        sides = [is_channel & (which >= side * taken) & (which < (side + 1) * taken) for side in range(2)]
        sides = [side.astype(F32).astype(BF16) for side in sides]
        row_column = split(iota((many, 2 * many), 0), channels)[0]
        column_column = split(iota((many, 2 * many), 1), channels)[0]
        same = (row_column == column_column) | (row_column + taken == column_column)
        for e in range(2):
            full = spread(pick16[:many], aw_ref[e], sides[0]) + spread(pick16[:many], aw_ref[e + 2], sides[1])
            first_ref[e * many : (e + 1) * many, :] = jnp.where(same, full, 0.0).astype(BF16)

    in_column = split(iota((outs, size), 1), channels)[0]
    out_column = split(iota((outs, size), 0), own_out)[1]
    me = lax.axis_index("wide")
    absolute = in_column + me * (2 * own_out) - 1
    inside = (absolute >= 0) & (absolute < 2 * own_out * wide)
    total = jnp.zeros((outs, size), F32)
    for tap in range(TAPS):
        here = (in_column == 2 * out_column + tap) & inside
        total = jnp.where(here, spread(pick_out16, cw_ref[tap], pick16), total)
    a2_ref[...] = total.astype(BF16)

    def along(left, vector_ref, out_ref):
        summed = jnp.sum(left * vector_ref[...].astype(F32), axis=1, keepdims=True)
        out_ref[...] = jnp.broadcast_to(summed, out_ref.shape)

    along(pick, ab_ref, b1_ref)
    along(pick_out, cb_ref, b2_ref)
    along(pick_out, hw_ref, h_ref)

    sparse_count = measured_ref.shape[0]
    wanted = (select_ref.shape[0], sparse_count)
    pick_view = (split(iota(wanted, 0), own_out)[0] == iota(wanted, 1)).astype(F32)
    along(pick_view, sparse_ref, select_ref)
    for k in range(sparse_count):
        target_ref[k * own_out : (k + 1) * own_out, :] = measured_ref[k]


def turn_kernel(routes, rw_ref, early_ref, late_ref, turned_ref, predicted_ref):
    wide = len(routes) + 1
    missing = origin(routes[-1])
    for pair in range(wide):
        view = lax.rem(missing + pair, wide)
        for e in range(2):
            tile = late_ref[2 * pair + e] if pair < 2 else early_ref[2 * (pair - 2) + e]
            predicted_ref[2 * view + e] = tile[: predicted_ref.shape[1]]
    turned = rw_ref[...].T
    high = turned.astype(BF16)
    turned_ref[:, : high.shape[1]] = high
    turned_ref[:, high.shape[1] :] = (turned - high.astype(F32)).astype(BF16)


def origin(route):
    return entry(sources(route, lax.axis_size("pair")), ("wide", "pair"))


def first_and_second_layer(current, previous, groups, firsts, a2_ref, b1, b2, h, own_out):
    outs = a2_ref.shape[0]
    channels = outs // own_out
    pieces = ([], [])
    for (first, taken), first_ref in zip(groups, firsts):
        rows = slice(first * channels, (first + taken) * channels)
        half = taken * channels
        stacked = jnp.concatenate([current[rows], previous[rows]], axis=0)
        summed = jnp.dot(first_ref[...], stacked, preferred_element_type=F32)
        for e in range(2):
            pieces[e].append(leaky_relu(summed[e * half : (e + 1) * half] + b1[rows]).astype(BF16))
    both = jnp.concatenate([jnp.concatenate(piece, axis=0) for piece in pieces], axis=1)
    hidden = leaky_relu(jnp.dot(a2_ref[...], both, preferred_element_type=F32) + b2) * h
    value = jnp.sum(hidden.reshape(outs // 8, 8, hidden.shape[1]), axis=0)
    apart = own_out
    while apart < 8:
        value += pltpu.roll(value, apart, 0)
        apart *= 2
    return value


def wider(ref, times):
    return jnp.concatenate([ref[...]] * times, axis=1)


def choose(select, view, tile, picked):
    repeated = jnp.concatenate([tile] * (select.shape[0] // 8), axis=0)
    return jnp.where(select == view.astype(F32), repeated, picked)


def early_kernel(routes, own_out, groups, *refs):
    wide = len(routes) + 1
    windows, firsts, refs = refs[: wide - 1], refs[wide - 1 : wide - 1 + len(groups)], refs[wide - 1 + len(groups) :]
    a2_ref, b1_ref, b2_ref, h_ref, select_ref, tiles_ref, picked_ref, next_ref, before_ref, views_ref = refs
    lanes = windows[0].shape[1]
    me = lax.axis_index("wide")
    missing = origin(routes[-1])
    slots = [lax.rem(source - missing + wide, wide) - 1 for source in [me] + [origin(route) for route in routes[:-1]]]
    if wide <= 4:
        values = [window[...] for window in windows]
        ordered = []
        for place in range(wide - 1):
            chosen = values[0]
            for value, slot in zip(values[1:], slots[1:]):
                chosen = jnp.where(slot == place, value, chosen)
            ordered.append(chosen)
        views = jnp.concatenate(ordered, axis=1)
    else:
        for window, slot in zip(windows, slots):
            views_ref[:, pl.ds(pl.multiple_of(slot * lanes, lanes), lanes)] = window[...]
        views = views_ref
    next_ref[...] = views[:, :lanes]
    before_ref[...] = views[:, (wide - 2) * lanes :]
    many = 2 if wide % 2 == 0 else 1
    b1, b2, h = wider(b1_ref, many), wider(b2_ref, 2 * many), wider(h_ref, 2 * many)
    select = select_ref[...]
    picked = jnp.zeros(select.shape, F32)
    for pair in range(0, wide - 2, many):
        previous = views[:, pair * lanes : (pair + many) * lanes]
        current = views[:, (pair + 1) * lanes : (pair + 1 + many) * lanes]
        value = first_and_second_layer(current, previous, groups, firsts, a2_ref, b1, b2, h, own_out)
        for e in range(2):
            for i in range(many):
                tile = value[:, (e * many + i) * lanes : (e * many + i + 1) * lanes]
                tiles_ref[2 * (pair + i) + e] = tile
                view = 2 * lax.rem(missing + 2 + pair + i, wide) + e
                picked = choose(select, view, tile, picked)
    picked_ref[...] = picked


def late_kernel(routes, own_out, groups, *refs):
    wide = len(routes) + 1
    window_ref, next_ref, before_ref, *firsts = refs[: 3 + len(groups)]
    a2_ref, b1_ref, b2_ref, h_ref, select_ref, target_ref, picked_ref, tiles_ref, residual_ref = refs[3 + len(groups) :]
    lanes = window_ref.shape[1]
    missing = origin(routes[-1])
    current = jnp.concatenate([window_ref[...], next_ref[...]], axis=1)
    previous = jnp.concatenate([before_ref[...], window_ref[...]], axis=1)
    b1, b2, h = wider(b1_ref, 2), wider(b2_ref, 4), wider(h_ref, 4)
    value = first_and_second_layer(current, previous, groups, firsts, a2_ref, b1, b2, h, own_out)
    select, picked = select_ref[...], picked_ref[...]
    for e in range(2):
        for i in range(2):
            tile = value[:, (2 * e + i) * lanes : (2 * e + i + 1) * lanes]
            tiles_ref[2 * i + e] = tile
            picked = choose(select, 2 * lax.rem(missing + i, wide) + e, tile, picked)
    residual_ref[...] = (picked - target_ref[...]).astype(BF16)


def adjoint_kernel(shifts, own_out, *refs):
    residuals, refs = refs[: len(shifts)], refs[len(shifts) :]
    turned_ref, out_ref = refs
    lanes = residuals[0].shape[1]
    weights = []
    for narrow_shift, pair_shift in shifts:
        narrow, pair = came_from("narrow", narrow_shift), came_from("pair", pair_shift)
        block = narrow * lax.axis_size("pair") + pair
        weights.append(turned_ref[pl.ds(pl.multiple_of(block * lanes, lanes), lanes), :])
    values = jnp.concatenate([ref[...] for ref in residuals], axis=1)
    both = jnp.dot(values, jnp.concatenate(weights, axis=0), preferred_element_type=F32)
    total = both[:, :lanes] + both[:, lanes:]
    for k in range(out_ref.shape[0]):
        out_ref[k] = total[k * own_out : (k + 1) * own_out]


def came_from(axis, distance):
    count = lax.axis_size(axis)
    return lax.rem(lax.axis_index(axis) - distance + count, count)


def send_both(block, narrow_distance, pair_distance):
    narrow, pair = lax.axis_size("narrow"), lax.axis_size("pair")
    route = []
    for i in range(narrow):
        for j in range(pair):
            target = (i + narrow_distance) % narrow * pair + (j + pair_distance) % pair
            route.append((i * pair + j, target))
    return lax.ppermute(block, ("narrow", "pair"), route)


def local(
    low_sino,
    angle_weight,
    angle_bias,
    column_weight,
    column_bias,
    head_weight,
    sparse_views,
    measured,
    row_weights,
):
    wide, narrow, pair = (lax.axis_size(axis) for axis in ("wide", "narrow", "pair"))
    _, channels, width, lanes = low_sino.shape
    own_out = width // wide // 2
    span = 2 * own_out + 2
    size, outs = span * channels, own_out * channels
    sparse_count = measured.shape[0]
    rows = row_weights.shape[1]
    flat = (sparse_count * own_out, lanes)
    shape = jax.ShapeDtypeStruct
    big = 16 if width <= 64 else 48

    small = (
        angle_weight,
        angle_bias[None],
        column_weight,
        column_bias[None],
        head_weight[None],
        measured,
        sparse_views,
    )
    routes = rounds(wide, pair)
    groups = column_groups(channels, span)
    rows_scratch = pltpu.VMEM((16 + (channels + 1) * width, lanes), F32)
    *windows, block = call(
        functools.partial(pack_kernel, routes),
        [shape((size, lanes), BF16)] * (wide - 1) + [shape(low_sino.shape[1:], BF16)],
        [pl.BlockSpec(memory_space=pltpu.HBM)],
        [rows_scratch, pltpu.SemaphoreType.DMA((2,))],
        vmem=53.5 if width <= 64 else 48,
    )(low_sino)
    windows = [
        lax.ppermute(window, ("wide", "pair"), [(p, t * pair + p % pair) for p, t in enumerate(route)])
        for window, route in zip(windows, routes)
    ]

    widths = sorted({taken for _, taken in groups})
    *firsts, a2, b1, b2, head, select, target, own = call(
        functools.partial(prepare_kernel, wide, own_out, groups),
        [shape((2 * taken * channels, 2 * taken * channels), BF16) for taken in widths]
        + [
            shape((outs, size), BF16),
            shape((size, lanes), F32),
            shape((outs, lanes), F32),
            shape((outs, lanes), F32),
            shape(flat, F32),
            shape(flat, F32),
            shape((size, lanes), BF16),
        ],
        [VMEM] * 8,
        [rows_scratch],
        vmem=big,
    )(*small, block)
    windows.insert(0, own)
    firsts = [firsts[widths.index(taken)] for _, taken in groups]

    window = shape((size, lanes), BF16)
    early_tiles, picked, following, before = call(
        functools.partial(early_kernel, routes, own_out, groups),
        [shape((2 * wide - 4, 8, lanes), F32), shape(flat, F32), window, window],
        [VMEM] * (wide + len(groups) + 4),
        [pltpu.VMEM((size, (wide - 1) * lanes), BF16)],
        vmem=big,
    )(*windows[:-1], *firsts, a2, b1, b2, head, select)
    late_tiles, residual = call(
        functools.partial(late_kernel, routes, own_out, groups),
        [shape((4, 8, lanes), F32), shape(flat, BF16)],
        [VMEM] * (len(groups) + 10),
        vmem=big,
    )(windows[-1], following, before, *firsts, a2, b1, b2, head, select, target, picked)

    turned, predicted = call(
        functools.partial(turn_kernel, routes),
        [shape((rows, 2 * lanes), BF16), shape((2 * wide, own_out, lanes), F32)],
        [VMEM] * 3,
        vmem=big,
    )(row_weights, early_tiles, late_tiles)
    shifts = [(0, t) for t in range(1, pair)] + [(s, 0) for s in range(1, narrow)]
    shifts += [(s, t) for s in range(1, narrow) for t in range(1, pair)]
    blocks = [residual] + [send_both(residual, s, t) for s, t in shifts]
    shifts.insert(0, (0, 0))
    adjoint = call(
        functools.partial(adjoint_kernel, shifts, own_out),
        shape((sparse_count, own_out, lanes), F32),
        [VMEM] * (len(blocks) + 1),
        vmem=big,
    )(*blocks, turned)
    return (predicted, adjoint)


def solution(mesh):
    in_specs = (
        P(("parts", "wide"), None, None, ("narrow", "pair")),
        P(),
        P(),
        P(),
        P(),
        P(),
        P(("parts", "narrow"), None),
        P("parts", "wide", ("narrow", "pair")),
        P(("narrow", "pair"), None),
    )
    out_specs = (P("parts", "wide", ("narrow", "pair")), P("parts", "wide", ("narrow", "pair")))
    return jax.shard_map(local, mesh=mesh, in_specs=in_specs, out_specs=out_specs, check_vma=False)
```
